128 devices in a mesh: dp: 4 (over x), context: 4 (over y), expert: 8 (over z, core).
Axes of the slice: x: 4, y: 4, z: 4, core: 2. Of those that a mesh axis runs over, the one named last changes fastest.
Arguments:
- tokens: bfloat16 [2, 4, 32, 192, 768], P(None, 'dp', ('context', 'expert')), may hold values from -6 to 6
- prior_logits: float32 [2, 4, 32, 192, 12], P(None, 'dp', ('context', 'expert')), may hold values from -3 to 3
- routes: int32 [2, 4, 32, 192, 2], P(None, 'dp', ('context', 'expert')), may hold values from 0 to 11, all different within a row; in each aligned block of 192 rows (0 to 191, 192 to 383, ..., all dimensions but the last counted through in order) at most 36 rows name the same one
- drops: int32 [2, 4, 32, 192, 2], P(None, 'dp', ('context', 'expert')), may hold values 0 or 1
- cont_lengths: int32 [2, 4, 32], P(None, 'dp', ('context', 'expert')), may hold values from 1 to 128, 3072 in all within a row
- norm_gain: bfloat16 [768], replicated, may hold values from 0.5 to 1.5
- w_query: bfloat16 [768, 768], replicated, may hold values from -0.21875 to 0.21875
- w_key: bfloat16 [768, 768], replicated, may hold values from -0.21875 to 0.21875
- w_value: bfloat16 [768, 768], replicated, may hold values from -0.21875 to 0.21875
- w_out: bfloat16 [768, 768], replicated, may hold values from -1.75 to 1.75
- ffn_gain: bfloat16 [768], replicated, may hold values from 0.5 to 1.5
- w_router: bfloat16 [768, 12], replicated, may hold values from -0.109375 to 0.109375
- w_const: bfloat16 [2, 768, 2], replicated, may hold values from -0.21875 to 0.21875
- const_vec: bfloat16 [2, 768], replicated, may hold values from -24 to 24
- w_gate: bfloat16 [8, 768, 2048], P('expert'), may hold values from -0.21875 to 0.21875
- w_up: bfloat16 [8, 768, 2048], P('expert'), may hold values from -0.21875 to 0.21875
- w_down: bfloat16 [8, 2048, 768], P('expert'), may hold values from -1 to 1
- out_grad: bfloat16 [2, 4, 32, 192, 768], P(None, 'dp', ('context', 'expert')), may hold values from -6 to 6
Outputs:
- mixed: bfloat16 [2, 4, 32, 192, 768], P(None, 'dp', ('context', 'expert'))
- tokens_grad: bfloat16 [2, 4, 32, 192, 768], P(None, 'dp', ('context', 'expert'))
- prior_grad: float32 [2, 4, 32, 192, 12], P(None, 'dp', ('context', 'expert'))
- norm_gain_grad: float32 [768], replicated
- w_query_grad: float32 [768, 768], replicated
- w_key_grad: float32 [768, 768], replicated
- w_value_grad: float32 [768, 768], replicated
- w_out_grad: float32 [768, 768], replicated
- ffn_gain_grad: float32 [768], replicated
- w_router_grad: float32 [768, 12], replicated
- w_const_grad: float32 [2, 768, 2], replicated
- const_vec_grad: float32 [2, 768], replicated
- w_gate_grad: float32 [8, 768, 2048], P('expert')
- w_up_grad: float32 [8, 768, 2048], P('expert')
- w_down_grad: float32 [8, 2048, 768], P('expert')
The draws below stay inside these ranges and needn't reach their ends.
Inputs may be any that keep to these rules, and one draw needn't show every extreme that they name: Targets 0 to 7 are feed-forward experts, 8 the zero expert, 9 the copy expert, the rest constant experts; a token's routes differ; among the 192 rows of one slot of one micro-batch no target is named more than 36 times, a bound that some block reaches. 1 drops the route. `cont_lengths`: the 32 lengths of a group sum to 3072, and the longest is 128.
All inputs are finite; a program needn't handle non-finite values. No bound on the sum of `drops` on one device may be relied on, other than what follows from the above.
Results may differ from the reference program's by a relative error of at most 0.03.
Values may be sent and summed in bfloat16 or wider, within the bound.
No kernel may reach another device: no remote copies, remote signals or barrier semaphores. Data moves between devices by JAX's collectives and lax.ppermute only.
A program may use at most 320 MiB of HBM per device.

```python
import math
import jax
import jax.numpy as jnp
import numpy as np
from jax import lax

D = 768
HEADS = 12
HEAD_SIZE = 64
FF = 2048
EXPERTS = 8
CONSTS = 2
TOP = 2
TARGETS = 12
MB = 2
CLEN = 128
SLOTS = 32
PROMPT = 2048
PROMPT_DEV = 64
ROWS = 192
CAP = 36
GROUPS = 4


def plant(entries, rng, least, high):
    spot = [jax.random.randint(jax.random.fold_in(rng, axis), (), 0, length) for axis, length in enumerate(entries.shape)]
    main_axis = entries.shape.index(max(entries.shape))
    neighbour = spot[:main_axis] + [(spot[main_axis] + 1) % entries.shape[main_axis]] + spot[main_axis + 1:]
    return entries.at[tuple(spot)].set(least).at[tuple(neighbour)].set(high)


def block_levels(stream_key, shape, cuts, least, largest):
    level, own = 1.0, jax.random.fold_in(stream_key, 6)
    for axis_at, parts in cuts:
        heights = jnp.exp(jax.random.uniform(jax.random.fold_in(own, axis_at), (parts,), jnp.float32, least / len(cuts), largest / len(cuts)))
        level = level * jnp.repeat(heights, shape[axis_at] // parts).reshape([-1 if axis == axis_at else 1 for axis in range(len(shape))])
    return level


def profile(amount, total, reach, skew):
    weights = [(1 << 20) // math.isqrt(rank ** skew) + 1 for rank in range(2, amount + 1)]
    spare, given = total - reach - (amount - 1), [1] * (amount - 1)
    while spare > 0:
        candidates = [i for i in range(amount - 1) if given[i] < reach]
        whole, remaining = sum([weights[i] for i in candidates]), spare
        for i in candidates:
            addition = min(reach - given[i], max(1, remaining * weights[i] // whole), spare)
            given[i] = given[i] + addition
            spare = spare - addition
    return np.array([reach] + given)


def ragged(stream_key, number_of, total, limit, skew):
    if number_of == 2:
        one = jax.random.randint(stream_key, (), max(1, total - limit), min(limit, total - 1) + 1)
        return jnp.stack([one, total - one])
    lengths = jnp.asarray(profile(number_of, total, limit, skew), jnp.int32)
    pairs = (number_of - 1) // 2
    source_of, sink = lengths[1:1 + 2 * pairs:2], lengths[2:2 + 2 * pairs:2]
    margin = jnp.minimum(source_of - 1, limit - sink)
    passed = jax.random.randint(jax.random.fold_in(stream_key, 1), (pairs,), 0, 1 << 20) % (margin + 1)
    lengths = lengths.at[1:1 + 2 * pairs:2].set(source_of - passed).at[2:2 + 2 * pairs:2].set(sink + passed)
    return lengths[jax.random.permutation(jax.random.fold_in(stream_key, 2), number_of)]


def shared_out(rng, own, number, rows, number_of, top, most, slope):
    ranking = jax.random.permutation(rng, number_of)
    packed, common = load_shares(number_of, rows * top, most, slope, True), load_shares(number_of, rows * top, most, slope, False)
    places = jnp.arange(number_of)

    def named(tallies, offset_by):
        used = int((tallies > 0).sum())
        fixed = max(1, used // 4)
        moved = fixed + (places - fixed + offset_by * (used - fixed)) % max(1, number_of - fixed)
        return jnp.zeros((number_of,), jnp.int32).at[ranking[jnp.where(places < fixed, places, moved)]].set(jnp.asarray(tallies, jnp.int32))

    tallies = jnp.where(number % 4 == 0, named(packed, number // 4), named(common, number - number // 4 - 1))
    mixed = jax.random.permutation(jax.random.fold_in(own, 3), number_of)
    donor, sink = mixed[0:number_of // 2 * 2:2], mixed[1:number_of // 2 * 2:2]
    margin = jnp.minimum(tallies[donor] - 1, most - tallies[sink]) // 2
    margin = jnp.where((donor == ranking[0]) | (sink == ranking[0]) | (tallies[sink] == 0), 0, jnp.maximum(margin, 0))
    moved = jax.random.randint(jax.random.fold_in(own, 4), (number_of // 2,), 0, 1 << 20) % (margin + 1)
    tallies = tallies.at[donor].add(-moved).at[sink].add(moved)
    items = jnp.searchsorted(jnp.cumsum(tallies), jnp.arange(rows * top), side="right").astype(jnp.int32)
    table = items.reshape(top, rows).T
    table = table[jax.random.permutation(jax.random.fold_in(own, 1), rows)]
    offset_by = jax.random.randint(jax.random.fold_in(own, 2), (rows, 1), 0, top)
    return jnp.take_along_axis(table, (jnp.arange(top)[None, :] + offset_by) % top, axis=1)


def load_shares(count, total, bound, skew, full):
    portions = [(1 << 20) // math.isqrt(rank ** skew) + 1 for rank in range(1, count + 1)]
    largest = bound if full else min(bound, max(-(-total // count), total * portions[0] // sum(portions)))
    least = 1 if total - largest >= count - 1 else 0
    holding, surplus = [largest] + [least] * (count - 1), total - largest - least * (count - 1)
    while surplus > 0:
        movable = [i for i in range(1, count) if holding[i] < largest] or [i for i in range(1, count) if holding[i] < bound]
        mass, remaining = sum([portions[i] for i in movable]), surplus
        for i in movable:
            extra = min(bound - holding[i], max(1, remaining * portions[i] // mass), surplus)
            holding[i] = holding[i] + extra
            surplus = surplus - extra
    return np.array(holding)


def scatter_about(key, extent, scale, reach, cuts=(), kind=jnp.bfloat16):
    array = scale * jax.random.normal(key, extent, jnp.float32)
    if cuts:
        array = array * block_levels(key, extent, cuts, -0.22, 0.18)
    return jnp.clip(array, -reach, reach).astype(kind)


def setup_inputs(seed: int = 0) -> dict:
    streams_of = jax.random.split(jax.random.key(seed), 19)
    tokens = scatter_about(streams_of[0], (MB, GROUPS, SLOTS, ROWS, D), 1.0, 6.0, ((1, 4), (2, 32)))
    prior_logits = scatter_about(streams_of[1], (MB, GROUPS, SLOTS, ROWS, TARGETS), 0.5, 3.0, ((1, 4), (2, 32)), jnp.float32)
    routes_keys = jax.random.split(jax.random.fold_in(streams_of[2], 1), MB * GROUPS * SLOTS * ROWS // ROWS)
    routes_turns = jax.random.permutation(jax.random.fold_in(streams_of[2], 3), MB * GROUPS * SLOTS * ROWS // ROWS)
    routes = jax.vmap(lambda own, number: shared_out(jax.random.fold_in(streams_of[2], 2), own, number, ROWS, TARGETS, TOP, CAP, 1))(routes_keys, routes_turns).reshape((MB, GROUPS, SLOTS, ROWS, TOP))
    drops = plant((jax.random.randint(streams_of[3], (MB, GROUPS, SLOTS, ROWS, TOP), 0, 8) < 1).astype(jnp.int32), jax.random.fold_in(streams_of[3], 1), 0, 1)
    cont_lengths = jax.vmap(lambda own: ragged(own, SLOTS, SLOTS * CLEN * 3 // 4, CLEN, 1))(jax.random.split(streams_of[4], MB * GROUPS)).reshape((MB, GROUPS, SLOTS)).astype(jnp.int32)
    norm_gain = jnp.clip(1.0 + 0.1 * jax.random.normal(streams_of[5], (D,), jnp.float32), 0.5, 1.5).astype(jnp.bfloat16)
    w_query = scatter_about(streams_of[6], (D, D), D ** -0.5, 0.21875)
    w_key = scatter_about(streams_of[7], (D, D), D ** -0.5, 0.21875)
    w_value = scatter_about(streams_of[8], (D, D), D ** -0.5, 0.21875)
    w_out = scatter_about(streams_of[9], (D, D), (D // 64) ** -0.5, 1.75)
    ffn_gain = jnp.clip(1.0 + 0.1 * jax.random.normal(streams_of[10], (D,), jnp.float32), 0.5, 1.5).astype(jnp.bfloat16)
    w_router = scatter_about(streams_of[11], (D, TARGETS), (4 * D) ** -0.5, 0.109375)
    w_const = scatter_about(streams_of[12], (CONSTS, D, 2), D ** -0.5, 0.21875)
    const_vec = scatter_about(streams_of[13], (CONSTS, D), 4.0, 24.0)
    w_gate = scatter_about(streams_of[14], (EXPERTS, D, FF), D ** -0.5, 0.21875, ((0, 8),))
    w_up = scatter_about(streams_of[15], (EXPERTS, D, FF), D ** -0.5, 0.21875, ((0, 8),))
    w_down = scatter_about(streams_of[16], (EXPERTS, FF, D), (FF // 64) ** -0.5, 1.0, ((0, 8),))
    out_grad = scatter_about(streams_of[17], (MB, GROUPS, SLOTS, ROWS, D), 1.0, 6.0, ((1, 4), (2, 32)))
    return dict(tokens=tokens, prior_logits=prior_logits, routes=routes, drops=drops, cont_lengths=cont_lengths, norm_gain=norm_gain, w_query=w_query, w_key=w_key, w_value=w_value, w_out=w_out, ffn_gain=ffn_gain, w_router=w_router, w_const=w_const, const_vec=const_vec, w_gate=w_gate, w_up=w_up, w_down=w_down, out_grad=out_grad)


@jax.custom_vjp
def low(v):
    return lax.optimization_barrier(v.astype(jnp.bfloat16)).astype(jnp.float32)

@jax.custom_vjp
def low_back(v):
    return v

def low_keep(v):
    return (low(v), None)

def low_pass(kept, grad):
    return (grad,)

def back_keep(v):
    return (v, None)

def back_low(kept, grad):
    return (low(grad),)
low.defvjp(low_keep, low_pass)
low_back.defvjp(back_keep, back_low)
highest = lax.Precision.HIGHEST
norm_eps = 1e-05
very_low = -1e+30

def rms_scale(values_in, gain_vec):
    return values_in * lax.rsqrt(lax.optimization_barrier(jnp.mean(values_in * values_in, axis=-1, keepdims=True)) + norm_eps) * gain_vec

def attend(queries, key_rows, value_rows, allowed):
    score_scale = 1.0 / math.sqrt(HEAD_SIZE)
    scores = low_back(jnp.einsum('qhd,khd->hqk', queries, key_rows, precision=highest) * score_scale)
    scores = jnp.where(allowed[None], scores, very_low)
    row_max = lax.optimization_barrier(jnp.max(scores, axis=-1, keepdims=True))
    weights = jnp.where(allowed[None], jnp.exp(scores - row_max), 0.0)
    prob_low = low(weights / lax.optimization_barrier(jnp.sum(weights, axis=-1, keepdims=True)))
    return jnp.einsum('hqk,khd->qhd', prob_low, value_rows, precision=highest)

def mixture(two_float, router_w, prior_row, const_w, const_v, route_out, route_ids, active):
    logits = jnp.dot(two_float, router_w, precision=highest) + prior_row
    chances = jax.nn.softmax(logits, axis=-1)
    target_hot = (route_ids[..., None] == jnp.arange(TARGETS, dtype=jnp.int32)).astype(jnp.float32)
    route_gate = lax.optimization_barrier(jnp.sum(target_hot * chances[..., None, :], axis=-1)) * active.astype(jnp.float32)
    mixed_out = lax.optimization_barrier(jnp.sum(route_gate[..., None] * route_out, axis=-2))
    copy_gate = lax.optimization_barrier(jnp.sum(route_gate * (route_ids == EXPERTS + 1).astype(jnp.float32), axis=-1))
    mixed_out = mixed_out + copy_gate[..., None] * two_float
    for const_index in range(CONSTS):
        shares = jax.nn.softmax(jnp.dot(two_float, const_w[const_index], precision=highest), axis=-1)
        const_gate = lax.optimization_barrier(jnp.sum(route_gate * (route_ids == EXPERTS + 2 + const_index).astype(jnp.float32), axis=-1))
        mixed_out = mixed_out + const_gate[..., None] * (shares[..., 0:1] * two_float + shares[..., 1:2] * const_v[const_index])
    return mixed_out

def group_forward(params, tokens_g, prior_g, route_ids, active):
    norm_gain, w_query, w_key, w_value, w_out, ffn_gain, w_router, w_const, const_vec, w_gate, w_up, w_down = params
    slot_count = tokens_g.shape[0]
    normed = low(rms_scale(tokens_g, norm_gain))

    def project(weight):
        return low_back(low(jnp.dot(normed, weight, precision=highest))).reshape(slot_count, ROWS, HEADS, HEAD_SIZE)
    queries = project(w_query)
    key_all = project(w_key)
    value_all = project(w_value)
    prompt_q = queries[:, :PROMPT_DEV].reshape(PROMPT, HEADS, HEAD_SIZE)
    prompt_k = key_all[:, :PROMPT_DEV].reshape(PROMPT, HEADS, HEAD_SIZE)
    prompt_v = value_all[:, :PROMPT_DEV].reshape(PROMPT, HEADS, HEAD_SIZE)
    block_rows = math.gcd(PROMPT, 512)
    key_pos = jnp.arange(PROMPT, dtype=jnp.int32)

    def prompt_block(block_id):
        first_row = block_id * block_rows
        query_block = lax.dynamic_slice_in_dim(prompt_q, first_row, block_rows, 0)
        allowed = (first_row + jnp.arange(block_rows, dtype=jnp.int32))[:, None] >= key_pos[None, :]
        return attend(query_block, prompt_k, prompt_v, allowed)
    prompt_out = lax.map(jax.checkpoint(prompt_block), jnp.arange(PROMPT // block_rows, dtype=jnp.int32))
    prompt_out = prompt_out.reshape(slot_count, PROMPT_DEV, D)
    causal = jnp.arange(CLEN)[:, None] >= jnp.arange(CLEN)[None, :]
    cont_allowed = jnp.concatenate([jnp.ones((CLEN, PROMPT), dtype=bool), causal], axis=1)

    def cont_block(pieces):
        cont_q, cont_k, cont_v = pieces
        return attend(cont_q, jnp.concatenate([prompt_k, cont_k], axis=0), jnp.concatenate([prompt_v, cont_v], axis=0), cont_allowed)
    cont_out = lax.map(jax.checkpoint(cont_block), (queries[:, PROMPT_DEV:], key_all[:, PROMPT_DEV:], value_all[:, PROMPT_DEV:]))
    attended = jnp.concatenate([prompt_out, cont_out.reshape(slot_count, CLEN, D)], axis=1)
    attended = low_back(low(attended))
    branch = low_back(jnp.dot(attended, w_out, precision=highest))
    residual = tokens_g + branch
    normed_two = low(rms_scale(residual, ffn_gain))
    routed_use = active * (route_ids < EXPERTS).astype(jnp.int32)
    expert_hot = (route_ids[..., None] == jnp.arange(EXPERTS, dtype=jnp.int32)).astype(jnp.int32) * routed_use[..., None]
    flat_hot = expert_hot.reshape(slot_count, ROWS * TOP, EXPERTS)
    route_rank = lax.optimization_barrier(jnp.sum((jnp.cumsum(flat_hot, axis=1) - 1) * flat_hot, axis=-1)).astype(jnp.int32).reshape(slot_count, ROWS, TOP)
    slot_ids = jnp.arange(slot_count, dtype=jnp.int32)[:, None, None]
    buffer_size = EXPERTS * slot_count * CAP
    flat_pos = jnp.where(routed_use > 0, (route_ids * slot_count + slot_ids) * CAP + route_rank, buffer_size).astype(jnp.int32).reshape(-1)
    routed = jnp.broadcast_to(normed_two[:, :, None, :], (slot_count, ROWS, TOP, D)).reshape(-1, D)
    buffer = jnp.zeros((buffer_size, D), jnp.float32).at[flat_pos].set(routed, mode='drop')
    expert_in = low_back(buffer).reshape(EXPERTS, slot_count * CAP, D)
    gate_pre = low_back(jnp.einsum('ecd,edf->ecf', expert_in, w_gate, precision=highest))
    up_pre = low_back(jnp.einsum('ecd,edf->ecf', expert_in, w_up, precision=highest))
    hidden = low(jax.nn.silu(gate_pre) * up_pre)
    expert_out = low_back(low(jnp.einsum('ecf,efd->ecd', hidden, w_down, precision=highest))).reshape(buffer_size, D)
    route_out = jnp.take(expert_out, flat_pos, axis=0, mode='fill', fill_value=0.0).reshape(slot_count, ROWS, TOP, D)
    return residual + mixture(normed_two, w_router, prior_g, w_const, const_vec, route_out, route_ids, active)

def reference(tokens, prior_logits, routes, drops, cont_lengths, norm_gain, w_query, w_key, w_value, w_out, ffn_gain, w_router, w_const, const_vec, w_gate, w_up, w_down, out_grad):
    group_count = MB * GROUPS
    cont_live = (jnp.arange(CLEN, dtype=jnp.int32)[None, None, None, :] < cont_lengths[..., None]).astype(jnp.int32)
    row_live = jnp.concatenate([jnp.ones((MB, GROUPS, SLOTS, PROMPT_DEV), jnp.int32), cont_live], axis=-1)
    active = (1 - drops) * row_live[..., None]
    params = tuple((weight_in.astype(jnp.float32) for weight_in in (norm_gain, w_query, w_key, w_value, w_out, ffn_gain, w_router, w_const, const_vec, w_gate, w_up, w_down)))
    tokens_f = tokens.astype(jnp.float32).reshape(group_count, SLOTS, ROWS, D)
    prior_f = prior_logits.reshape(group_count, SLOTS, ROWS, TARGETS)
    route_f = routes.reshape(group_count, SLOTS, ROWS, TOP)
    active_f = active.reshape(group_count, SLOTS, ROWS, TOP)

    def forward(params_in, tokens_in, prior_in):

        def group_step(unused_in, pieces):
            return (unused_in, jax.checkpoint(group_forward)(params_in, *pieces))
        unused_out, outputs = lax.scan(group_step, jnp.zeros((), jnp.float32), (tokens_in, prior_in, route_f, active_f))
        return outputs
    layer_out, pullback = jax.vjp(forward, params, tokens_f, prior_f)
    param_grads, token_grads, prior_grads = pullback(out_grad.astype(jnp.float32).reshape(group_count, SLOTS, ROWS, D))
    shape_full = (MB, GROUPS, SLOTS, ROWS)
    return (layer_out.reshape(shape_full + (D,)).astype(jnp.bfloat16), token_grads.reshape(shape_full + (D,)).astype(jnp.bfloat16), prior_grads.reshape(shape_full + (TARGETS,)), param_grads[0], param_grads[1], param_grads[2], param_grads[3], param_grads[4], param_grads[5], param_grads[6], param_grads[7], param_grads[8], param_grads[9], param_grads[10], param_grads[11])
```

```python
import functools
import math

import jax
import jax.numpy as jnp
from jax import lax
from jax.experimental import pallas as pl
from jax.experimental.pallas import tpu as pltpu
from jax.sharding import Mesh, PartitionSpec as P

HEADS = 12
HEAD_SIZE = 64
EXPERTS = 8
CONSTS = 2
TARGETS = 12
CLEN = 128
QUAD = 4
LANES = 128

norm_eps = 1e-05
very_low = -1e30
highest = lax.Precision.HIGHEST
f32 = jnp.float32
bf16 = jnp.bfloat16
CHIPS = ("context", "z")
ALL_CHIPS = ("dp", "context", "z")
EXPERT = ("z", "core")


def dot_nn(left, right, **kw):
    return jnp.dot(left, right, preferred_element_type=f32, **kw)


def dot_nt(left, right, **kw):
    return lax.dot_general(left, right, (((1,), (1,)), ((), ())), preferred_element_type=f32, **kw)


def dot_tn(left, right, **kw):
    return lax.dot_general(left, right, (((0,), (0,)), ((), ())), preferred_element_type=f32, **kw)


def iota(shape, dim):
    return lax.broadcasted_iota(jnp.int32, shape, dim)


def params():
    return pltpu.CompilerParams(vmem_limit_bytes=63_400_000)


def head_masks(dtype):
    lane_head = iota((1, QUAD * HEAD_SIZE), 1) // HEAD_SIZE
    return [(lane_head == h).astype(f32).astype(dtype) for h in range(QUAD)]


def spread(rows, prompt, dtype):
    masks = head_masks(dtype)
    return jnp.concatenate(
        [rows[:prompt] * m for m in masks] + [rows[prompt:] * m for m in masks], axis=0
    )


def gather_heads(stacked, prompt, dtype):
    masks = head_masks(dtype)
    top, low = 0.0, 0.0
    first = QUAD * prompt
    for h in range(QUAD):
        top = top + stacked[h * prompt : (h + 1) * prompt] * masks[h]
        low = low + stacked[first + h * CLEN : first + (h + 1) * CLEN] * masks[h]
    return jnp.concatenate([top, low], axis=0)


def key_slots(core, keys, prompt, shape, dim):
    j = iota(shape, dim)
    half = keys // 2
    other = (j >= half).astype(jnp.int32)
    slot = ((j - other * half) // prompt) * 2 + jnp.where(other > 0, 1 - core, core)
    return slot * prompt + (j & (prompt - 1))


def attn_fwd_kernel(
    base_ref, normed_ref, near_ref, far_ref, wq_ref, wkv_ref, o_ref, lse_ref, q_ref, kv_ref
):
    prompt = q_ref.shape[0] - CLEN
    keys = kv_ref.shape[0] - CLEN
    half = keys // 2
    wide = QUAD * HEAD_SIZE
    masks = head_masks(bf16)
    masks_f = head_masks(f32)
    ones = jnp.ones((8, LANES), f32)

    def to_row(column):
        spare = jnp.where(iota((column.shape[0], LANES), 1) == 0, column, 0.0)
        return dot_nt(ones, spare, precision=highest)

    q = dot_nn(normed_ref[...], wq_ref[...]).astype(bf16).astype(f32)
    q_ref[...] = (q * (1.0 / math.sqrt(HEAD_SIZE))).astype(bf16)
    w_kv = wkv_ref[...]
    for rows, at in ((near_ref, 0), (far_ref, half)):
        for r in range(0, half, 512):
            kv_ref[at + r : at + r + 512] = dot_nn(rows[r : r + 512], w_kv).astype(bf16)
    kv_ref[keys:] = dot_nn(normed_ref[prompt:], w_kv).astype(bf16)
    q_top, q_low = q_ref[:prompt], q_ref[prompt:]
    q_p = jnp.concatenate([q_top * m for m in masks], axis=0)
    s = dot_nt(q_p, kv_ref[:keys, :wide])
    limit = base_ref[0] + (iota((QUAD * prompt, 1), 0) & (prompt - 1))
    s = jnp.where(key_slots(base_ref[1], keys, prompt, (1, keys), 1) <= limit, s, very_low)
    top = jnp.max(s, axis=1, keepdims=True)
    p = jnp.exp(s - top)
    total = jnp.sum(p, axis=1, keepdims=True)
    out = dot_nn(p.astype(bf16), kv_ref[:keys, wide:]) * (1.0 / total)
    lse_ref[:, : QUAD * prompt] = to_row(top + jnp.log(total))
    o_ref[:prompt] = sum(out[h * prompt : (h + 1) * prompt] * masks_f[h] for h in range(QUAD))
    low_out = 0.0
    per = 2
    for part in range(QUAD // per):
        hs = range(part * per, (part + 1) * per)
        rows = per * CLEN
        q_c = jnp.concatenate([q_low * masks[h] for h in hs], axis=0)
        s = dot_nt(q_c, kv_ref[:keys, :wide])
        own = dot_nt(q_c, kv_ref[keys:, :wide])
        own = jnp.where(
            iota((1, CLEN), 1) <= (iota((rows, 1), 0) & (CLEN - 1)), own, very_low
        )
        top = jnp.maximum(
            jnp.max(s, axis=1, keepdims=True), jnp.max(own, axis=1, keepdims=True)
        )
        p = jnp.exp(s - top)
        p_own = jnp.exp(own - top)
        total = jnp.sum(p, axis=1, keepdims=True) + jnp.sum(p_own, axis=1, keepdims=True)
        out = dot_nn(p.astype(bf16), kv_ref[:keys, wide:])
        out = out + dot_nn(p_own.astype(bf16), kv_ref[keys:, wide:])
        out = out * (1.0 / total)
        at = QUAD * prompt + part * rows
        lse_ref[:, at : at + rows] = to_row(top + jnp.log(total))
        for i, h in enumerate(hs):
            low_out = low_out + out[i * CLEN : (i + 1) * CLEN] * masks_f[h]
    o_ref[prompt:] = low_out


def attn_fwd(base, normed, near, far, w_query, w_kv):
    rows, width = normed.shape
    half = near.shape[0]
    every = 2 * half + CLEN
    quads = HEADS // QUAD
    wide = QUAD * HEAD_SIZE
    col = lambda n, w=wide: pl.BlockSpec((n, w), lambda g, b: (0, g))
    whole = lambda n: pl.BlockSpec((n, width), lambda g, b: (0, 0))
    return pl.pallas_call(
        attn_fwd_kernel,
        grid_spec=pltpu.PrefetchScalarGridSpec(
            num_scalar_prefetch=1,
            grid=(quads,),
            in_specs=[whole(rows), whole(half), whole(half), col(width), col(width, 2 * wide)],
            out_specs=[
                col(rows),
                pl.BlockSpec((None, 8, QUAD * rows), lambda g, b: (g, 0, 0)),
                col(rows),
                col(every, 2 * wide),
            ],
        ),
        out_shape=[
            jax.ShapeDtypeStruct((rows, width), f32),
            jax.ShapeDtypeStruct((quads, 8, QUAD * rows), f32),
            jax.ShapeDtypeStruct((rows, width), bf16),
            jax.ShapeDtypeStruct((every, 2 * width), bf16),
        ],
        compiler_params=params(),
        cost_estimate=pl.CostEstimate(
            flops=16 * rows * every * width + 4 * every * width * width,
            bytes_accessed=4 * every * width,
            transcendentals=rows * every * HEADS,
        ),
        name="attn_fwd",
    )(base, normed, near, far, w_query, w_kv)


def attn_bwd_kernel(
    base_ref, q_ref, kv_ref, do_ref, o_ref, lse_ref, dq_ref, dkv_ref, qm, dom, dqt, *, block
):
    prompt = q_ref.shape[0] - CLEN
    keys = kv_ref.shape[0] - CLEN
    wide = QUAD * HEAD_SIZE
    qm[...] = spread(q_ref[...], prompt, bf16)
    dom[...] = spread(do_ref[...], prompt, bf16)
    prod = spread(do_ref[...].astype(f32) * o_ref[...], prompt, f32)
    delta = dot_nt(jnp.ones((8, prod.shape[1]), f32), prod, precision=highest)[0:1]
    lse = lse_ref[0:1, :]
    first = QUAD * prompt
    limit = base_ref[0] + (iota((1, first), 1) & (prompt - 1))
    q_all, do_all = qm[...], dom[...]

    def one(rows, mask):
        kk, vv = kv_ref[rows, :wide], kv_ref[rows, wide:]
        p = jnp.exp(dot_nt(kk, q_all) - lse)
        p = mask(p)
        ds = p * (dot_nt(vv, do_all) - delta)
        pb, dsb = p.astype(bf16), ds.astype(bf16)
        dkv_ref[rows, :wide] = dot_nn(dsb, q_all).astype(bf16)
        dkv_ref[rows, wide:] = dot_nn(pb, do_all).astype(bf16)
        return dot_tn(kk, dsb)

    def own_mask(p):
        lane = iota((1, p.shape[1]), 1)
        own_row = jnp.where(lane < first, -1, (lane - first) & (CLEN - 1))
        return jnp.where(iota((CLEN, 1), 0) <= own_row, p, 0.0)

    dqt[...] = one(pl.ds(keys, CLEN), own_mask)

    def step(i, unused):
        at = pl.multiple_of(i * block, block)

        def mask(p):
            half = (at >= keys // 2).astype(jnp.int32)
            core = jnp.where(half > 0, 1 - base_ref[1], base_ref[1])
            j = at - half * (keys // 2) + iota((block, 1), 0)
            where = ((j // prompt) * 2 + core) * prompt + (j & (prompt - 1))
            seen = where <= limit
            return jnp.concatenate([jnp.where(seen, p[:, :first], 0.0), p[:, first:]], axis=1)

        dqt[...] += one(pl.ds(at, block), mask)
        return unused

    lax.fori_loop(0, keys // block, step, 0)
    dq = gather_heads(dqt[...].T, prompt, f32)
    dq_ref[...] = (dq * (1.0 / math.sqrt(HEAD_SIZE))).astype(bf16)


def attn_bwd(base, q, kv, do, o, lse, block=256):
    rows, width = q.shape
    every = kv.shape[0]
    quads = HEADS // QUAD
    wide = QUAD * HEAD_SIZE
    col = lambda n, w=wide: pl.BlockSpec((n, w), lambda g, b: (0, g))
    return pl.pallas_call(
        functools.partial(attn_bwd_kernel, block=block),
        grid_spec=pltpu.PrefetchScalarGridSpec(
            num_scalar_prefetch=1,
            grid=(quads,),
            in_specs=[
                col(rows), col(every, 2 * wide), col(rows), col(rows),
                pl.BlockSpec((None, 8, QUAD * rows), lambda g, b: (g, 0, 0)),
            ],
            out_specs=[col(rows), col(every, 2 * wide)],
            scratch_shapes=[
                pltpu.VMEM((QUAD * rows, wide), bf16),
                pltpu.VMEM((QUAD * rows, wide), bf16),
                pltpu.VMEM((wide, QUAD * rows), f32),
            ],
        ),
        out_shape=[
            jax.ShapeDtypeStruct((rows, width), bf16),
            jax.ShapeDtypeStruct((every, 2 * width), bf16),
        ],
        compiler_params=params(),
        cost_estimate=pl.CostEstimate(
            flops=40 * rows * every * width,
            bytes_accessed=8 * every * width,
            transcendentals=rows * every * HEADS,
        ),
        name="attn_bwd",
    )(base, q, kv, do, o, lse)


def route_kernel(
    x_ref, attn_ref, wout_ref, gain_ref, wr_ref, prior_ref, eff_ref, efft_ref, og_ref,
    resid_ref, two_ref, ch_ref, send_ref, sel_ref, selt_ref, gate_ref, *, cap,
):
    rows, width = x_ref.shape
    slots = EXPERTS * cap
    resid = x_ref[...].astype(f32) + dot_nn(attn_ref[...].astype(bf16), wout_ref[...])
    resid_ref[...] = resid
    inv = lax.rsqrt(jnp.mean(resid * resid, axis=1, keepdims=True) + norm_eps)
    two = (resid * inv * gain_ref[...]).astype(bf16)
    two_ref[...] = two
    lane = iota((1, LANES), 1)
    logits = dot_nn(two, wr_ref[...]) + prior_ref[...]
    masked = jnp.where(lane < TARGETS, logits, very_low)
    e = jnp.exp(masked - jnp.max(masked, axis=1, keepdims=True))
    ch = e * (1.0 / jnp.sum(e, axis=1, keepdims=True))
    for j in range(CONSTS):
        at = TARGETS + 2 * j
        diff = logits[:, at + 1 : at + 2] - logits[:, at : at + 1]
        ch = jnp.where(lane == at, 1.0 / (1.0 + jnp.exp(diff)), ch)
        ch = jnp.where(lane == at + 1, 1.0 / (1.0 + jnp.exp(-diff)), ch)
    ch_ref[...] = ch
    target = iota((16, rows), 0)
    hot_t = ((target == efft_ref[0:1, :]) | (target == efft_ref[1:2, :])).astype(f32)
    before = (iota((rows, rows), 0) < iota((rows, rows), 1)).astype(f32).astype(bf16)
    rank_t = dot_nn(hot_t.astype(bf16), before)
    rank_t = jnp.where(hot_t > 0.0, rank_t, -1.0)
    place = iota((cap, 1), 0).astype(f32)
    sel = jnp.concatenate(
        [(place == rank_t[i : i + 1, :]).astype(f32) for i in range(EXPERTS)], axis=0
    )
    sel_b = sel.astype(bf16)
    sel_ref[...] = sel_b
    hot = ((lane == eff_ref[:, 0:1]) | (lane == eff_ref[:, 1:2])).astype(f32)
    after = (iota((rows, rows), 0) > iota((rows, rows), 1)).astype(f32).astype(bf16)
    rank = dot_nn(after, hot.astype(bf16))
    rank = jnp.where(hot > 0.0, rank, -1.0)
    slot = iota((1, slots), 1)
    widen = (slot // cap == iota((LANES, 1), 0)).astype(f32).astype(bf16)
    rank_s = dot_nn(rank.astype(bf16), widen)
    selt_ref[...] = (rank_s == (slot % cap).astype(f32)).astype(f32).astype(bf16)
    ch_s = dot_nn(sel, ch, precision=highest)
    of_slot = iota((slots, 1), 0) // cap
    gate = jnp.sum(jnp.where(lane == of_slot, ch_s, 0.0), axis=1, keepdims=True)
    gate_ref[...] = jnp.broadcast_to(gate, gate_ref.shape)
    send_ref[:, :width] = dot_nn(sel_b, two).astype(bf16)
    send_ref[:, width:] = (gate * dot_nn(sel_b, og_ref[...])).astype(bf16)


def route(x, attn, w_out, gain, wr, prior, eff, efft, og, cap):
    rows, width = x.shape
    slots = EXPERTS * cap
    return pl.pallas_call(
        functools.partial(route_kernel, cap=cap),
        out_shape=[
            jax.ShapeDtypeStruct((rows, width), f32),
            jax.ShapeDtypeStruct((rows, width), bf16),
            jax.ShapeDtypeStruct((rows, LANES), f32),
            jax.ShapeDtypeStruct((slots, 2 * width), bf16),
            jax.ShapeDtypeStruct((slots, rows), bf16),
            jax.ShapeDtypeStruct((rows, slots), bf16),
            jax.ShapeDtypeStruct((slots, LANES), f32),
        ],
        compiler_params=params(),
        cost_estimate=pl.CostEstimate(
            flops=6 * rows * width * width, bytes_accessed=4 * width * width, transcendentals=0
        ),
        name="route",
    )(x, attn, w_out, gain, wr, prior, eff, efft, og)


def expert_kernel(
    x_ref, g_ref, wg_ref, wu_ref, wd_ref, out_ref, hid_ref, gg_ref, ug_ref, fwd, back
):
    step = pl.program_id(0)
    width = x_ref.shape[1]

    @pl.when(step == 0)
    def _():
        fwd[...] = jnp.zeros_like(fwd)
        back[...] = jnp.zeros_like(back)

    x, g = x_ref[...], g_ref[...]
    gate = dot_nn(x, wg_ref[...])
    up = dot_nn(x, wu_ref[...])
    hid_grad = dot_nt(g, wd_ref[...])
    sig = 1.0 / (1.0 + jnp.exp(-gate))
    act = gate * sig
    hid = (act * up).astype(bf16)
    gg = (hid_grad * up * (sig + act * (1.0 - sig))).astype(bf16)
    ug = (hid_grad * act).astype(bf16)
    hid_ref[...] = hid
    gg_ref[...] = gg
    ug_ref[...] = ug
    fwd[...] += dot_nn(hid, wd_ref[...])
    back[...] += dot_nt(gg, wg_ref[...]) + dot_nt(ug, wu_ref[...])

    @pl.when(step == pl.num_programs(0) - 1)
    def _():
        out_ref[:, :width] = fwd[...].astype(bf16)
        out_ref[:, width:] = back[...].astype(bf16)


def experts(rows_in, w_gate, w_up, w_down, tile=256):
    rows = rows_in.shape[0]
    width = rows_in.shape[1] // 2
    hidden = w_gate.shape[2]
    half = lambda i: pl.BlockSpec((rows, width), lambda t, i=i: (0, i))
    inner = pl.BlockSpec((None, width, tile), lambda t: (0, 0, t))
    mid = pl.BlockSpec((rows, tile), lambda t: (0, t))
    return pl.pallas_call(
        expert_kernel,
        grid=(hidden // tile,),
        in_specs=[half(0), half(1), inner, inner, pl.BlockSpec((None, tile, width), lambda t: (0, t, 0))],
        out_specs=[pl.BlockSpec((rows, 2 * width), lambda t: (0, 0)), mid, mid, mid],
        out_shape=[jax.ShapeDtypeStruct((rows, 2 * width), bf16)]
        + [jax.ShapeDtypeStruct((rows, hidden), bf16)] * 3,
        scratch_shapes=[pltpu.VMEM((rows, width), f32), pltpu.VMEM((rows, width), f32)],
        compiler_params=params(),
        cost_estimate=pl.CostEstimate(
            flops=14 * rows * width * hidden,
            bytes_accessed=6 * width * hidden,
            transcendentals=rows * hidden,
        ),
        name="experts",
    )(rows_in, rows_in, w_gate, w_up, w_down)


def expert_wgrad_kernel(*refs, count):
    ins, (dg_ref, du_ref, dd_ref, xt) = refs[: 5 * count], refs[5 * count :]
    rows = ins[0].shape[0]

    @pl.when(pl.program_id(0) == 0)
    def _():
        for m in range(count):
            xt[:, m * rows : (m + 1) * rows] = ins[5 * m][...].T

    g, hid, gg, ug = (
        jnp.concatenate([ins[5 * m + i][...] for m in range(count)], axis=0) for i in range(1, 5)
    )
    dg_ref[...] = dot_nn(xt[...], gg).astype(bf16)
    du_ref[...] = dot_nn(xt[...], ug).astype(bf16)
    dd_ref[...] = dot_tn(hid, g).astype(bf16)


def expert_wgrad(parts, tile=256):
    rows = parts[0][0].shape[0]
    width = parts[0][0].shape[1] // 2
    hidden = parts[0][1].shape[1]
    half = lambda i: pl.BlockSpec((rows, width), lambda t, i=i: (0, i))
    mid = pl.BlockSpec((rows, tile), lambda t: (0, t))
    specs, args = [], []
    for rows_in, hid, gg, ug in parts:
        specs += [half(0), half(1), mid, mid, mid]
        args += [rows_in, rows_in, hid, gg, ug]
    inner = pl.BlockSpec((width, tile), lambda t: (0, t))
    return pl.pallas_call(
        functools.partial(expert_wgrad_kernel, count=len(parts)),
        grid=(hidden // tile,),
        in_specs=specs,
        out_specs=[inner, inner, pl.BlockSpec((tile, width), lambda t: (t, 0))],
        out_shape=[
            jax.ShapeDtypeStruct((width, hidden), bf16),
            jax.ShapeDtypeStruct((width, hidden), bf16),
            jax.ShapeDtypeStruct((hidden, width), bf16),
        ],
        scratch_shapes=[pltpu.VMEM((width, len(parts) * rows), bf16)],
        compiler_params=params(),
        cost_estimate=pl.CostEstimate(
            flops=6 * len(parts) * rows * width * hidden,
            bytes_accessed=6 * width * hidden,
            transcendentals=0,
        ),
        name="expert_wgrad",
    )(*args)


def combine_kernel(
    resid_ref, two_ref, ch_ref, eff_ref, og_ref, ret_ref, sel_ref, selt_ref, gate_ref,
    wout_ref, gain_ref, wr_ref, cv_ref,
    mixed_ref, rtot_ref, branch_ref, ag_ref, dl_ref, small_ref, *, cap,
):
    rows, width = resid_ref.shape
    slots = EXPERTS * cap
    lane = iota((1, LANES), 1)
    resid, two_b, ch = resid_ref[...], two_ref[...], ch_ref[...]
    two = two_b.astype(f32)
    og_b = og_ref[...]
    og = og_b.astype(f32)
    eo = ret_ref[:, :width].astype(f32)
    sel, selt = sel_ref[...], selt_ref[...]
    hot = ((lane == eff_ref[:, 0:1]) | (lane == eff_ref[:, 1:2])).astype(f32)
    dgate = jnp.sum(dot_nn(sel, og_b) * eo, axis=1, keepdims=True)
    by_target = jnp.where(lane == iota((slots, 1), 0) // cap, dgate, 0.0)
    dval = dot_nn(selt.astype(f32), by_target, precision=highest)
    self_dot = jnp.sum(og * two, axis=1, keepdims=True)
    cv_dot = dot_nt(og_b, cv_ref[...])
    gates = ch * hot
    keep = gates[:, EXPERTS + 1 : EXPERTS + 2]
    dval = jnp.where(lane == EXPERTS + 1, self_dot, dval)
    mixed = resid + dot_nn(selt, (gate_ref[:, 0:1] * eo).astype(bf16))
    dl_const = jnp.zeros((rows, LANES), f32)
    coef_cv = jnp.zeros((rows, LANES), f32)
    for j in range(CONSTS):
        e, at = EXPERTS + 2 + j, TARGETS + 2 * j
        a0, a1 = ch[:, at : at + 1], ch[:, at + 1 : at + 2]
        gate = gates[:, e : e + 1]
        with_cv = cv_dot[:, e : e + 1]
        dval = jnp.where(lane == e, a0 * self_dot + a1 * with_cv, dval)
        keep = keep + gate * a0
        mixed = mixed + (gate * a1) * cv_ref[e : e + 1, :].astype(f32)
        coef_cv = jnp.where(lane == TARGETS + 2 * CONSTS + j, gate * a1, coef_cv)
        da0, da1 = gate * self_dot, gate * with_cv
        mean = a0 * da0 + a1 * da1
        dl_const = jnp.where(lane == at, a0 * (da0 - mean), dl_const)
        dl_const = jnp.where(lane == at + 1, a1 * (da1 - mean), dl_const)
    mixed = mixed + keep * two
    mixed_ref[...] = mixed.astype(bf16)
    ch = jnp.where(lane < TARGETS, ch, 0.0)
    dch = hot * dval
    dl = ch * (dch - jnp.sum(ch * dch, axis=1, keepdims=True)) + dl_const
    dl_ref[...] = dl
    dl_hi = dl.astype(bf16)
    dl_lo = (dl - dl_hi.astype(f32)).astype(bf16)
    cc_hi = coef_cv.astype(bf16)
    cc_lo = (coef_cv - cc_hi.astype(f32)).astype(bf16)
    small = dot_tn(dl_hi, two_b) + dot_tn(dl_lo, two_b) + dot_tn(cc_hi, og_b) + dot_tn(cc_lo, og_b)
    two_grad = (
        keep * og
        + dot_nt(dl_hi, wr_ref[...])
        + dot_nt(dl_lo, wr_ref[...])
        + dot_nn(selt, ret_ref[:, width:])
    )
    inv = lax.rsqrt(jnp.mean(resid * resid, axis=1, keepdims=True) + norm_eps)
    xhat = resid * inv
    gain_grad = jnp.sum(two_grad * xhat, axis=0, keepdims=True)
    small_ref[...] = jnp.where(
        iota((small_ref.shape[0], 1), 0) == TARGETS + 3 * CONSTS, gain_grad, small[: small_ref.shape[0]]
    )
    scaled = two_grad * gain_ref[...]
    rtot = og + inv * (scaled - xhat * jnp.mean(scaled * xhat, axis=1, keepdims=True))
    rtot_ref[...] = rtot
    branch = rtot.astype(bf16)
    branch_ref[...] = branch
    ag_ref[...] = dot_nt(branch, wout_ref[...]).astype(bf16)


def combine(resid, two, ch, eff, og, ret, sel, selt, gate, w_out, gain, wr, cv, cap):
    rows, width = resid.shape
    return pl.pallas_call(
        functools.partial(combine_kernel, cap=cap),
        out_shape=[
            jax.ShapeDtypeStruct((rows, width), bf16),
            jax.ShapeDtypeStruct((rows, width), f32),
            jax.ShapeDtypeStruct((rows, width), bf16),
            jax.ShapeDtypeStruct((rows, width), bf16),
            jax.ShapeDtypeStruct((rows, LANES), f32),
            jax.ShapeDtypeStruct((24, width), f32),
        ],
        compiler_params=params(),
        cost_estimate=pl.CostEstimate(
            flops=6 * rows * width * width, bytes_accessed=4 * width * width, transcendentals=0
        ),
        name="combine",
    )(resid, two, ch, eff, og, ret, sel, selt, gate, w_out, gain, wr, cv)


def back_proj_kernel(
    dkv_ref, own_ref, wkv_ref, near_ref, far_ref, normed_ref, dq_ref, wq_ref,
    give_ref, keep_ref, mine_ref, gain_ref, *, steps,
):
    t = pl.program_id(0)

    @pl.when(t == 0)
    def _():
        prompt = normed_ref.shape[0] - CLEN
        mine = dot_nt(dq_ref[...], wq_ref[...])
        low = mine[prompt:] + dot_nt(own_ref[...], wkv_ref[...])
        mine_ref[:prompt] = mine[:prompt]
        mine_ref[prompt:] = low
        normed = normed_ref[...].astype(f32)
        total = jnp.sum(mine[:prompt] * normed[:prompt], axis=0, keepdims=True)
        total = total + jnp.sum(low * normed[prompt:], axis=0, keepdims=True)
        gain_ref[...] = jnp.broadcast_to(total, gain_ref.shape)

    part = dot_nt(dkv_ref[...], wkv_ref[...])

    @pl.when(t < steps)
    def _():
        give_ref[...] = part.astype(bf16)
        gain_ref[...] += jnp.sum(part * far_ref[...].astype(f32), axis=0, keepdims=True)

    @pl.when(t >= steps)
    def _():
        keep_ref[...] = part
        gain_ref[...] += jnp.sum(part * near_ref[...].astype(f32), axis=0, keepdims=True)


def back_proj(dkv, w_kv, near, far, normed, dq, w_query, block=256):
    rows, width = normed.shape
    half = near.shape[0]
    steps = half // block
    whole = lambda n, w=width: pl.BlockSpec((n, w), lambda t: (0, 0))
    first = pl.BlockSpec((block, width), lambda t: (jnp.minimum(t, steps - 1), 0))
    last = pl.BlockSpec((block, width), lambda t: (jnp.maximum(t - steps, 0), 0))
    return pl.pallas_call(
        functools.partial(back_proj_kernel, steps=steps),
        grid=(2 * steps,),
        in_specs=[
            pl.BlockSpec((block, 2 * width), lambda t: ((t + steps) % (2 * steps), 0)),
            pl.BlockSpec((CLEN, 2 * width), lambda t: (2 * half // CLEN, 0)),
            whole(width, 2 * width), last, first, whole(rows), whole(rows), whole(width),
        ],
        out_specs=[first, last, whole(rows), whole(8)],
        out_shape=[
            jax.ShapeDtypeStruct((half, width), bf16),
            jax.ShapeDtypeStruct((half, width), f32),
            jax.ShapeDtypeStruct((rows, width), f32),
            jax.ShapeDtypeStruct((8, width), f32),
        ],
        compiler_params=params(),
        cost_estimate=pl.CostEstimate(
            flops=8 * half * width * width, bytes_accessed=12 * half * width, transcendentals=0
        ),
        name="back_proj",
    )(dkv, dkv, w_kv, near, far, normed, dq, w_query)


PIECES = 8
UNIT = 48
PACK = 160


def dense_wgrad_kernel(core_ref, *refs, count):
    ins = refs[: 9 * count]
    gain_ref, give_ref, keep_ref, every_t, normed_t, attn_t = refs[9 * count :]
    t = pl.program_id(0)
    half_steps = PIECES // 2
    piece = (t + half_steps * (1 - core_ref[0])) % PIECES
    rows, width = ins[2].shape
    prompt = rows - CLEN
    half = ins[0].shape[0]
    each = 2 * half + CLEN

    @pl.when(t == 0)
    def _():
        for m in range(count):
            near, far, normed, attn = (ins[9 * m + i] for i in range(4))
            at = m * each
            every_t[:, at : at + half] = near[...].T
            every_t[:, at + half : at + 2 * half] = far[...].T
            every_t[:, at + 2 * half : at + each] = normed[prompt:].T
            normed_t[:, m * rows : (m + 1) * rows] = normed[...].T
            attn_t[:, m * rows : (m + 1) * rows] = attn[...].astype(bf16).T

    stack = lambda i: jnp.concatenate([ins[9 * m + i][...] for m in range(count)], axis=0)

    def write(grad):
        low = grad.astype(bf16)
        small = sum(ins[9 * m + 7][...] for m in range(count))
        gain = sum(ins[9 * m + 8][0:1, :] for m in range(count)) / gain_ref[...]
        small = jnp.where(
            iota((small.shape[0], 1), 0) == TARGETS + 3 * CONSTS + 1, gain, small
        ).astype(bf16)

        def into(out_ref):
            out_ref[:, 3 * UNIT :, :] = jnp.zeros((16, PACK - 3 * UNIT, LANES), bf16)
            for k in range(16):
                for j in range(3):
                    out_ref[k, j * UNIT : (j + 1) * UNIT, :] = low[
                        k * UNIT : (k + 1) * UNIT, j * LANES : (j + 1) * LANES
                    ]
            for i in range(width // LANES):

                @pl.when(piece == i)
                def _():
                    block = small[:, i * LANES : (i + 1) * LANES]
                    out_ref[0, 3 * UNIT : 3 * UNIT + 16, :] = block[:16]
                    out_ref[1, 3 * UNIT : 3 * UNIT + 8, :] = block[16:24]

        @pl.when(t < half_steps)
        def _():
            into(give_ref)

        @pl.when(t >= half_steps)
        def _():
            into(keep_ref)

    @pl.when(piece < 2)
    def _():
        write(dot_nn(normed_t[...], stack(4)))

    @pl.when((piece >= 2) & (piece < 6))
    def _():
        write(dot_nn(every_t[...], stack(5)))

    @pl.when(piece >= 6)
    def _():
        write(dot_nn(attn_t[...], stack(6)))


def dense_wgrad(core, gain, parts):
    near, _, normed = parts[0][:3]
    rows, width = normed.shape
    half = near.shape[0]
    each = 2 * half + CLEN
    steps = PIECES // 2
    cols = 4 * width // PIECES
    piece = lambda t, c: (t + steps * (1 - c[0])) % PIECES
    whole = lambda n: pl.BlockSpec((n, width), lambda t, c: (0, 0))
    part = lambda n, lo, hi: pl.BlockSpec(
        (n, cols), lambda t, c: (0, jnp.clip(piece(t, c) - lo, 0, hi))
    )
    specs, args = [], []
    for p in parts:
        specs += [
            whole(half), whole(half), whole(rows), whole(rows),
            part(rows, 0, 1), part(each, 2, 3), part(rows, 6, 1), whole(24), whole(8),
        ]
        args += list(p)
    out = lambda f: pl.BlockSpec((16, PACK, LANES), lambda t, c: (f(t), 0, 0))
    count = len(parts)
    return pl.pallas_call(
        functools.partial(dense_wgrad_kernel, count=count),
        grid_spec=pltpu.PrefetchScalarGridSpec(
            num_scalar_prefetch=1,
            grid=(PIECES,),
            in_specs=specs + [whole(1)],
            out_specs=[
                out(lambda t: jnp.minimum(t, steps - 1)), out(lambda t: jnp.maximum(t - steps, 0))
            ],
            scratch_shapes=[
                pltpu.VMEM((width, count * each), bf16),
                pltpu.VMEM((width, count * rows), bf16),
                pltpu.VMEM((width, count * rows), bf16),
            ],
        ),
        out_shape=[jax.ShapeDtypeStruct((16 * steps, PACK, LANES), bf16)] * 2,
        compiler_params=params(),
        cost_estimate=pl.CostEstimate(
            flops=4 * count * each * width * width,
            bytes_accessed=6 * count * each * width,
            transcendentals=0,
        ),
        name="dense_wgrad",
    )(core, *args, gain)


def unpack_kernel(core_ref, mine_ref, other_ref, *outs):
    first = core_ref[0] == 0
    steps = PIECES // 2
    width = outs[0].shape[0]
    sub = QUAD * HEAD_SIZE // LANES
    per = width // LANES
    small_ref = outs[4]

    def take(i, k, lo, hi):
        a = mine_ref[(i % steps) * 16 + k, lo:hi, :]
        b = other_ref[(i % steps) * 16 + k, lo:hi, :]
        pick = first if i < steps else jnp.logical_not(first)
        return jnp.where(pick, a.astype(f32), b.astype(f32))

    for i in range(PIECES):
        for j in range(3):
            block = i * 3 + j
            if block < per:
                out, at = outs[0], block
            elif block < 3 * per:
                g, r = divmod(block - per, 2 * sub)
                out, at = outs[1 + r // sub], g * sub + r % sub
            else:
                out, at = outs[3], block - 3 * per
            for k in range(16):
                out[k * UNIT : (k + 1) * UNIT, at * LANES : (at + 1) * LANES] = take(
                    i, k, j * UNIT, (j + 1) * UNIT
                )
        if i < per:
            cols = slice(i * LANES, (i + 1) * LANES)
            small_ref[:16, cols] = take(i, 0, 3 * UNIT, 3 * UNIT + 16)
            small_ref[16:, cols] = take(i, 1, 3 * UNIT, 3 * UNIT + 16)[:8]


def unpack(core, mine, other, width):
    vmem = pl.BlockSpec(memory_space=pltpu.VMEM)
    return pl.pallas_call(
        unpack_kernel,
        in_specs=[pl.BlockSpec(memory_space=pltpu.SMEM), vmem, vmem],
        out_specs=[vmem] * 5,
        out_shape=[jax.ShapeDtypeStruct((width, width), f32)] * 4
        + [jax.ShapeDtypeStruct((24, width), f32)],
        compiler_params=params(),
        cost_estimate=pl.CostEstimate(
            flops=4 * width * width, bytes_accessed=24 * width * width, transcendentals=0
        ),
        name="unpack",
    )(core, mine, other)


def swap_cores(rows):
    return lax.ppermute(rows, "core", [(0, 1), (1, 0)])


def exchange(blocks, axes):
    return lax.all_to_all(blocks, axes, split_axis=0, concat_axis=0, tiled=True)


def spread_out(piece, axes):
    count = lax.axis_size(axes)
    return exchange(jnp.broadcast_to(piece[None], (count,) + piece.shape), axes)


def after(value, *others):
    return lax.optimization_barrier((value, *others))[0]


def on_device(
    tokens, prior_logits, routes, drops, cont_lengths, norm_gain, w_query, w_key, w_value, w_out,
    ffn_gain, w_router, w_const, const_vec, w_gate, w_up, w_down, out_grad,
):
    micros, rows, width = tokens.shape[0], tokens.shape[3], tokens.shape[4]
    prompt = rows - CLEN
    cap = -(-(rows * 3 // 16) // 8) * 8
    quads, wide = HEADS // QUAD, QUAD * HEAD_SIZE
    chips = lax.axis_size(CHIPS)
    half = chips * prompt
    core = lax.axis_index("core").astype(jnp.int32)
    base = jnp.stack([(lax.axis_index(CHIPS).astype(jnp.int32) * 2 + core) * prompt, core])
    score_scale = 1.0 / math.sqrt(HEAD_SIZE)
    gain_one = norm_gain.astype(f32)
    gain_two = ffn_gain.astype(f32).reshape(1, width)

    x = tokens[:, 0, 0]
    x_f = x.astype(f32)
    inv_one = lax.rsqrt(jnp.mean(x_f * x_f, axis=-1, keepdims=True) + norm_eps)
    normed = (x_f * inv_one * gain_one).astype(bf16)
    gathered = [spread_out(normed[0, :prompt], CHIPS)]
    for m in range(1, micros):
        gathered.append(spread_out(normed[m, :prompt], CHIPS))

    wr = jnp.concatenate(
        [w_router] + [w_const[j] for j in range(CONSTS)]
        + [jnp.zeros((width, LANES - TARGETS - 2 * CONSTS), bf16)], axis=1,
    )
    cv = jnp.zeros((LANES, width), bf16).at[EXPERTS + 2 : EXPERTS + 2 + CONSTS].set(const_vec)
    w_kv = jnp.concatenate(
        [w[:, g * wide : (g + 1) * wide] for g in range(quads) for w in (w_key, w_value)], axis=1
    )
    row_ids = jnp.arange(rows, dtype=jnp.int32)
    og = out_grad[:, 0, 0]
    live = row_ids[None] < prompt + cont_lengths[:, 0]
    active = (1 - drops[:, 0, 0]) * live[..., None].astype(jnp.int32)
    eff = jnp.where(active > 0, routes[:, 0, 0], -1)
    efft = jnp.swapaxes(eff, 1, 2)
    prior = jnp.pad(prior_logits[:, 0, 0], ((0, 0), (0, 0), (0, LANES - TARGETS)))

    st = []
    for m in range(micros):
        s = {}
        s["normed"] = normed[m]
        if m:
            gathered[m] = after(gathered[m], st[m - 1]["attn"])
        s["near"] = gathered[m].reshape(half, width)
        s["far"] = swap_cores(s["near"])
        s["attn"], s["lse"], s["q"], s["kv"] = attn_fwd(
            base, s["normed"], s["near"], s["far"], w_query, w_kv
        )
        s["resid"], s["two"], s["ch"], send, s["sel"], s["selt"], s["gate"] = route(
            x[m], s["attn"], w_out, gain_two, wr, prior[m], eff[m], efft[m], og[m], cap
        )
        s["recv"] = exchange(send.reshape(EXPERTS, cap, 2 * width), EXPERT).reshape(
            EXPERTS * cap, 2 * width
        )
        st.append(s)
    for s in st:
        ret, s["hid"], s["gg"], s["ug"] = experts(s["recv"], w_gate, w_up, w_down)
        s["ret"] = exchange(ret.reshape(EXPERTS, cap, 2 * width), EXPERT).reshape(
            EXPERTS * cap, 2 * width
        )
    wide_grads = expert_wgrad([(s["recv"], s["hid"], s["gg"], s["ug"]) for s in st])
    st[0]["ret"] = after(st[0]["ret"], wide_grads)
    wide_sum = lax.psum(tuple(wide_grads), ("dp", "context"))

    mixed, prior_grads, parts = [], [], []
    for m, s in enumerate(st):
        out, s["rtot"], branch, ag, dl, small = combine(
            s["resid"], s["two"], s["ch"], eff[m], og[m], s["ret"], s["sel"], s["selt"], s["gate"],
            w_out, gain_two, wr, cv, cap,
        )
        mixed.append(out)
        prior_grads.append(dl[:, :TARGETS])
        dq, dkv = attn_bwd(base, s["q"], s["kv"], ag, s["attn"], s["lse"])
        give, keep, s["mine"], gain = back_proj(
            dkv, w_kv, s["near"], s["far"], s["normed"], dq, w_query
        )
        keep = (keep + swap_cores(give).astype(f32)).astype(bf16)
        s["scatter"] = exchange(keep.reshape(chips, prompt, width), CHIPS)
        parts.append(
            (s["near"], s["far"], s["normed"], s["attn"], dq, dkv, branch, small, gain)
        )
    core_arg = core.reshape(1)
    give, keep = dense_wgrad(core_arg, gain_one.reshape(1, width), parts)
    keep = (keep.astype(f32) + swap_cores(give).astype(f32)).astype(bf16)
    own = jnp.sum(exchange(keep, ALL_CHIPS).astype(f32), axis=0).astype(bf16)
    own = after(own, wide_sum)
    own = spread_out(own, ALL_CHIPS)
    *dense, rest = unpack(core_arg, own, swap_cores(own), width)
    token_grads = []
    for m, s in enumerate(st):
        total = jnp.sum(s["scatter"].astype(f32), axis=0)
        grad = (s["mine"] + jnp.pad(total, ((0, CLEN), (0, 0)))) * gain_one
        xhat = x_f[m] * inv_one[m]
        grad = inv_one[m] * (grad - xhat * jnp.mean(grad * xhat, axis=-1, keepdims=True))
        token_grads.append((s["rtot"] + grad).astype(bf16))
    lift = lambda parts: jnp.stack(parts)[:, None, None]
    return (
        lift(mixed),
        lift(token_grads),
        lift(prior_grads),
        rest[TARGETS + 3 * CONSTS + 1],
        *dense,
        rest[TARGETS + 3 * CONSTS],
        rest[:TARGETS].T,
        jnp.stack([rest[TARGETS + 2 * j : TARGETS + 2 * j + 2].T for j in range(CONSTS)]),
        rest[TARGETS + 2 * CONSTS : TARGETS + 3 * CONSTS],
        *(g.astype(f32)[None] for g in wide_sum),
    )


def solution(mesh):
    shape = mesh.devices.shape
    split = Mesh(
        mesh.devices.reshape(shape[0], shape[1], shape[2] // 2, 2), ("dp", "context", "z", "core")
    )
    slot = P(None, "dp", ("context", "z", "core"), None, None)
    expert = P(("z", "core"), None, None)
    return jax.shard_map(
        on_device,
        mesh=split,
        in_specs=(
            slot, slot, slot, slot, P(None, "dp", ("context", "z", "core")),
            *(P(),) * 9,
            *(expert,) * 3,
            slot,
        ),
        out_specs=(slot, slot, slot, *(P(),) * 9, *(expert,) * 3),
        check_vma=False,
    )
```

```python
import functools
import math

import jax
import jax.numpy as jnp
from jax import lax
from jax.experimental import pallas as pl
from jax.experimental.pallas import tpu as pltpu
from jax.sharding import Mesh, PartitionSpec as P

HEADS = 12
HEAD_SIZE = 64
EXPERTS = 8
CONSTS = 2
TARGETS = 12
CLEN = 128
QUAD = 4
LANES = 128

norm_eps = 1e-05
very_low = -1e30
highest = lax.Precision.HIGHEST
f32 = jnp.float32
bf16 = jnp.bfloat16
CHIPS = ("z", "context")
PLANE = ("dp", "context")
ALL_CHIPS = ("z",) + PLANE
EXPERT = ("z", "core")


def dot_nn(left, right, **kw):
    return jnp.dot(left, right, preferred_element_type=f32, **kw)


def dot_nt(left, right, **kw):
    return lax.dot_general(left, right, (((1,), (1,)), ((), ())), preferred_element_type=f32, **kw)


def dot_tn(left, right, **kw):
    return lax.dot_general(left, right, (((0,), (0,)), ((), ())), preferred_element_type=f32, **kw)


def iota(shape, dim):
    return lax.broadcasted_iota(jnp.int32, shape, dim)


def params():
    return pltpu.CompilerParams(vmem_limit_bytes=63_400_000)


def head_masks(dtype):
    lane_head = iota((1, QUAD * HEAD_SIZE), 1) // HEAD_SIZE
    return [(lane_head == h).astype(f32).astype(dtype) for h in range(QUAD)]


def spread(rows, prompt, dtype):
    masks = head_masks(dtype)
    return jnp.concatenate(
        [rows[:prompt] * m for m in masks] + [rows[prompt:] * m for m in masks], axis=0
    )


def gather_heads(stacked, prompt, dtype):
    masks = head_masks(dtype)
    top, low = 0.0, 0.0
    first = QUAD * prompt
    for h in range(QUAD):
        top = top + stacked[h * prompt : (h + 1) * prompt] * masks[h]
        low = low + stacked[first + h * CLEN : first + (h + 1) * CLEN] * masks[h]
    return jnp.concatenate([top, low], axis=0)


def key_places(core, keys, prompt, chips, j):
    half = keys // 2
    other = jnp.where(j >= half, 1, 0)
    chip = (j - other * half) // prompt
    chip = (chip % chips[0]) * chips[1] + chip // chips[0]
    slot = chip * 2 + jnp.where(other > 0, 1 - core, core)
    return slot * prompt + (j & (prompt - 1))


def attn_fwd_kernel(
    base_ref, normed_ref, near_ref, far_ref, wq_ref, wk_ref, wv_ref, o_ref, lse_ref, q_ref, kv_ref,
    *, chips,
):
    prompt = q_ref.shape[0] - CLEN
    keys = kv_ref.shape[0] - CLEN
    half = keys // 2
    wide = QUAD * HEAD_SIZE
    masks = head_masks(bf16)
    masks_f = head_masks(f32)
    ones = jnp.ones((8, LANES), f32)

    def to_row(column):
        spare = jnp.where(iota((column.shape[0], LANES), 1) == 0, column, 0.0)
        return dot_nt(ones, spare, precision=highest)

    q = dot_nn(normed_ref[...], wq_ref[...]).astype(bf16).astype(f32)
    q_ref[...] = (q * (1.0 / math.sqrt(HEAD_SIZE))).astype(bf16)
    for w_ref, cols in ((wk_ref, slice(0, wide)), (wv_ref, slice(wide, 2 * wide))):
        for rows, at in ((near_ref, 0), (far_ref, half)):
            kv_ref[at : at + half, cols] = dot_nn(rows[...], w_ref[...]).astype(bf16)
        kv_ref[keys:, cols] = dot_nn(normed_ref[prompt:], w_ref[...]).astype(bf16)
    q_top, q_low = q_ref[:prompt], q_ref[prompt:]
    q_p = jnp.concatenate([q_top * m for m in masks], axis=0)
    s = dot_nt(q_p, kv_ref[:keys, :wide])
    limit = base_ref[0] + (iota((QUAD * prompt, 1), 0) & (prompt - 1))
    s = jnp.where(key_places(base_ref[1], keys, prompt, chips, iota((1, keys), 1)) <= limit, s, very_low)
    top = jnp.max(s, axis=1, keepdims=True)
    p = jnp.exp(s - top)
    total = jnp.sum(p, axis=1, keepdims=True)
    out = dot_nn(p.astype(bf16), kv_ref[:keys, wide:]) * (1.0 / total)
    lse_ref[:, : QUAD * prompt] = to_row(top + jnp.log(total))
    o_ref[:prompt] = sum(out[h * prompt : (h + 1) * prompt] * masks_f[h] for h in range(QUAD))
    low_out = 0.0
    per = 2
    for part in range(QUAD // per):
        hs = range(part * per, (part + 1) * per)
        rows = per * CLEN
        q_c = jnp.concatenate([q_low * masks[h] for h in hs], axis=0)
        s = dot_nt(q_c, kv_ref[:keys, :wide])
        own = dot_nt(q_c, kv_ref[keys:, :wide])
        own = jnp.where(
            iota((1, CLEN), 1) <= (iota((rows, 1), 0) & (CLEN - 1)), own, very_low
        )
        top = jnp.maximum(
            jnp.max(s, axis=1, keepdims=True), jnp.max(own, axis=1, keepdims=True)
        )
        p = jnp.exp(s - top)
        p_own = jnp.exp(own - top)
        total = jnp.sum(p, axis=1, keepdims=True) + jnp.sum(p_own, axis=1, keepdims=True)
        out = dot_nn(p.astype(bf16), kv_ref[:keys, wide:])
        out = out + dot_nn(p_own.astype(bf16), kv_ref[keys:, wide:])
        out = out * (1.0 / total)
        at = QUAD * prompt + part * rows
        lse_ref[:, at : at + rows] = to_row(top + jnp.log(total))
        for i, h in enumerate(hs):
            low_out = low_out + out[i * CLEN : (i + 1) * CLEN] * masks_f[h]
    o_ref[prompt:] = low_out


def attn_fwd(base, normed, near, far, w_query, w_key, w_value, chips, micro):
    rows, width = normed.shape[1:]
    half = near.shape[0]
    every = 2 * half + CLEN
    quads = HEADS // QUAD
    wide = QUAD * HEAD_SIZE
    col = lambda n, w=wide: pl.BlockSpec((n, w), lambda g, b: (0, g))
    whole = lambda n: pl.BlockSpec((n, width), lambda g, b: (0, 0))
    return pl.pallas_call(
        functools.partial(attn_fwd_kernel, chips=chips),
        grid_spec=pltpu.PrefetchScalarGridSpec(
            num_scalar_prefetch=1,
            grid=(quads,),
            in_specs=[
                pl.BlockSpec((None, rows, width), lambda g, b: (micro, 0, 0)),
                whole(half), whole(half), col(width), col(width), col(width),
            ],
            out_specs=[
                col(rows),
                pl.BlockSpec((None, 8, QUAD * rows), lambda g, b: (g, 0, 0)),
                col(rows),
                col(every, 2 * wide),
            ],
        ),
        out_shape=[
            jax.ShapeDtypeStruct((rows, width), f32),
            jax.ShapeDtypeStruct((quads, 8, QUAD * rows), f32),
            jax.ShapeDtypeStruct((rows, width), bf16),
            jax.ShapeDtypeStruct((every, 2 * width), bf16),
        ],
        compiler_params=params(),
        cost_estimate=pl.CostEstimate(
            flops=16 * rows * every * width + 4 * every * width * width,
            bytes_accessed=4 * every * width,
            transcendentals=rows * every * HEADS,
        ),
        name="attn_fwd",
    )(base, normed, near, far, w_query, w_key, w_value)


def attn_bwd_kernel(
    base_ref, q_ref, kv_ref, do_ref, o_ref, lse_ref, wq_ref, wk_ref, wv_ref, near_ref, far_ref, normed_ref,
    dq_ref, dkv_ref, give_ref, keep_ref, mine_ref, gain_ref, qm, dom, dqt, dq_all, dkv_all,
    *, block, quads, chips,
):
    g = pl.program_id(0)
    prompt = q_ref.shape[0] - CLEN
    keys = kv_ref.shape[0] - CLEN
    wide = QUAD * HEAD_SIZE

    @pl.when(g < quads)
    def _():
        qm[...] = spread(q_ref[...], prompt, bf16)
        dom[...] = spread(do_ref[...], prompt, bf16)
        prod = spread(do_ref[...].astype(f32) * o_ref[...], prompt, f32)
        delta = dot_nt(jnp.ones((8, prod.shape[1]), f32), prod, precision=highest)[0:1]
        lse = lse_ref[0:1, :]
        first = QUAD * prompt
        ahead = (iota((prompt, first), 1) & (prompt - 1)) - iota((prompt, first), 0)
        q_all, do_all = qm[...], dom[...]

        def one(rows, mask):
            kk, vv = kv_ref[rows, :wide], kv_ref[rows, wide:]
            p = jnp.exp(dot_nt(kk, q_all) - lse)
            p = mask(p)
            ds = p * (dot_nt(vv, do_all) - delta)
            pb, dsb = p.astype(bf16), ds.astype(bf16)
            dk = dot_nn(dsb, q_all).astype(bf16)
            dv = dot_nn(pb, do_all).astype(bf16)
            dkv_ref[rows, :wide] = dk
            dkv_ref[rows, wide:] = dv
            dkv_all[g, rows, :wide] = dk
            dkv_all[g, rows, wide:] = dv
            return dot_tn(kk, dsb)

        def own_mask(p):
            lane = iota((1, p.shape[1]), 1)
            own_row = jnp.where(lane < first, -1, (lane - first) & (CLEN - 1))
            return jnp.where(iota((CLEN, 1), 0) <= own_row, p, 0.0)

        dqt[...] = one(pl.ds(keys, CLEN), own_mask)

        def step(i, unused):
            at = pl.multiple_of(i * block, block)

            def mask(p):
                rows = []
                for r in range(0, block, prompt):
                    gap = key_places(base_ref[1], keys, prompt, chips, at + r) - base_ref[0]
                    rows.append(jnp.where(ahead >= gap, p[r : r + prompt, :first], 0.0))
                return jnp.concatenate([jnp.concatenate(rows, axis=0), p[:, first:]], axis=1)

            dqt[...] += one(pl.ds(at, block), mask)
            return unused

        lax.fori_loop(0, keys // block, step, 0)
        dq = gather_heads(dqt[...].T, prompt, f32)
        dq = (dq * (1.0 / math.sqrt(HEAD_SIZE))).astype(bf16)
        dq_ref[...] = dq
        dq_all[g] = dq

    @pl.when(g == quads)
    def _():
        half = keys // 2

        def every(lo, hi, at):
            parts = [dkv_all[i, lo:hi, at : at + wide] for i in range(quads)]
            return jnp.concatenate(parts, axis=1)

        def back(lo, hi):
            return dot_nt(every(lo, hi, 0), wk_ref[...]) + dot_nt(every(lo, hi, wide), wv_ref[...])

        part = back(half, keys)
        give_ref[...] = part.astype(bf16)
        gain = jnp.sum(part * far_ref[...].astype(f32), axis=0, keepdims=True)
        part = back(0, half)
        keep_ref[...] = part.astype(bf16)
        gain = gain + jnp.sum(part * near_ref[...].astype(f32), axis=0, keepdims=True)
        dq = jnp.concatenate([dq_all[i] for i in range(quads)], axis=1)
        mine = dot_nt(dq, wq_ref[...])
        low = mine[prompt:] + back(keys, keys + CLEN)
        mine_ref[:prompt] = mine[:prompt]
        mine_ref[prompt:] = low
        normed = normed_ref[...].astype(f32)
        gain = gain + jnp.sum(mine[:prompt] * normed[:prompt], axis=0, keepdims=True)
        gain = gain + jnp.sum(low * normed[prompt:], axis=0, keepdims=True)
        gain_ref[...] = jnp.broadcast_to(gain, gain_ref.shape)


def attn_bwd(base, q, kv, do, o, lse, w_query, w_key, w_value, near, far, normed, chips, micro, block=1024):
    rows, width = q.shape
    every = kv.shape[0]
    half = near.shape[0]
    quads = HEADS // QUAD
    wide = QUAD * HEAD_SIZE
    at = lambda g: jnp.minimum(g, quads - 1)
    col = lambda n, w=wide: pl.BlockSpec((n, w), lambda g, b: (0, at(g)))
    whole = lambda n: pl.BlockSpec((n, width), lambda g, b: (0, 0))
    return pl.pallas_call(
        functools.partial(attn_bwd_kernel, block=min(block, half), quads=quads, chips=chips),
        grid_spec=pltpu.PrefetchScalarGridSpec(
            num_scalar_prefetch=1,
            grid=(quads + 1,),
            in_specs=[
                col(rows), col(every, 2 * wide), col(rows), col(rows),
                pl.BlockSpec((None, 8, QUAD * rows), lambda g, b: (at(g), 0, 0)),
                whole(width), whole(width), whole(width), whole(half), whole(half),
                pl.BlockSpec((None, rows, width), lambda g, b: (micro, 0, 0)),
            ],
            out_specs=[
                col(rows), col(every, 2 * wide), whole(half), whole(half), whole(rows), whole(8)
            ],
            scratch_shapes=[
                pltpu.VMEM((QUAD * rows, wide), bf16),
                pltpu.VMEM((QUAD * rows, wide), bf16),
                pltpu.VMEM((wide, QUAD * rows), f32),
                pltpu.VMEM((quads, rows, wide), bf16),
                pltpu.VMEM((quads, every, 2 * wide), bf16),
            ],
        ),
        out_shape=[
            jax.ShapeDtypeStruct((rows, width), bf16),
            jax.ShapeDtypeStruct((every, 2 * width), bf16),
            jax.ShapeDtypeStruct((half, width), bf16),
            jax.ShapeDtypeStruct((half, width), bf16),
            jax.ShapeDtypeStruct((rows, width), f32),
            jax.ShapeDtypeStruct((8, width), f32),
        ],
        compiler_params=params(),
        cost_estimate=pl.CostEstimate(
            flops=40 * rows * every * width + 4 * every * width * width,
            bytes_accessed=12 * every * width,
            transcendentals=rows * every * HEADS,
        ),
        name="attn_bwd",
    )(base, q, kv, do, o, lse, w_query, w_key, w_value, near, far, normed)


def route_kernel(
    x_ref, attn_ref, wout_ref, gain_ref, wr_ref, prior_ref, eff_ref, efft_ref, og_ref,
    resid_ref, two_ref, ch_ref, send_ref, sel_ref, selt_ref, gate_ref, *, cap,
):
    rows, width = x_ref.shape
    slots = EXPERTS * cap
    resid = x_ref[...].astype(f32) + dot_nn(attn_ref[...].astype(bf16), wout_ref[...])
    resid_ref[...] = resid
    inv = lax.rsqrt(jnp.mean(resid * resid, axis=1, keepdims=True) + norm_eps)
    two = (resid * inv * gain_ref[...]).astype(bf16)
    two_ref[...] = two
    lane = iota((1, LANES), 1)
    logits = dot_nn(two, wr_ref[...]) + prior_ref[...]
    masked = jnp.where(lane < TARGETS, logits, very_low)
    e = jnp.exp(masked - jnp.max(masked, axis=1, keepdims=True))
    ch = e * (1.0 / jnp.sum(e, axis=1, keepdims=True))
    for j in range(CONSTS):
        at = TARGETS + 2 * j
        diff = logits[:, at + 1 : at + 2] - logits[:, at : at + 1]
        ch = jnp.where(lane == at, 1.0 / (1.0 + jnp.exp(diff)), ch)
        ch = jnp.where(lane == at + 1, 1.0 / (1.0 + jnp.exp(-diff)), ch)
    ch_ref[...] = ch
    target = iota((16, rows), 0)
    hot_t = ((target == efft_ref[0:1, :]) | (target == efft_ref[1:2, :])).astype(f32)
    before = (iota((rows, rows), 0) < iota((rows, rows), 1)).astype(f32).astype(bf16)
    rank_t = dot_nn(hot_t.astype(bf16), before)
    rank_t = jnp.where(hot_t > 0.0, rank_t, -1.0)
    place = iota((cap, 1), 0).astype(f32)
    sel = jnp.concatenate(
        [(place == rank_t[i : i + 1, :]).astype(f32) for i in range(EXPERTS)], axis=0
    )
    sel_b = sel.astype(bf16)
    sel_ref[...] = sel_b
    hot = ((lane == eff_ref[:, 0:1]) | (lane == eff_ref[:, 1:2])).astype(f32)
    after = (iota((rows, rows), 0) > iota((rows, rows), 1)).astype(f32).astype(bf16)
    rank = dot_nn(after, hot.astype(bf16))
    rank = jnp.where(hot > 0.0, rank, -1.0)
    slot = iota((1, slots), 1)
    widen = (slot // cap == iota((LANES, 1), 0)).astype(f32).astype(bf16)
    rank_s = dot_nn(rank.astype(bf16), widen)
    selt_ref[...] = (rank_s == (slot % cap).astype(f32)).astype(f32).astype(bf16)
    ch_s = dot_nn(sel, ch, precision=highest)
    of_slot = iota((slots, 1), 0) // cap
    gate = jnp.sum(jnp.where(lane == of_slot, ch_s, 0.0), axis=1, keepdims=True)
    gate_ref[...] = jnp.broadcast_to(gate, gate_ref.shape)
    send_ref[:, :width] = dot_nn(sel_b, two).astype(bf16)
    send_ref[:, width:] = (gate * dot_nn(sel_b, og_ref[...])).astype(bf16)


def of_micro(array, micro):
    return pl.BlockSpec((None,) + array.shape[1:], lambda i: (micro,) + (0,) * (array.ndim - 1))


def all_of(array):
    return pl.BlockSpec(array.shape, lambda i: (0,) * array.ndim)


def route(x, attn, w_out, gain, wr, prior, eff, efft, og, cap, micro):
    rows, width = x.shape[1:]
    slots = EXPERTS * cap
    return pl.pallas_call(
        functools.partial(route_kernel, cap=cap),
        grid=(1,),
        in_specs=[
            of_micro(x, micro), all_of(attn), all_of(w_out), all_of(gain), all_of(wr),
            of_micro(prior, micro), of_micro(eff, micro), of_micro(efft, micro), of_micro(og, micro),
        ],
        out_shape=[
            jax.ShapeDtypeStruct((rows, width), f32),
            jax.ShapeDtypeStruct((rows, width), bf16),
            jax.ShapeDtypeStruct((rows, LANES), f32),
            jax.ShapeDtypeStruct((slots, 2 * width), bf16),
            jax.ShapeDtypeStruct((slots, rows), bf16),
            jax.ShapeDtypeStruct((rows, slots), bf16),
            jax.ShapeDtypeStruct((slots, LANES), f32),
        ],
        compiler_params=params(),
        cost_estimate=pl.CostEstimate(
            flops=6 * rows * width * width, bytes_accessed=4 * width * width, transcendentals=0
        ),
        name="route",
    )(x, attn, w_out, gain, wr, prior, eff, efft, og)


def expert_kernel(
    x_ref, g_ref, wg_ref, wu_ref, wd_ref, out_ref, hid_ref, gg_ref, ug_ref, fwd, back
):
    step = pl.program_id(0)
    width = x_ref.shape[1]

    @pl.when(step == 0)
    def _():
        fwd[...] = jnp.zeros_like(fwd)
        back[...] = jnp.zeros_like(back)

    x, g = x_ref[...], g_ref[...]
    gate = dot_nn(x, wg_ref[...])
    up = dot_nn(x, wu_ref[...])
    hid_grad = dot_nt(g, wd_ref[...])
    sig = 1.0 / (1.0 + jnp.exp(-gate))
    act = gate * sig
    hid = (act * up).astype(bf16)
    gg = (hid_grad * up * (sig + act * (1.0 - sig))).astype(bf16)
    ug = (hid_grad * act).astype(bf16)
    hid_ref[...] = hid
    gg_ref[...] = gg
    ug_ref[...] = ug
    fwd[...] += dot_nn(hid, wd_ref[...])
    back[...] += dot_nt(gg, wg_ref[...]) + dot_nt(ug, wu_ref[...])

    @pl.when(step == pl.num_programs(0) - 1)
    def _():
        out_ref[:, :width] = fwd[...].astype(bf16)
        out_ref[:, width:] = back[...].astype(bf16)


def experts(rows_in, w_gate, w_up, w_down, tile=256):
    rows = rows_in.shape[0]
    width = rows_in.shape[1] // 2
    hidden = w_gate.shape[2]
    half = lambda i: pl.BlockSpec((rows, width), lambda t, i=i: (0, i))
    inner = pl.BlockSpec((None, width, tile), lambda t: (0, 0, t))
    mid = pl.BlockSpec((rows, tile), lambda t: (0, t))
    return pl.pallas_call(
        expert_kernel,
        grid=(hidden // tile,),
        in_specs=[half(0), half(1), inner, inner, pl.BlockSpec((None, tile, width), lambda t: (0, t, 0))],
        out_specs=[pl.BlockSpec((rows, 2 * width), lambda t: (0, 0)), mid, mid, mid],
        out_shape=[jax.ShapeDtypeStruct((rows, 2 * width), bf16)]
        + [jax.ShapeDtypeStruct((rows, hidden), bf16)] * 3,
        scratch_shapes=[pltpu.VMEM((rows, width), f32), pltpu.VMEM((rows, width), f32)],
        compiler_params=params(),
        cost_estimate=pl.CostEstimate(
            flops=14 * rows * width * hidden,
            bytes_accessed=6 * width * hidden,
            transcendentals=rows * hidden,
        ),
        name="experts",
    )(rows_in, rows_in, w_gate, w_up, w_down)


def expert_wgrad_kernel(*refs, count):
    ins, (dg_ref, du_ref, dd_ref, xt) = refs[: 5 * count], refs[5 * count :]
    rows = ins[0].shape[0]

    @pl.when(pl.program_id(0) == 0)
    def _():
        for m in range(count):
            xt[:, m * rows : (m + 1) * rows] = ins[5 * m][...].T

    g, hid, gg, ug = (
        jnp.concatenate([ins[5 * m + i][...] for m in range(count)], axis=0) for i in range(1, 5)
    )
    dg_ref[...] = dot_nn(xt[...], gg).astype(bf16)
    du_ref[...] = dot_nn(xt[...], ug).astype(bf16)
    dd_ref[...] = dot_tn(hid, g).astype(bf16)


def expert_wgrad(parts, tile=256):
    rows = parts[0][0].shape[0]
    width = parts[0][0].shape[1] // 2
    hidden = parts[0][1].shape[1]
    half = lambda i: pl.BlockSpec((rows, width), lambda t, i=i: (0, i))
    mid = pl.BlockSpec((rows, tile), lambda t: (0, t))
    specs, args = [], []
    for rows_in, hid, gg, ug in parts:
        specs += [half(0), half(1), mid, mid, mid]
        args += [rows_in, rows_in, hid, gg, ug]
    inner = pl.BlockSpec((width, tile), lambda t: (0, t))
    return pl.pallas_call(
        functools.partial(expert_wgrad_kernel, count=len(parts)),
        grid=(hidden // tile,),
        in_specs=specs,
        out_specs=[inner, inner, pl.BlockSpec((tile, width), lambda t: (t, 0))],
        out_shape=[
            jax.ShapeDtypeStruct((width, hidden), bf16),
            jax.ShapeDtypeStruct((width, hidden), bf16),
            jax.ShapeDtypeStruct((hidden, width), bf16),
        ],
        scratch_shapes=[pltpu.VMEM((width, len(parts) * rows), bf16)],
        compiler_params=params(),
        cost_estimate=pl.CostEstimate(
            flops=6 * len(parts) * rows * width * hidden,
            bytes_accessed=6 * width * hidden,
            transcendentals=0,
        ),
        name="expert_wgrad",
    )(*args)


def combine_kernel(
    resid_ref, two_ref, ch_ref, eff_ref, og_ref, ret_ref, sel_ref, selt_ref, gate_ref,
    wout_ref, gain_ref, wr_ref, cv_ref,
    mixed_ref, rtot_ref, branch_ref, ag_ref, dl_ref, small_ref, *, cap,
):
    rows, width = resid_ref.shape
    slots = EXPERTS * cap
    lane = iota((1, LANES), 1)
    resid, two_b, ch = resid_ref[...], two_ref[...], ch_ref[...]
    two = two_b.astype(f32)
    og_b = og_ref[...]
    og = og_b.astype(f32)
    eo = ret_ref[:, :width].astype(f32)
    sel, selt = sel_ref[...], selt_ref[...]
    hot = ((lane == eff_ref[:, 0:1]) | (lane == eff_ref[:, 1:2])).astype(f32)
    dgate = jnp.sum(dot_nn(sel, og_b) * eo, axis=1, keepdims=True)
    by_target = jnp.where(lane == iota((slots, 1), 0) // cap, dgate, 0.0)
    dval = dot_nn(selt.astype(f32), by_target, precision=highest)
    self_dot = jnp.sum(og * two, axis=1, keepdims=True)
    cv_dot = dot_nt(og_b, cv_ref[...])
    gates = ch * hot
    keep = gates[:, EXPERTS + 1 : EXPERTS + 2]
    dval = jnp.where(lane == EXPERTS + 1, self_dot, dval)
    mixed = resid + dot_nn(selt, (gate_ref[:, 0:1] * eo).astype(bf16))
    dl_const = jnp.zeros((rows, LANES), f32)
    coef_cv = jnp.zeros((rows, LANES), f32)
    for j in range(CONSTS):
        e, at = EXPERTS + 2 + j, TARGETS + 2 * j
        a0, a1 = ch[:, at : at + 1], ch[:, at + 1 : at + 2]
        gate = gates[:, e : e + 1]
        with_cv = cv_dot[:, e : e + 1]
        dval = jnp.where(lane == e, a0 * self_dot + a1 * with_cv, dval)
        keep = keep + gate * a0
        mixed = mixed + (gate * a1) * cv_ref[e : e + 1, :].astype(f32)
        coef_cv = jnp.where(lane == TARGETS + 2 * CONSTS + j, gate * a1, coef_cv)
        da0, da1 = gate * self_dot, gate * with_cv
        mean = a0 * da0 + a1 * da1
        dl_const = jnp.where(lane == at, a0 * (da0 - mean), dl_const)
        dl_const = jnp.where(lane == at + 1, a1 * (da1 - mean), dl_const)
    mixed = mixed + keep * two
    mixed_ref[...] = mixed.astype(bf16)
    ch = jnp.where(lane < TARGETS, ch, 0.0)
    dch = hot * dval
    dl = ch * (dch - jnp.sum(ch * dch, axis=1, keepdims=True)) + dl_const
    dl_ref[...] = dl
    dl_hi = dl.astype(bf16)
    dl_lo = (dl - dl_hi.astype(f32)).astype(bf16)
    cc_hi = coef_cv.astype(bf16)
    cc_lo = (coef_cv - cc_hi.astype(f32)).astype(bf16)
    small = dot_tn(dl_hi, two_b) + dot_tn(dl_lo, two_b) + dot_tn(cc_hi, og_b) + dot_tn(cc_lo, og_b)
    two_grad = (
        keep * og
        + dot_nt(dl_hi, wr_ref[...])
        + dot_nt(dl_lo, wr_ref[...])
        + dot_nn(selt, ret_ref[:, width:])
    )
    inv = lax.rsqrt(jnp.mean(resid * resid, axis=1, keepdims=True) + norm_eps)
    xhat = resid * inv
    gain_grad = jnp.sum(two_grad * xhat, axis=0, keepdims=True)
    small_ref[...] = jnp.where(
        iota((small_ref.shape[0], 1), 0) == TARGETS + 3 * CONSTS, gain_grad, small[: small_ref.shape[0]]
    )
    scaled = two_grad * gain_ref[...]
    rtot = og + inv * (scaled - xhat * jnp.mean(scaled * xhat, axis=1, keepdims=True))
    rtot_ref[...] = rtot
    branch = rtot.astype(bf16)
    branch_ref[...] = branch
    ag_ref[...] = dot_nt(branch, wout_ref[...]).astype(bf16)


def combine(resid, two, ch, eff, og, ret, sel, selt, gate, w_out, gain, wr, cv, cap, micro):
    rows, width = resid.shape
    return pl.pallas_call(
        functools.partial(combine_kernel, cap=cap),
        grid=(1,),
        in_specs=[
            all_of(resid), all_of(two), all_of(ch), of_micro(eff, micro), of_micro(og, micro),
            all_of(ret), all_of(sel), all_of(selt), all_of(gate), all_of(w_out), all_of(gain),
            all_of(wr), all_of(cv),
        ],
        out_shape=[
            jax.ShapeDtypeStruct((rows, width), bf16),
            jax.ShapeDtypeStruct((rows, width), f32),
            jax.ShapeDtypeStruct((rows, width), bf16),
            jax.ShapeDtypeStruct((rows, width), bf16),
            jax.ShapeDtypeStruct((rows, LANES), f32),
            jax.ShapeDtypeStruct((24, width), f32),
        ],
        compiler_params=params(),
        cost_estimate=pl.CostEstimate(
            flops=6 * rows * width * width, bytes_accessed=4 * width * width, transcendentals=0
        ),
        name="combine",
    )(resid, two, ch, eff, og, ret, sel, selt, gate, w_out, gain, wr, cv)


UNIT = 48
PACK = 160
PART = 512


def place(out_ref, step, grad):
    low = grad.astype(bf16)
    per = low.shape[0] // UNIT
    for j in range(low.shape[1] // LANES):
        for k in range(per):
            out_ref[j * per + k, step * UNIT : (step + 1) * UNIT, :] = low[
                k * UNIT : (k + 1) * UNIT, j * LANES : (j + 1) * LANES
            ]


def clear_tail(out_ref):
    out_ref[:, 3 * UNIT :, :] = jnp.zeros((out_ref.shape[0], PACK - 3 * UNIT, LANES), bf16)


def wgrad_kv_kernel(*refs, count):
    ins, (gain_ref, out_ref) = refs[: 6 * count], refs[6 * count :]
    t = pl.program_id(0)
    grad = 0.0
    for m in range(count):
        near, far, normed, dkv, _, _ = ins[6 * m : 6 * m + 6]
        half, rows = near.shape[0], normed.shape[0]
        grad = grad + dot_tn(near[...], dkv[:half]) + dot_tn(far[...], dkv[half : 2 * half])
        grad = grad + dot_tn(normed[rows - CLEN :], dkv[2 * half :])
    for i in range(3):

        @pl.when(t == i)
        def _():
            place(out_ref, i, grad)

    @pl.when(t == 0)
    def _():
        clear_tail(out_ref)
        small = sum(ins[6 * m + 4][...] for m in range(count))
        gain = sum(ins[6 * m + 5][0:1, :] for m in range(count)) / gain_ref[...]
        small = jnp.where(
            iota((small.shape[0], 1), 0) == TARGETS + 3 * CONSTS + 1, gain, small
        ).astype(bf16)
        for i in range(small.shape[1] // LANES):
            block = small[:, i * LANES : (i + 1) * LANES]
            out_ref[2 * i, 3 * UNIT : 3 * UNIT + 16, :] = block[:16]
            out_ref[2 * i + 1, 3 * UNIT : 3 * UNIT + 8, :] = block[16:24]


def wgrad_kv(gain, parts):
    rows, width = parts[0][2].shape[1:]
    half = parts[0][0].shape[0]
    whole = lambda n: pl.BlockSpec((n, width), lambda t: (0, 0))
    specs, args = [], []
    for m, p in enumerate(parts):
        specs += [
            whole(half), whole(half),
            pl.BlockSpec((None, rows, width), lambda t, m=m: (m, 0, 0)),
            pl.BlockSpec((2 * half + CLEN, PART), lambda t: (0, t)), whole(24), whole(8),
        ]
        args += list(p)
    count = len(parts)
    chunks = width // UNIT * PART // LANES
    return pl.pallas_call(
        functools.partial(wgrad_kv_kernel, count=count),
        grid=(2 * width // PART,),
        in_specs=specs + [whole(1)],
        out_specs=pl.BlockSpec((chunks, PACK, LANES), lambda t: (0, 0, 0)),
        out_shape=jax.ShapeDtypeStruct((chunks, PACK, LANES), bf16),
        compiler_params=params(),
        cost_estimate=pl.CostEstimate(
            flops=4 * count * (2 * half + CLEN) * width * width,
            bytes_accessed=12 * count * half * width,
            transcendentals=0,
        ),
        name="wgrad_kv",
    )(*args, gain)


def wgrad_qo_kernel(*refs, count):
    ins, out_ref = refs[: 4 * count], refs[4 * count]
    stack = lambda i: jnp.concatenate([ins[4 * m + i][...] for m in range(count)], axis=0)
    normed, dq, attn, branch = (stack(i) for i in range(4))
    width = dq.shape[1]
    query = dot_tn(normed, dq)
    out = dot_tn(attn.astype(bf16), branch)
    clear_tail(out_ref)
    both = jnp.concatenate([query, out], axis=1)
    for i in range(2 * width // PART):
        place(out_ref, i, both[:, i * PART : (i + 1) * PART])


def wgrad_qo(parts):
    rows, width = parts[0][1].shape
    chunks = width // UNIT * PART // LANES
    count = len(parts)
    specs = [s for m, p in enumerate(parts) for s in [of_micro(p[0], m)] + [all_of(a) for a in p[1:]]]
    return pl.pallas_call(
        functools.partial(wgrad_qo_kernel, count=count),
        grid=(1,),
        in_specs=specs,
        out_shape=jax.ShapeDtypeStruct((chunks, PACK, LANES), bf16),
        compiler_params=params(),
        cost_estimate=pl.CostEstimate(
            flops=4 * count * rows * width * width,
            bytes_accessed=6 * width * width,
            transcendentals=0,
        ),
        name="wgrad_qo",
    )(*[a for p in parts for a in p])


def unpack_kernel(core_ref, mine_ref, other_ref, *outs):
    query, key, value, out, gains, router, const, const_vec = outs
    first = core_ref[0] == 0
    width = query.shape[0]
    per = width // UNIT
    sub = QUAD * HEAD_SIZE // LANES
    cols = width // LANES

    def take(low, chunk, lo, hi):
        a, b = mine_ref[chunk, lo:hi, :], other_ref[chunk, lo:hi, :]
        pick = first if low else jnp.logical_not(first)
        return jnp.where(pick, a.astype(f32), b.astype(f32))

    for low in (True, False):
        for step in range(2 * width // PART):
            for j in range(PART // LANES):
                block = step * (PART // LANES) + j
                if low:
                    g, r = divmod(block, 2 * sub)
                    ref, at = (key, value)[r // sub], g * sub + r % sub
                else:
                    ref, at = (query, out)[block // cols], block % cols
                for k in range(per):
                    ref[k * UNIT : (k + 1) * UNIT, at * LANES : (at + 1) * LANES] = take(
                        low, j * per + k, step * UNIT, (step + 1) * UNIT
                    )
    for i in range(cols):
        at = slice(i * LANES, (i + 1) * LANES)
        small = take(True, 2 * i, 3 * UNIT, 3 * UNIT + 16)
        rest = take(True, 2 * i + 1, 3 * UNIT, 3 * UNIT + 16)
        router[:, at] = small[:TARGETS]
        for c in range(CONSTS):
            const[c, :, at] = small[TARGETS + 2 * c : TARGETS + 2 * c + 2]
        const_vec[:, at] = rest[:CONSTS]
        gains[:, at] = rest[CONSTS : CONSTS + 2]


def unpack(core, mine, other, width):
    vmem = pl.BlockSpec(memory_space=pltpu.VMEM)
    shapes = [(width, width)] * 4 + [
        (2, width), (TARGETS, width), (CONSTS, 2, width), (CONSTS, width)
    ]
    return pl.pallas_call(
        unpack_kernel,
        in_specs=[pl.BlockSpec(memory_space=pltpu.SMEM), vmem, vmem],
        out_specs=[vmem] * len(shapes),
        out_shape=[jax.ShapeDtypeStruct(s, f32) for s in shapes],
        compiler_params=params(),
        cost_estimate=pl.CostEstimate(
            flops=4 * width * width, bytes_accessed=24 * width * width, transcendentals=0
        ),
        name="unpack",
    )(core, mine, other)


def swap_cores(rows):
    return lax.ppermute(rows, "core", [(0, 1), (1, 0)])


def exchange(blocks, axes):
    return lax.all_to_all(blocks, axes, split_axis=0, concat_axis=0, tiled=True)


def spread_out(piece, axes):
    count = lax.axis_size(axes)
    return exchange(jnp.broadcast_to(piece[None], (count,) + piece.shape), axes)


def sum_ring(parts, axis):
    count = lax.axis_size(axis)
    me = lax.axis_index(axis)
    part = lambda i: lax.dynamic_index_in_dim(parts, i, 1, keepdims=False)
    total = part(me).astype(f32)
    for step in range(1, count):
        ring = [(i, (i + step) % count) for i in range(count)]
        total = total + lax.ppermute(part((me + step) % count), axis, ring).astype(f32)
    return total


def after(value, *others):
    return lax.optimization_barrier((value, *others))[0]


def on_device(
    tokens, prior_logits, routes, drops, cont_lengths, norm_gain, w_query, w_key, w_value, w_out,
    ffn_gain, w_router, w_const, const_vec, w_gate, w_up, w_down, out_grad,
):
    micros, rows, width = tokens.shape[0], tokens.shape[3], tokens.shape[4]
    prompt = rows - CLEN
    cap = -(-(rows * 3 // 16) // 8) * 8
    chips = (lax.axis_size("context"), lax.axis_size("z"))
    half = chips[0] * chips[1] * prompt
    core = lax.axis_index("core").astype(jnp.int32)
    base = jnp.stack([lax.axis_index(("context", "z", "core")).astype(jnp.int32) * prompt, core])
    score_scale = 1.0 / math.sqrt(HEAD_SIZE)
    gain_one = norm_gain.astype(f32)
    gain_two = ffn_gain.astype(f32).reshape(1, width)

    gain_row = gain_one.reshape(1, width)
    core_arg = core.reshape(1)
    x = tokens[:, 0, 0]
    x_f = x.astype(f32)
    inv_one = lax.rsqrt(jnp.mean(x_f * x_f, axis=-1, keepdims=True) + norm_eps)
    normed = (x_f * inv_one * gain_one).astype(bf16)
    gathered = [spread_out(normed[0, :prompt], CHIPS)]
    for m in range(1, micros):
        gathered.append(spread_out(normed[m, :prompt], CHIPS))

    wr = jnp.concatenate(
        [w_router] + [w_const[j] for j in range(CONSTS)]
        + [jnp.zeros((width, LANES - TARGETS - 2 * CONSTS), bf16)], axis=1,
    )
    cv = jnp.zeros((LANES, width), bf16).at[EXPERTS + 2 : EXPERTS + 2 + CONSTS].set(const_vec)
    row_ids = jnp.arange(rows, dtype=jnp.int32)
    og = out_grad[:, 0, 0]
    live = row_ids[None] < prompt + cont_lengths[:, 0]
    active = (1 - drops[:, 0, 0]) * live[..., None].astype(jnp.int32)
    eff = jnp.where(active > 0, routes[:, 0, 0], -1)
    efft = jnp.swapaxes(eff, 1, 2)
    prior = jnp.pad(prior_logits[:, 0, 0], ((0, 0), (0, 0), (0, LANES - TARGETS)))

    st = []
    for m in range(micros):
        s = {}
        if m:
            gathered[m] = after(gathered[m], st[m - 1]["attn"])
        else:
            gathered[m] = after(gathered[m], wr, cv, eff, efft, prior, base, core_arg, gain_row, gain_two)
        s["near"] = gathered[m].reshape(half, width)
        s["far"] = swap_cores(s["near"])
        s["attn"], s["lse"], s["q"], s["kv"] = attn_fwd(
            base, normed, s["near"], s["far"], w_query, w_key, w_value, chips, m
        )
        s["resid"], s["two"], s["ch"], send, s["sel"], s["selt"], s["gate"] = route(
            x, s["attn"], w_out, gain_two, wr, prior, eff, efft, og, cap, m
        )
        s["recv"] = exchange(send.reshape(EXPERTS, cap, 2 * width), EXPERT).reshape(
            EXPERTS * cap, 2 * width
        )
        st.append(s)
    for s in st:
        ret, s["hid"], s["gg"], s["ug"] = experts(s["recv"], w_gate, w_up, w_down)
        s["ret"] = exchange(ret.reshape(EXPERTS, cap, 2 * width), EXPERT).reshape(
            EXPERTS * cap, 2 * width
        )
    wide_grads = expert_wgrad([(s["recv"], s["hid"], s["gg"], s["ug"]) for s in st])
    st[0]["ret"] = after(st[0]["ret"], wide_grads)
    wide_sum = lax.psum(tuple(wide_grads), ("dp", "context"))

    mixed, prior_grads, kv_parts, qo_parts = [], [], [], []
    last = micros - 1
    for m, s in enumerate(st):
        out, s["rtot"], branch, ag, dl, small = combine(
            s["resid"], s["two"], s["ch"], eff, og, s["ret"], s["sel"], s["selt"], s["gate"],
            w_out, gain_two, wr, cv, cap, m,
        )
        mixed.append(out)
        prior_grads.append(dl[:, :TARGETS])
        if m < last:
            ag = after(ag, st[m + 1]["ret"])
        dq, dkv, give, keep, s["mine"], gain = attn_bwd(
            base, s["q"], s["kv"], ag, s["attn"], s["lse"], w_query, w_key, w_value,
            s["near"], s["far"], normed, chips, m,
        )
        kv_parts.append((s["near"], s["far"], normed, dkv, small, gain))
        qo_parts.append((normed, dq, s["attn"], branch))
        if m:
            give = after(give, st[m - 1]["scatter"])
        come = swap_cores(give)
        if m == last:
            qo = wgrad_qo(qo_parts)
            come = after(come, qo)
        keep = (keep.astype(f32) + come.astype(f32)).astype(bf16)
        s["scatter"] = exchange(keep.reshape(chips[1], chips[0] * prompt, width), "z")
    kv = wgrad_kv(gain_row, kv_parts)
    st[last]["scatter"] = after(st[last]["scatter"], kv)
    give = after(jnp.where(core == 0, qo, kv), st[last]["scatter"])
    keep = jnp.where(core == 0, kv, qo)
    keep = (keep.astype(f32) + swap_cores(give).astype(f32)).astype(bf16)
    keep = keep.reshape((chips[1], -1) + keep.shape[1:])
    keep = jnp.sum(exchange(keep, "z").astype(f32), axis=0).astype(bf16)
    rings = [jnp.sum(s["scatter"].astype(f32), axis=0).astype(bf16) for s in st]
    totals = sum_ring(jnp.stack(rings).reshape(micros, chips[0], prompt, width), "context")
    keep = after(keep, totals)
    own = jnp.sum(exchange(keep, PLANE).astype(f32), axis=0).astype(bf16)
    own = after(own, wide_sum)
    own = spread_out(own, ALL_CHIPS)
    token_grads = []
    for m, s in enumerate(st):
        total = totals[m]
        grad = (s["mine"] + jnp.pad(total, ((0, CLEN), (0, 0)))) * gain_one
        xhat = x_f[m] * inv_one[m]
        grad = inv_one[m] * (grad - xhat * jnp.mean(grad * xhat, axis=-1, keepdims=True))
        token_grads.append((s["rtot"] + grad).astype(bf16))
    lift = lambda parts: jnp.stack(parts)[:, None, None]
    wide_out = [g.astype(f32)[None] for g in wide_sum]
    rows_out = [lift(mixed), lift(token_grads), lift(prior_grads)]
    own = after(own, wide_out, rows_out)
    query, key, value, out, gains, router, const, vec = unpack(
        core_arg, own, swap_cores(own), width
    )
    return (
        *rows_out,
        gains[1],
        query,
        key,
        value,
        out,
        gains[0],
        router.T,
        jnp.swapaxes(const, 1, 2),
        vec,
        *wide_out,
    )


def solution(mesh):
    shape = mesh.devices.shape
    split = Mesh(
        mesh.devices.reshape(shape[0], shape[1], shape[2] // 2, 2), ("dp", "context", "z", "core")
    )
    slot = P(None, "dp", ("context", "z", "core"), None, None)
    expert = P(("z", "core"), None, None)
    return jax.shard_map(
        on_device,
        mesh=split,
        in_specs=(
            slot, slot, slot, slot, P(None, "dp", ("context", "z", "core")),
            *(P(),) * 9,
            *(expert,) * 3,
            slot,
        ),
        out_specs=(slot, slot, slot, *(P(),) * 9, *(expert,) * 3),
        check_vma=False,
    )
```

```python
import functools
import math

import jax
import jax.numpy as jnp
from jax import lax
from jax.experimental import pallas as pl
from jax.experimental.pallas import tpu as pltpu
from jax.sharding import Mesh, PartitionSpec as P

HEADS = 12
HEAD_SIZE = 64
EXPERTS = 8
CONSTS = 2
TARGETS = 12
CLEN = 128
QUAD = 4
LANES = 128

norm_eps = 1e-05
very_low = -1e30
highest = lax.Precision.HIGHEST
f32 = jnp.float32
bf16 = jnp.bfloat16
CHIPS = ("z", "context")
FIRST, REST = "z", ("dp", "context")
ALL_CHIPS = (FIRST,) + REST
EXPERT = ("z", "core")


def dot_nn(left, right, **kw):
    return jnp.dot(left, right, preferred_element_type=f32, **kw)


def dot_nt(left, right, **kw):
    return lax.dot_general(left, right, (((1,), (1,)), ((), ())), preferred_element_type=f32, **kw)


def dot_tn(left, right, **kw):
    return lax.dot_general(left, right, (((0,), (0,)), ((), ())), preferred_element_type=f32, **kw)


def iota(shape, dim):
    return lax.broadcasted_iota(jnp.int32, shape, dim)


def params():
    return pltpu.CompilerParams(vmem_limit_bytes=63_400_000)


def head_masks(dtype):
    lane_head = iota((1, QUAD * HEAD_SIZE), 1) // HEAD_SIZE
    return [(lane_head == h).astype(f32).astype(dtype) for h in range(QUAD)]


def spread(rows, prompt, dtype):
    masks = head_masks(dtype)
    return jnp.concatenate(
        [rows[:prompt] * m for m in masks] + [rows[prompt:] * m for m in masks], axis=0
    )


def gather_heads(stacked, prompt, dtype):
    masks = head_masks(dtype)
    top, low = 0.0, 0.0
    first = QUAD * prompt
    for h in range(QUAD):
        top = top + stacked[h * prompt : (h + 1) * prompt] * masks[h]
        low = low + stacked[first + h * CLEN : first + (h + 1) * CLEN] * masks[h]
    return jnp.concatenate([top, low], axis=0)


def key_places(core, keys, prompt, chips, j):
    half = keys // 2
    other = jnp.where(j >= half, 1, 0)
    chip = (j - other * half) // prompt
    chip = (chip % chips[0]) * chips[1] + chip // chips[0]
    slot = chip * 2 + jnp.where(other > 0, 1 - core, core)
    return slot * prompt + (j & (prompt - 1))


def attn_fwd_kernel(
    base_ref, normed_ref, near_ref, far_ref, wq_ref, wk_ref, wv_ref,
    x_ref, wout_ref, gain_ref, wr_ref, prior_ref, eff_ref, efft_ref, og_ref,
    o_ref, lse_ref, q_ref, kv_ref,
    resid_ref, two_ref, ch_ref, send_ref, sel_ref, selt_ref, gate_ref, o_all,
    *, chips, cap,
):
    g = pl.program_id(0)
    prompt = q_ref.shape[0] - CLEN
    keys = kv_ref.shape[0] - CLEN
    half = keys // 2
    wide = QUAD * HEAD_SIZE
    masks = head_masks(bf16)
    masks_f = head_masks(f32)
    ones = jnp.ones((8, LANES), f32)

    def to_row(column):
        spare = jnp.where(iota((column.shape[0], LANES), 1) == 0, column, 0.0)
        return dot_nt(ones, spare, precision=highest)

    q = dot_nn(normed_ref[...], wq_ref[...]).astype(bf16).astype(f32)
    q_ref[...] = (q * (1.0 / math.sqrt(HEAD_SIZE))).astype(bf16)
    for w_ref, cols in ((wk_ref, slice(0, wide)), (wv_ref, slice(wide, 2 * wide))):
        for rows, at in ((near_ref, 0), (far_ref, half)):
            kv_ref[at : at + half, cols] = dot_nn(rows[...], w_ref[...]).astype(bf16)
        kv_ref[keys:, cols] = dot_nn(normed_ref[prompt:], w_ref[...]).astype(bf16)
    q_top, q_low = q_ref[:prompt], q_ref[prompt:]
    q_p = jnp.concatenate([q_top * m for m in masks], axis=0)
    s = dot_nt(q_p, kv_ref[:keys, :wide])
    limit = base_ref[0] + (iota((QUAD * prompt, 1), 0) & (prompt - 1))
    s = jnp.where(key_places(base_ref[1], keys, prompt, chips, iota((1, keys), 1)) <= limit, s, very_low)
    top = jnp.max(s, axis=1, keepdims=True)
    p = jnp.exp(s - top)
    total = jnp.sum(p, axis=1, keepdims=True)
    out = dot_nn(p.astype(bf16), kv_ref[:keys, wide:]) * (1.0 / total)
    lse_ref[:, : QUAD * prompt] = to_row(top + jnp.log(total))
    top_out = sum(out[h * prompt : (h + 1) * prompt] * masks_f[h] for h in range(QUAD))
    low_out = 0.0
    per = 2
    for part in range(QUAD // per):
        hs = range(part * per, (part + 1) * per)
        rows = per * CLEN
        q_c = jnp.concatenate([q_low * masks[h] for h in hs], axis=0)
        s = dot_nt(q_c, kv_ref[:keys, :wide])
        own = dot_nt(q_c, kv_ref[keys:, :wide])
        own = jnp.where(
            iota((1, CLEN), 1) <= (iota((rows, 1), 0) & (CLEN - 1)), own, very_low
        )
        top = jnp.maximum(
            jnp.max(s, axis=1, keepdims=True), jnp.max(own, axis=1, keepdims=True)
        )
        p = jnp.exp(s - top)
        p_own = jnp.exp(own - top)
        total = jnp.sum(p, axis=1, keepdims=True) + jnp.sum(p_own, axis=1, keepdims=True)
        out = dot_nn(p.astype(bf16), kv_ref[:keys, wide:])
        out = out + dot_nn(p_own.astype(bf16), kv_ref[keys:, wide:])
        out = out * (1.0 / total)
        at = QUAD * prompt + part * rows
        lse_ref[:, at : at + rows] = to_row(top + jnp.log(total))
        for i, h in enumerate(hs):
            low_out = low_out + out[i * CLEN : (i + 1) * CLEN] * masks_f[h]
    attn = jnp.concatenate([top_out, low_out], axis=0)
    o_ref[...] = attn
    o_all[g] = attn.astype(bf16)

    @pl.when(g == o_all.shape[0] - 1)
    def _():
        attended = jnp.concatenate([o_all[i] for i in range(o_all.shape[0])], axis=1)
        route(
            attended, x_ref, wout_ref, gain_ref, wr_ref, prior_ref, eff_ref, efft_ref, og_ref,
            resid_ref, two_ref, ch_ref, send_ref, sel_ref, selt_ref, gate_ref, cap,
        )


def attn_fwd(
    base, normed, near, far, w_query, w_key, w_value, x, w_out, gain, wr, prior, eff, efft, og,
    chips, cap, micro,
):
    rows, width = normed.shape[1:]
    half = near.shape[0]
    every = 2 * half + CLEN
    quads = HEADS // QUAD
    wide = QUAD * HEAD_SIZE
    slots = EXPERTS * cap
    col = lambda n, w=wide: pl.BlockSpec((n, w), lambda g, b: (0, g))
    whole = lambda n, w=width: pl.BlockSpec((n, w), lambda g, b: (0, 0))
    of_micro = lambda a: pl.BlockSpec((None,) + a.shape[1:], lambda g, b: (micro, 0, 0))
    routed = [
        ((rows, width), f32), ((rows, width), bf16), ((rows, LANES), f32), ((slots, 2 * width), bf16),
        ((slots, rows), bf16), ((rows, slots), bf16), ((slots, LANES), f32),
    ]
    return pl.pallas_call(
        functools.partial(attn_fwd_kernel, chips=chips, cap=cap),
        grid_spec=pltpu.PrefetchScalarGridSpec(
            num_scalar_prefetch=1,
            grid=(quads,),
            in_specs=[
                of_micro(normed), whole(half), whole(half), col(width), col(width), col(width),
                of_micro(x), whole(width), whole(1), whole(width, LANES), of_micro(prior),
                of_micro(eff), of_micro(efft), of_micro(og),
            ],
            out_specs=[
                col(rows),
                pl.BlockSpec((None, 8, QUAD * rows), lambda g, b: (g, 0, 0)),
                col(rows),
                col(every, 2 * wide),
            ]
            + [whole(*s) for s, _ in routed],
            scratch_shapes=[pltpu.VMEM((quads, rows, wide), bf16)],
        ),
        out_shape=[
            jax.ShapeDtypeStruct((rows, width), f32),
            jax.ShapeDtypeStruct((quads, 8, QUAD * rows), f32),
            jax.ShapeDtypeStruct((rows, width), bf16),
            jax.ShapeDtypeStruct((every, 2 * width), bf16),
        ]
        + [jax.ShapeDtypeStruct(s, t) for s, t in routed],
        compiler_params=params(),
        cost_estimate=pl.CostEstimate(
            flops=16 * rows * every * width + 4 * every * width * width,
            bytes_accessed=4 * every * width,
            transcendentals=rows * every * HEADS,
        ),
        name="attn_fwd",
    )(base, normed, near, far, w_query, w_key, w_value, x, w_out, gain, wr, prior, eff, efft, og)


def attn_bwd_kernel(
    base_ref, q_ref, kv_ref, o_ref, lse_ref,
    resid_ref, two_ref, ch_ref, eff_ref, og_ref, ret_ref, sel_ref, selt_ref, gate_ref,
    wout_ref, gain_ref, wr_ref, cv_ref,
    dq_ref, dkv_ref, mixed_ref, rtot_ref, branch_ref, dl_ref, small_ref, qm, dom, dqt, do_all,
    *, block, chips, cap,
):
    g = pl.program_id(0)
    quads = do_all.shape[0]

    @pl.when(g == 0)
    def _():
        grad = combine(
            resid_ref, two_ref, ch_ref, eff_ref, og_ref, ret_ref, sel_ref, selt_ref, gate_ref,
            wout_ref, gain_ref, wr_ref, cv_ref,
            mixed_ref, rtot_ref, branch_ref, dl_ref, small_ref, cap,
        )
        for i in range(quads):
            do_all[i] = grad[:, i * QUAD * HEAD_SIZE : (i + 1) * QUAD * HEAD_SIZE]

    do_now = do_all[g]
    prompt = q_ref.shape[0] - CLEN
    keys = kv_ref.shape[0] - CLEN
    wide = QUAD * HEAD_SIZE
    qm[...] = spread(q_ref[...], prompt, bf16)
    dom[...] = spread(do_now, prompt, bf16)
    prod = spread(do_now.astype(f32) * o_ref[...], prompt, f32)
    delta = dot_nt(jnp.ones((8, prod.shape[1]), f32), prod, precision=highest)[0:1]
    lse = lse_ref[0:1, :]
    first = QUAD * prompt
    ahead = (iota((prompt, first), 1) & (prompt - 1)) - iota((prompt, first), 0)
    q_all, do_all = qm[...], dom[...]

    def one(rows, mask):
        kk, vv = kv_ref[rows, :wide], kv_ref[rows, wide:]
        p = jnp.exp(dot_nt(kk, q_all) - lse)
        p = mask(p)
        ds = p * (dot_nt(vv, do_all) - delta)
        pb, dsb = p.astype(bf16), ds.astype(bf16)
        dkv_ref[rows, :wide] = dot_nn(dsb, q_all).astype(bf16)
        dkv_ref[rows, wide:] = dot_nn(pb, do_all).astype(bf16)
        return dot_tn(kk, dsb)

    def own_mask(p):
        lane = iota((1, p.shape[1]), 1)
        own_row = jnp.where(lane < first, -1, (lane - first) & (CLEN - 1))
        return jnp.where(iota((CLEN, 1), 0) <= own_row, p, 0.0)

    dqt[...] = one(pl.ds(keys, CLEN), own_mask)

    def step(i, unused):
        at = i * block

        def mask(p):
            rows = []
            for r in range(0, block, prompt):
                gap = key_places(base_ref[1], keys, prompt, chips, at + r) - base_ref[0]
                rows.append(jnp.where(ahead >= gap, p[r : r + prompt, :first], 0.0))
            return jnp.concatenate([jnp.concatenate(rows, axis=0), p[:, first:]], axis=1)

        dqt[...] += one(pl.ds(at, block), mask)
        return unused

    for i in range(keys // block):
        step(i, 0)
    dq = gather_heads(dqt[...].T, prompt, f32)
    dq = (dq * (1.0 / math.sqrt(HEAD_SIZE))).astype(bf16)
    dq_ref[...] = dq


def attn_bwd(
    base, q, kv, o, lse, resid, two, ch, eff, og, ret, sel, selt, gate, w_out, gain, wr, cv,
    chips, cap, micro, block=1024,
):
    rows, width = q.shape
    every = kv.shape[0]
    quads = HEADS // QUAD
    wide = QUAD * HEAD_SIZE
    col = lambda n, w=wide: pl.BlockSpec((n, w), lambda g, b: (0, g))
    whole = lambda a: pl.BlockSpec(a.shape, lambda g, b: (0, 0))
    of_micro = lambda a: pl.BlockSpec((None,) + a.shape[1:], lambda g, b: (micro, 0, 0))
    mixing = [
        jax.ShapeDtypeStruct((rows, width), bf16),
        jax.ShapeDtypeStruct((rows, width), f32),
        jax.ShapeDtypeStruct((rows, width), bf16),
        jax.ShapeDtypeStruct((rows, LANES), f32),
        jax.ShapeDtypeStruct((24, width), f32),
    ]
    return pl.pallas_call(
        functools.partial(
            attn_bwd_kernel, block=min(block, (every - CLEN) // 2), chips=chips, cap=cap
        ),
        grid_spec=pltpu.PrefetchScalarGridSpec(
            num_scalar_prefetch=1,
            grid=(quads,),
            in_specs=[
                col(rows), col(every, 2 * wide), col(rows),
                pl.BlockSpec((None, 8, QUAD * rows), lambda g, b: (g, 0, 0)),
                whole(resid), whole(two), whole(ch), of_micro(eff), of_micro(og), whole(ret),
                whole(sel), whole(selt), whole(gate), whole(w_out), whole(gain), whole(wr), whole(cv),
            ],
            out_specs=[col(rows), col(every, 2 * wide)] + [whole(a) for a in mixing],
            scratch_shapes=[
                pltpu.VMEM((QUAD * rows, wide), bf16),
                pltpu.VMEM((QUAD * rows, wide), bf16),
                pltpu.VMEM((wide, QUAD * rows), f32),
                pltpu.VMEM((quads, rows, wide), bf16),
            ],
        ),
        out_shape=[
            jax.ShapeDtypeStruct((rows, width), bf16),
            jax.ShapeDtypeStruct((every, 2 * width), bf16),
        ]
        + mixing,
        compiler_params=params(),
        cost_estimate=pl.CostEstimate(
            flops=40 * rows * every * width,
            bytes_accessed=8 * every * width,
            transcendentals=rows * every * HEADS,
        ),
        name="attn_bwd",
    )(base, q, kv, o, lse, resid, two, ch, eff, og, ret, sel, selt, gate, w_out, gain, wr, cv)


def back_proj_kernel(*refs, count, own):
    ins, (wk_ref, wv_ref), rest = refs[: 3 * count], refs[3 * count : 3 * count + 2], refs[3 * count + 2 :]
    wide = QUAD * HEAD_SIZE
    quads = HEADS // QUAD

    def back(ref):
        pick = lambda at: jnp.concatenate(
            [ref[:, 2 * g * wide + at : 2 * g * wide + at + wide] for g in range(quads)], axis=1
        )
        return dot_nt(pick(0), wk_ref[...]) + dot_nt(pick(wide), wv_ref[...])

    for m in range(count):
        part_ref, own_ref, dq_ref = ins[3 * m : 3 * m + 3]

        @pl.when(pl.program_id(0) == m)
        def _():
            if own:
                wq_ref, out_ref, mine_ref = rest
                mine = dot_nt(dq_ref[...], wq_ref[...])
                prompt = mine.shape[0] - CLEN
                mine_ref[:prompt] = mine[:prompt]
                mine_ref[prompt:] = mine[prompt:] + back(own_ref)
            else:
                (out_ref,) = rest
            out_ref[...] = back(part_ref).astype(bf16)


def back_proj(parts, w_key, w_value, w_query, which):
    own = which == 0
    count = len(parts)
    rows, width = parts[0][1].shape
    every = parts[0][0].shape[0]
    half = (every - CLEN) // 2
    whole = lambda n: pl.BlockSpec((n, width), lambda t: (0, 0))
    by_micro = lambda n: pl.BlockSpec((None, n, width), lambda t: (t, 0, 0))
    specs, args = [], []
    for dkv, dq in parts:
        specs += [
            pl.BlockSpec((half, 2 * width), lambda t: (which, 0)),
            pl.BlockSpec((CLEN, 2 * width), lambda t: (2 * half // CLEN, 0)),
            whole(rows),
        ]
        args += [dkv, dkv, dq]
    out_specs, out_shape = [by_micro(half)], [jax.ShapeDtypeStruct((count, half, width), bf16)]
    if own:
        out_specs.append(by_micro(rows))
        out_shape.append(jax.ShapeDtypeStruct((count, rows, width), f32))
    return pl.pallas_call(
        functools.partial(back_proj_kernel, count=count, own=own),
        grid=(count,),
        in_specs=specs + [whole(width)] * (3 if own else 2),
        out_specs=out_specs,
        out_shape=out_shape,
        compiler_params=params(),
        cost_estimate=pl.CostEstimate(
            flops=4 * count * half * width * width,
            bytes_accessed=8 * count * half * width,
            transcendentals=0,
        ),
        name="back_proj",
    )(*args, w_key, w_value, *([w_query] if own else []))


def route(
    attended, x_ref, wout_ref, gain_ref, wr_ref, prior_ref, eff_ref, efft_ref, og_ref,
    resid_ref, two_ref, ch_ref, send_ref, sel_ref, selt_ref, gate_ref, cap,
):
    rows, width = x_ref.shape
    slots = EXPERTS * cap
    resid = x_ref[...].astype(f32) + dot_nn(attended, wout_ref[...])
    resid_ref[...] = resid
    inv = lax.rsqrt(jnp.mean(resid * resid, axis=1, keepdims=True) + norm_eps)
    two = (resid * inv * gain_ref[...]).astype(bf16)
    two_ref[...] = two
    lane = iota((1, LANES), 1)
    logits = dot_nn(two, wr_ref[...]) + prior_ref[...]
    masked = jnp.where(lane < TARGETS, logits, very_low)
    e = jnp.exp(masked - jnp.max(masked, axis=1, keepdims=True))
    ch = e * (1.0 / jnp.sum(e, axis=1, keepdims=True))
    for j in range(CONSTS):
        at = TARGETS + 2 * j
        diff = logits[:, at + 1 : at + 2] - logits[:, at : at + 1]
        ch = jnp.where(lane == at, 1.0 / (1.0 + jnp.exp(diff)), ch)
        ch = jnp.where(lane == at + 1, 1.0 / (1.0 + jnp.exp(-diff)), ch)
    ch_ref[...] = ch
    target = iota((16, rows), 0)
    hot_t = ((target == efft_ref[0:1, :]) | (target == efft_ref[1:2, :])).astype(f32)
    before = (iota((rows, rows), 0) < iota((rows, rows), 1)).astype(f32).astype(bf16)
    rank_t = dot_nn(hot_t.astype(bf16), before)
    rank_t = jnp.where(hot_t > 0.0, rank_t, -1.0)
    place = iota((cap, 1), 0).astype(f32)
    sel = jnp.concatenate(
        [(place == rank_t[i : i + 1, :]).astype(f32) for i in range(EXPERTS)], axis=0
    )
    sel_b = sel.astype(bf16)
    sel_ref[...] = sel_b
    hot = ((lane == eff_ref[:, 0:1]) | (lane == eff_ref[:, 1:2])).astype(f32)
    after = (iota((rows, rows), 0) > iota((rows, rows), 1)).astype(f32).astype(bf16)
    rank = dot_nn(after, hot.astype(bf16))
    rank = jnp.where(hot > 0.0, rank, -1.0)
    slot = iota((1, slots), 1)
    widen = (slot // cap == iota((LANES, 1), 0)).astype(f32).astype(bf16)
    rank_s = dot_nn(rank.astype(bf16), widen)
    selt_ref[...] = (rank_s == (slot % cap).astype(f32)).astype(f32).astype(bf16)
    ch_s = dot_nn(sel, ch, precision=highest)
    of_slot = iota((slots, 1), 0) // cap
    gate = jnp.sum(jnp.where(lane == of_slot, ch_s, 0.0), axis=1, keepdims=True)
    gate_ref[...] = jnp.broadcast_to(gate, gate_ref.shape)
    send_ref[:, :width] = dot_nn(sel_b, two).astype(bf16)
    send_ref[:, width:] = (gate * dot_nn(sel_b, og_ref[...])).astype(bf16)


def expert_kernel(
    x_ref, g_ref, wg_ref, wu_ref, wd_ref, out_ref, hid_ref, gg_ref, ug_ref, fwd, back
):
    step = pl.program_id(0)
    width = x_ref.shape[1]

    @pl.when(step == 0)
    def _():
        fwd[...] = jnp.zeros_like(fwd)
        back[...] = jnp.zeros_like(back)

    x, g = x_ref[...], g_ref[...]
    gate = dot_nn(x, wg_ref[...])
    up = dot_nn(x, wu_ref[...])
    hid_grad = dot_nt(g, wd_ref[...])
    sig = 1.0 / (1.0 + jnp.exp(-gate))
    act = gate * sig
    hid = (act * up).astype(bf16)
    gg = (hid_grad * up * (sig + act * (1.0 - sig))).astype(bf16)
    ug = (hid_grad * act).astype(bf16)
    hid_ref[...] = hid
    gg_ref[...] = gg
    ug_ref[...] = ug
    fwd[...] += dot_nn(hid, wd_ref[...])
    back[...] += dot_nt(gg, wg_ref[...]) + dot_nt(ug, wu_ref[...])

    @pl.when(step == pl.num_programs(0) - 1)
    def _():
        out_ref[:, :width] = fwd[...].astype(bf16)
        out_ref[:, width:] = back[...].astype(bf16)


def experts(rows_in, w_gate, w_up, w_down, tile=512):
    rows = rows_in.shape[0]
    width = rows_in.shape[1] // 2
    hidden = w_gate.shape[2]
    half = lambda i: pl.BlockSpec((rows, width), lambda t, i=i: (0, i))
    inner = pl.BlockSpec((None, width, tile), lambda t: (0, 0, t))
    mid = pl.BlockSpec((rows, tile), lambda t: (0, t))
    return pl.pallas_call(
        expert_kernel,
        grid=(hidden // tile,),
        in_specs=[half(0), half(1), inner, inner, pl.BlockSpec((None, tile, width), lambda t: (0, t, 0))],
        out_specs=[pl.BlockSpec((rows, 2 * width), lambda t: (0, 0)), mid, mid, mid],
        out_shape=[jax.ShapeDtypeStruct((rows, 2 * width), bf16)]
        + [jax.ShapeDtypeStruct((rows, hidden), bf16)] * 3,
        scratch_shapes=[pltpu.VMEM((rows, width), f32), pltpu.VMEM((rows, width), f32)],
        compiler_params=params(),
        cost_estimate=pl.CostEstimate(
            flops=14 * rows * width * hidden,
            bytes_accessed=6 * width * hidden,
            transcendentals=rows * hidden,
        ),
        name="experts",
    )(rows_in, rows_in, w_gate, w_up, w_down)


def expert_wgrad_kernel(*refs, count):
    ins, (dg_ref, du_ref, dd_ref, xt) = refs[: 5 * count], refs[5 * count :]
    rows = ins[0].shape[0]

    @pl.when(pl.program_id(0) == 0)
    def _():
        for m in range(count):
            xt[:, m * rows : (m + 1) * rows] = ins[5 * m][...].T

    g, hid, gg, ug = (
        jnp.concatenate([ins[5 * m + i][...] for m in range(count)], axis=0) for i in range(1, 5)
    )
    dg_ref[...] = dot_nn(xt[...], gg).astype(bf16)
    du_ref[...] = dot_nn(xt[...], ug).astype(bf16)
    dd_ref[...] = dot_tn(hid, g).astype(bf16)


def expert_wgrad(parts, tile=512):
    rows = parts[0][0].shape[0]
    width = parts[0][0].shape[1] // 2
    hidden = parts[0][1].shape[1]
    half = lambda i: pl.BlockSpec((rows, width), lambda t, i=i: (0, i))
    mid = pl.BlockSpec((rows, tile), lambda t: (0, t))
    specs, args = [], []
    for rows_in, hid, gg, ug in parts:
        specs += [half(0), half(1), mid, mid, mid]
        args += [rows_in, rows_in, hid, gg, ug]
    inner = pl.BlockSpec((width, tile), lambda t: (0, t))
    return pl.pallas_call(
        functools.partial(expert_wgrad_kernel, count=len(parts)),
        grid=(hidden // tile,),
        in_specs=specs,
        out_specs=[inner, inner, pl.BlockSpec((tile, width), lambda t: (t, 0))],
        out_shape=[
            jax.ShapeDtypeStruct((width, hidden), bf16),
            jax.ShapeDtypeStruct((width, hidden), bf16),
            jax.ShapeDtypeStruct((hidden, width), bf16),
        ],
        scratch_shapes=[pltpu.VMEM((width, len(parts) * rows), bf16)],
        compiler_params=params(),
        cost_estimate=pl.CostEstimate(
            flops=6 * len(parts) * rows * width * hidden,
            bytes_accessed=6 * width * hidden,
            transcendentals=0,
        ),
        name="expert_wgrad",
    )(*args)


def combine(
    resid_ref, two_ref, ch_ref, eff_ref, og_ref, ret_ref, sel_ref, selt_ref, gate_ref,
    wout_ref, gain_ref, wr_ref, cv_ref,
    mixed_ref, rtot_ref, branch_ref, dl_ref, small_ref, cap,
):
    rows, width = resid_ref.shape
    slots = EXPERTS * cap
    lane = iota((1, LANES), 1)
    resid, two_b, ch = resid_ref[...], two_ref[...], ch_ref[...]
    two = two_b.astype(f32)
    og_b = og_ref[...]
    og = og_b.astype(f32)
    eo = ret_ref[:, :width].astype(f32)
    sel, selt = sel_ref[...], selt_ref[...]
    hot = ((lane == eff_ref[:, 0:1]) | (lane == eff_ref[:, 1:2])).astype(f32)
    dgate = jnp.sum(dot_nn(sel, og_b) * eo, axis=1, keepdims=True)
    by_target = jnp.where(lane == iota((slots, 1), 0) // cap, dgate, 0.0)
    dval = dot_nn(selt.astype(f32), by_target, precision=highest)
    self_dot = jnp.sum(og * two, axis=1, keepdims=True)
    cv_dot = dot_nt(og_b, cv_ref[...])
    gates = ch * hot
    keep = gates[:, EXPERTS + 1 : EXPERTS + 2]
    dval = jnp.where(lane == EXPERTS + 1, self_dot, dval)
    mixed = resid + dot_nn(selt, (gate_ref[:, 0:1] * eo).astype(bf16))
    dl_const = jnp.zeros((rows, LANES), f32)
    coef_cv = jnp.zeros((rows, LANES), f32)
    for j in range(CONSTS):
        e, at = EXPERTS + 2 + j, TARGETS + 2 * j
        a0, a1 = ch[:, at : at + 1], ch[:, at + 1 : at + 2]
        gate = gates[:, e : e + 1]
        with_cv = cv_dot[:, e : e + 1]
        dval = jnp.where(lane == e, a0 * self_dot + a1 * with_cv, dval)
        keep = keep + gate * a0
        mixed = mixed + (gate * a1) * cv_ref[e : e + 1, :].astype(f32)
        coef_cv = jnp.where(lane == TARGETS + 2 * CONSTS + j, gate * a1, coef_cv)
        da0, da1 = gate * self_dot, gate * with_cv
        mean = a0 * da0 + a1 * da1
        dl_const = jnp.where(lane == at, a0 * (da0 - mean), dl_const)
        dl_const = jnp.where(lane == at + 1, a1 * (da1 - mean), dl_const)
    mixed = mixed + keep * two
    mixed_ref[...] = mixed.astype(bf16)
    ch = jnp.where(lane < TARGETS, ch, 0.0)
    dch = hot * dval
    dl = ch * (dch - jnp.sum(ch * dch, axis=1, keepdims=True)) + dl_const
    dl_ref[...] = dl
    dl_hi = dl.astype(bf16)
    dl_lo = (dl - dl_hi.astype(f32)).astype(bf16)
    cc_hi = coef_cv.astype(bf16)
    cc_lo = (coef_cv - cc_hi.astype(f32)).astype(bf16)
    small = dot_tn(dl_hi, two_b) + dot_tn(dl_lo, two_b) + dot_tn(cc_hi, og_b) + dot_tn(cc_lo, og_b)
    two_grad = (
        keep * og
        + dot_nt(dl_hi, wr_ref[...])
        + dot_nt(dl_lo, wr_ref[...])
        + dot_nn(selt, ret_ref[:, width:])
    )
    inv = lax.rsqrt(jnp.mean(resid * resid, axis=1, keepdims=True) + norm_eps)
    xhat = resid * inv
    gain_grad = jnp.sum(two_grad * xhat, axis=0, keepdims=True)
    small_ref[...] = jnp.where(
        iota((small_ref.shape[0], 1), 0) == TARGETS + 3 * CONSTS, gain_grad, small[: small_ref.shape[0]]
    )
    scaled = two_grad * gain_ref[...]
    rtot = og + inv * (scaled - xhat * jnp.mean(scaled * xhat, axis=1, keepdims=True))
    rtot_ref[...] = rtot
    branch = rtot.astype(bf16)
    branch_ref[...] = branch
    return dot_nt(branch, wout_ref[...]).astype(bf16)


def of_micro(array, micro):
    return pl.BlockSpec((None,) + array.shape[1:], lambda i: (micro,) + (0,) * (array.ndim - 1))


def all_of(array):
    return pl.BlockSpec(array.shape, lambda i: (0,) * array.ndim)


UNIT = 48
PACK = 160
PART = 512


def place(out_ref, step, grad):
    low = grad.astype(bf16)
    per = low.shape[0] // UNIT
    for j in range(low.shape[1] // LANES):
        for k in range(per):
            out_ref[j * per + k, step * UNIT : (step + 1) * UNIT, :] = low[
                k * UNIT : (k + 1) * UNIT, j * LANES : (j + 1) * LANES
            ]


def clear_tail(out_ref):
    out_ref[:, 3 * UNIT :, :] = jnp.zeros((out_ref.shape[0], PACK - 3 * UNIT, LANES), bf16)


def wgrad_kv_kernel(core_ref, *refs, count):
    ins, (qo_ref, give_ref, keep_ref) = refs[: 5 * count], refs[5 * count :]
    t = pl.program_id(0)
    grad = 0.0
    for m in range(count):
        near, far, normed, dkv, _ = ins[5 * m : 5 * m + 5]
        half, rows = near.shape[0], normed.shape[0]
        grad = grad + dot_tn(near[...], dkv[:half]) + dot_tn(far[...], dkv[half : 2 * half])
        grad = grad + dot_tn(normed[rows - CLEN :], dkv[2 * half :])

    def fill(kv_ref, other_ref):
        for i in range(3):

            @pl.when(t == i)
            def _():
                place(kv_ref, i, grad)
                other_ref[:, i * UNIT : (i + 1) * UNIT, :] = qo_ref[...]

        @pl.when(t == 0)
        def _():
            clear_tail(kv_ref)
            clear_tail(other_ref)
            small = sum(ins[5 * m + 4][...] for m in range(count)).astype(bf16)
            for i in range(small.shape[1] // LANES):
                block = small[:, i * LANES : (i + 1) * LANES]
                kv_ref[2 * i, 3 * UNIT : 3 * UNIT + 16, :] = block[:16]
                kv_ref[2 * i + 1, 3 * UNIT : 3 * UNIT + 8, :] = block[16:24]

    @pl.when(core_ref[0] == 0)
    def _():
        fill(keep_ref, give_ref)

    @pl.when(core_ref[0] != 0)
    def _():
        fill(give_ref, keep_ref)


def wgrad_kv(core, qo, parts):
    rows, width = parts[0][2].shape[1:]
    half = parts[0][0].shape[0]
    whole = lambda n: pl.BlockSpec((n, width), lambda t, c: (0, 0))
    specs, args = [], []
    for m, p in enumerate(parts):
        specs += [
            whole(half), whole(half),
            pl.BlockSpec((None, rows, width), lambda t, c, m=m: (m, 0, 0)),
            pl.BlockSpec((2 * half + CLEN, PART), lambda t, c: (0, t)), whole(24),
        ]
        args += list(p)
    count = len(parts)
    chunks = qo.shape[0]
    specs.append(pl.BlockSpec((chunks, UNIT, LANES), lambda t, c: (0, t, 0)))
    return pl.pallas_call(
        functools.partial(wgrad_kv_kernel, count=count),
        grid_spec=pltpu.PrefetchScalarGridSpec(
            num_scalar_prefetch=1,
            grid=(2 * width // PART,),
            in_specs=specs,
            out_specs=[pl.BlockSpec((chunks, PACK, LANES), lambda t, c: (0, 0, 0))] * 2,
        ),
        out_shape=[jax.ShapeDtypeStruct((chunks, PACK, LANES), bf16)] * 2,
        compiler_params=params(),
        cost_estimate=pl.CostEstimate(
            flops=4 * count * (2 * half + CLEN) * width * width,
            bytes_accessed=12 * count * half * width,
            transcendentals=0,
        ),
        name="wgrad_kv",
    )(core, *args, qo)


def wgrad_qo_kernel(*refs, count):
    ins, out_ref = refs[: 4 * count], refs[4 * count]
    stack = lambda i: jnp.concatenate([ins[4 * m + i][...] for m in range(count)], axis=0)
    normed, dq, attn, branch = (stack(i) for i in range(4))
    width = dq.shape[1]
    query = dot_tn(normed, dq)
    out = dot_tn(attn.astype(bf16), branch)
    half = PART // 2
    for i in range(2 * width // PART):
        at = slice(i * half, (i + 1) * half)
        place(out_ref, i, jnp.concatenate([query[:, at], out[:, at]], axis=1))


def wgrad_qo(parts):
    rows, width = parts[0][1].shape
    chunks = width // UNIT * PART // LANES
    count = len(parts)
    specs = [s for m, p in enumerate(parts) for s in [of_micro(p[0], m)] + [all_of(a) for a in p[1:]]]
    return pl.pallas_call(
        functools.partial(wgrad_qo_kernel, count=count),
        grid=(1,),
        in_specs=specs,
        out_shape=jax.ShapeDtypeStruct((chunks, 3 * UNIT, LANES), bf16),
        compiler_params=params(),
        cost_estimate=pl.CostEstimate(
            flops=4 * count * rows * width * width,
            bytes_accessed=6 * width * width,
            transcendentals=0,
        ),
        name="wgrad_qo",
    )(*[a for p in parts for a in p])


def unpack_kernel(
    core_ref, mine_ref, other_ref, mine_tail, other_tail, gain_ref, wq_ref, wk_ref, wv_ref,
    query, key, value, out, gains, router, const, const_vec, total,
):
    step = pl.program_id(0)
    width = query.shape[0]
    per = width // UNIT
    cols = PART // 2 // LANES

    def fill(low, high, low_tail):
        for part, refs in ((low, (key, value)), (high, (query, out))):
            for j in range(2 * cols):
                ref, at = refs[j // cols], (j % cols) * LANES
                for k in range(per):
                    ref[k * UNIT : (k + 1) * UNIT, at : at + LANES] = part[j * per + k].astype(f32)

        @pl.when(step == 0)
        def _():
            for i in range(width // LANES):
                at = slice(i * LANES, (i + 1) * LANES)
                small = low_tail[2 * i].astype(f32)
                rest = low_tail[2 * i + 1].astype(f32)
                router[:, at] = small[:TARGETS]
                for c in range(CONSTS):
                    const[c, :, at] = small[TARGETS + 2 * c : TARGETS + 2 * c + 2]
                const_vec[:, at] = rest[:CONSTS]
                gains[0:1, at] = rest[CONSTS : CONSTS + 1]

    @pl.when(core_ref[0] == 0)
    def _():
        fill(mine_ref, other_ref, mine_tail)

    @pl.when(core_ref[0] != 0)
    def _():
        fill(other_ref, mine_ref, other_tail)

    part = 0.0
    for grad, w_ref in ((query, wq_ref), (key, wk_ref), (value, wv_ref)):
        prod = grad[...] * w_ref[...].astype(f32)
        part = part + sum(prod[:, i * LANES : (i + 1) * LANES] for i in range(cols))

    @pl.when(step == 0)
    def _():
        total[...] = part

    @pl.when(step > 0)
    def _():
        total[...] += part

    @pl.when(step == pl.num_programs(0) - 1)
    def _():
        summed = dot_nt(jnp.ones((8, LANES), f32), total[...], precision=highest)[0:1]
        gains[1:2, :] = summed / gain_ref[...]


def unpack(core, mine, other, gain, w_query, w_key, w_value):
    width = w_query.shape[0]
    chunks = mine.shape[0]
    body = pl.BlockSpec((chunks, UNIT, LANES), lambda t, c: (0, t, 0))
    tail = pl.BlockSpec((chunks, PACK - 3 * UNIT, LANES), lambda t, c: (0, 3 * UNIT // (PACK - 3 * UNIT), 0))
    col = pl.BlockSpec((width, PART // 2), lambda t, c: (0, t))
    small = [(2, width), (TARGETS, width), (CONSTS, 2, width), (CONSTS, width)]
    whole = lambda s: pl.BlockSpec(s, lambda t, c: (0,) * len(s))
    return pl.pallas_call(
        unpack_kernel,
        grid_spec=pltpu.PrefetchScalarGridSpec(
            num_scalar_prefetch=1,
            grid=(2 * width // PART,),
            in_specs=[body, body, tail, tail, whole((1, width)), col, col, col],
            out_specs=[col] * 4 + [whole(s) for s in small],
            scratch_shapes=[pltpu.VMEM((width, LANES), f32)],
        ),
        out_shape=[jax.ShapeDtypeStruct(s, f32) for s in [(width, width)] * 4 + small],
        compiler_params=params(),
        cost_estimate=pl.CostEstimate(
            flops=4 * width * width, bytes_accessed=24 * width * width, transcendentals=0
        ),
        name="unpack",
    )(core, mine, other, mine, other, gain, w_query, w_key, w_value)


def swap_cores(rows):
    return lax.ppermute(rows, "core", [(0, 1), (1, 0)])


def exchange(blocks, axes):
    return lax.all_to_all(blocks, axes, split_axis=0, concat_axis=0, tiled=True)


def spread_out(piece, axes):
    count = lax.axis_size(axes)
    return exchange(jnp.broadcast_to(piece[None], (count,) + piece.shape), axes)


def sum_ring(parts, axis, dim=0):
    count = lax.axis_size(axis)
    me = lax.axis_index(axis)
    part = lambda i: lax.dynamic_index_in_dim(parts, i, dim, keepdims=False)
    total = part(me).astype(f32)
    for step in range(1, count):
        ring = [(i, (i + step) % count) for i in range(count)]
        total = total + lax.ppermute(part((me + step) % count), axis, ring).astype(f32)
    return total


def after(value, *others):
    return lax.optimization_barrier((value, *others))[0]


def on_device(
    tokens, prior_logits, routes, drops, cont_lengths, norm_gain, w_query, w_key, w_value, w_out,
    ffn_gain, w_router, w_const, const_vec, w_gate, w_up, w_down, out_grad,
):
    micros, rows, width = tokens.shape[0], tokens.shape[3], tokens.shape[4]
    prompt = rows - CLEN
    cap = -(-(rows * 3 // 16) // 8) * 8
    chips = (lax.axis_size("context"), lax.axis_size("z"))
    half = chips[0] * chips[1] * prompt
    core = lax.axis_index("core").astype(jnp.int32)
    base = jnp.stack([lax.axis_index(("context", "z", "core")).astype(jnp.int32) * prompt, core])
    score_scale = 1.0 / math.sqrt(HEAD_SIZE)
    gain_one = norm_gain.astype(f32)
    gain_two = ffn_gain.astype(f32).reshape(1, width)

    gain_row = gain_one.reshape(1, width)
    core_arg = core.reshape(1)
    x = tokens[:, 0, 0]
    x_f = x.astype(f32)
    inv_one = lax.rsqrt(jnp.mean(x_f * x_f, axis=-1, keepdims=True) + norm_eps)
    normed = (x_f * inv_one * gain_one).astype(bf16)
    gathered = [spread_out(normed[0, :prompt], CHIPS)]
    for m in range(1, micros):
        gathered.append(spread_out(normed[m, :prompt], CHIPS))

    wr = jnp.concatenate(
        [w_router] + [w_const[j] for j in range(CONSTS)]
        + [jnp.zeros((width, LANES - TARGETS - 2 * CONSTS), bf16)], axis=1,
    )
    cv = jnp.zeros((LANES, width), bf16).at[EXPERTS + 2 : EXPERTS + 2 + CONSTS].set(const_vec)
    row_ids = jnp.arange(rows, dtype=jnp.int32)
    og = out_grad[:, 0, 0]
    live = row_ids[None] < prompt + cont_lengths[:, 0]
    active = (1 - drops[:, 0, 0]) * live[..., None].astype(jnp.int32)
    eff = jnp.where(active > 0, routes[:, 0, 0], -1)
    efft = jnp.swapaxes(eff, 1, 2)
    prior = jnp.pad(prior_logits[:, 0, 0], ((0, 0), (0, 0), (0, LANES - TARGETS)))

    st = []
    for m in range(micros):
        s = {}
        if m:
            gathered[m] = after(gathered[m], st[m - 1]["attn"])
        else:
            gathered[m] = after(gathered[m], wr, cv, eff, efft, prior, base, core_arg, gain_row, gain_two)
        s["near"] = gathered[m].reshape(half, width)
        s["far"] = swap_cores(s["near"])
        (
            s["attn"], s["lse"], s["q"], s["kv"],
            s["resid"], s["two"], s["ch"], send, s["sel"], s["selt"], s["gate"],
        ) = attn_fwd(
            base, normed, s["near"], s["far"], w_query, w_key, w_value,
            x, w_out, gain_two, wr, prior, eff, efft, og, chips, cap, m,
        )
        s["recv"] = exchange(send.reshape(EXPERTS, cap, 2 * width), EXPERT).reshape(
            EXPERTS * cap, 2 * width
        )
        st.append(s)
    for s in st:
        ret, s["hid"], s["gg"], s["ug"] = experts(s["recv"], w_gate, w_up, w_down)
        s["ret"] = exchange(ret.reshape(EXPERTS, cap, 2 * width), EXPERT).reshape(
            EXPERTS * cap, 2 * width
        )
    wide_grads = expert_wgrad([(s["recv"], s["hid"], s["gg"], s["ug"]) for s in st])
    for m in range(micros - 1):
        st[m]["ret"] = after(st[m]["ret"], wide_grads, st[m + 1]["ret"])
    wide_sum = lax.psum(tuple(wide_grads), ("dp", "context"))

    lift = lambda parts: jnp.stack(parts)[:, None, None]
    mixed, prior_grads, kv_parts, qo_parts, back_parts = [], [], [], [], []
    for m, s in enumerate(st):
        dq, dkv, out, s["rtot"], branch, dl, small = attn_bwd(
            base, s["q"], s["kv"], s["attn"], s["lse"],
            s["resid"], s["two"], s["ch"], eff, og, s["ret"], s["sel"], s["selt"], s["gate"],
            w_out, gain_two, wr, cv, chips, cap, m,
        )
        mixed.append(out)
        prior_grads.append(dl[:, :TARGETS])
        kv_parts.append((s["near"], s["far"], normed, dkv, small))
        qo_parts.append((normed, dq, s["attn"], branch))
        back_parts.append((dkv, dq))
    qo = wgrad_qo(qo_parts)
    give, keep = wgrad_kv(core_arg, qo, kv_parts)
    back_parts[0] = (after(back_parts[0][0], give), back_parts[0][1])
    (give_rows,) = back_proj(back_parts, w_key, w_value, w_query, 1)
    come = after(swap_cores(give), give_rows)
    keep = (keep.astype(f32) + come.astype(f32)).astype(bf16)
    dense = exchange(keep.reshape((lax.axis_size(FIRST), -1) + keep.shape[1:]), FIRST)
    come = swap_cores(give_rows)
    keep, mine = back_proj(back_parts, w_key, w_value, w_query, 0)
    rows_sum = (keep.astype(f32) + come.astype(f32)).astype(bf16)
    dense = after(dense, rows_sum)
    rows_sum = rows_sum.reshape(micros, chips[1], chips[0] * prompt, width)
    rows_sum = sum_ring(rows_sum, "z", 1).astype(bf16)
    dense = jnp.sum(dense.astype(f32), axis=0).astype(bf16)
    dense = jnp.sum(exchange(dense, REST).astype(f32), axis=0).astype(bf16)
    dense = after(dense, wide_sum, rows_sum)
    dense = spread_out(dense, ALL_CHIPS)
    wide_out = [g.astype(f32)[None] for g in wide_sum[1:]]
    mixed, prior_grads = lift(mixed), lift(prior_grads)
    rows_sum = after(rows_sum, wide_out, mixed, prior_grads)
    totals = sum_ring(rows_sum.reshape(micros, chips[0], prompt, width), "context", 1)
    token_grads = []
    for m, s in enumerate(st):
        grad = (mine[m] + jnp.pad(totals[m], ((0, CLEN), (0, 0)))) * gain_one
        xhat = x_f[m] * inv_one[m]
        grad = inv_one[m] * (grad - xhat * jnp.mean(grad * xhat, axis=-1, keepdims=True))
        token_grads.append((s["rtot"] + grad).astype(bf16))
    wide_out = [after(wide_sum[0], dense).astype(f32)[None]] + wide_out
    dense = after(dense, totals)
    rows_out = [mixed, lift(token_grads), prior_grads]
    query, key, value, out, gains, router, const, vec = unpack(
        core_arg, dense, swap_cores(dense), gain_row, w_query, w_key, w_value
    )
    return (
        *rows_out,
        gains[1],
        query,
        key,
        value,
        out,
        gains[0],
        router.T,
        jnp.swapaxes(const, 1, 2),
        vec,
        *wide_out,
    )


def solution(mesh):
    shape = mesh.devices.shape
    split = Mesh(
        mesh.devices.reshape(shape[0], shape[1], shape[2] // 2, 2), ("dp", "context", "z", "core")
    )
    slot = P(None, "dp", ("context", "z", "core"), None, None)
    expert = P(("z", "core"), None, None)
    return jax.shard_map(
        on_device,
        mesh=split,
        in_specs=(
            slot, slot, slot, slot, P(None, "dp", ("context", "z", "core")),
            *(P(),) * 9,
            *(expert,) * 3,
            slot,
        ),
        out_specs=(slot, slot, slot, *(P(),) * 9, *(expert,) * 3),
        check_vma=False,
    )
```

```python
import functools
import math

import jax
import jax.numpy as jnp
from jax import lax
from jax.experimental import pallas as pl
from jax.experimental.pallas import tpu as pltpu
from jax.sharding import Mesh, PartitionSpec as P

HEADS = 12
HEAD_SIZE = 64
EXPERTS = 8
CONSTS = 2
TARGETS = 12
CLEN = 128
QUAD = 4
LANES = 128

norm_eps = 1e-05
very_low = -1e30
highest = lax.Precision.HIGHEST
f32 = jnp.float32
bf16 = jnp.bfloat16
CHIPS = ("z", "context")
FIRST, REST = "z", ("dp", "context")
ALL_CHIPS = (FIRST,) + REST
EXPERT = ("z", "core")


def dot_nn(left, right, **kw):
    return jnp.dot(left, right, preferred_element_type=f32, **kw)


def dot_nt(left, right, **kw):
    return lax.dot_general(left, right, (((1,), (1,)), ((), ())), preferred_element_type=f32, **kw)


def dot_tn(left, right, **kw):
    return lax.dot_general(left, right, (((0,), (0,)), ((), ())), preferred_element_type=f32, **kw)


def halves(wide):
    high = wide.astype(bf16)
    return high, (wide - high.astype(f32)).astype(bf16)


def iota(shape, dim):
    return lax.broadcasted_iota(jnp.int32, shape, dim)


def params():
    return pltpu.CompilerParams(vmem_limit_bytes=63_400_000)


def head_masks(dtype):
    lane_head = iota((1, QUAD * HEAD_SIZE), 1) // HEAD_SIZE
    return [(lane_head == h).astype(f32).astype(dtype) for h in range(QUAD)]


def spread(rows, prompt, dtype):
    masks = head_masks(dtype)
    return jnp.concatenate(
        [rows[:prompt] * m for m in masks] + [rows[prompt:] * m for m in masks], axis=0
    )


def gather_heads(stacked, prompt, dtype):
    masks = head_masks(dtype)
    top, low = 0.0, 0.0
    first = QUAD * prompt
    for h in range(QUAD):
        top = top + stacked[h * prompt : (h + 1) * prompt] * masks[h]
        low = low + stacked[first + h * CLEN : first + (h + 1) * CLEN] * masks[h]
    return jnp.concatenate([top, low], axis=0)


def first_norm_kernel(x_ref, gain_ref, normed_ref, copies_ref, prompt_ref):
    x = x_ref[...].astype(f32)
    scale = lax.rsqrt(jnp.mean(x * x, axis=1, keepdims=True) + norm_eps)
    normed = (x * scale * gain_ref[...]).astype(bf16)
    normed_ref[...] = normed
    prompt = copies_ref.shape[1]
    prompt_ref[...] = normed[:prompt]

    @pl.when(pl.program_id(0) == 0)
    def _():
        for i in range(copies_ref.shape[0]):
            copies_ref[i] = normed[:prompt]


def first_norm(x, gain, copies):
    micros, rows, width = x.shape
    of_micro = pl.BlockSpec((None, rows, width), lambda m: (m, 0, 0))
    shape = (copies, rows - CLEN, width)
    return pl.pallas_call(
        first_norm_kernel,
        grid=(micros,),
        in_specs=[of_micro, pl.BlockSpec((1, width), lambda m: (0, 0))],
        out_specs=[
            of_micro,
            pl.BlockSpec(shape, lambda m: (0, 0, 0)),
            pl.BlockSpec(shape[1:], lambda m: (m, 0)),
        ],
        out_shape=[
            jax.ShapeDtypeStruct(x.shape, bf16),
            jax.ShapeDtypeStruct(shape, bf16),
            jax.ShapeDtypeStruct((micros * shape[1], width), bf16),
        ],
        compiler_params=params(),
        cost_estimate=pl.CostEstimate(
            flops=8 * micros * rows * width, bytes_accessed=4 * micros * rows * width, transcendentals=0
        ),
        name="first_norm",
    )(x, gain)


def key_places(core, keys, prompt, chips, j):
    half = keys // 2
    other = jnp.where(j >= half, 1, 0)
    chip = (j - other * half) // prompt
    chip = (chip % chips[0]) * chips[1] + chip // chips[0]
    slot = chip * 2 + jnp.where(other > 0, 1 - core, core)
    return slot * prompt + (j & (prompt - 1))


def attn_fwd_kernel(
    base_ref, normed_ref, near_ref, far_ref, wq_ref, wkv_ref,
    x_ref, wout_ref, gain_ref, wr_ref, prior_ref, eff_ref, efft_ref, og_ref,
    o_ref, lse_ref, q_ref, kv_ref,
    resid_ref, two_ref, ch_ref, send_ref, sel_ref, selt_ref, gate_ref, o_all,
    *, chips, cap,
):
    g = pl.program_id(0)
    prompt = q_ref.shape[0] - CLEN
    keys = kv_ref.shape[0] - CLEN
    half = keys // 2
    wide = QUAD * HEAD_SIZE
    masks = head_masks(bf16)
    masks_f = head_masks(f32)
    ones = jnp.ones((8, LANES), f32)

    def to_row(column):
        spare = jnp.where(iota((column.shape[0], LANES), 1) == 0, column, 0.0)
        return dot_nt(ones, spare, precision=highest)

    q = dot_nn(normed_ref[...], wq_ref[...]).astype(bf16).astype(f32)
    q_ref[...] = (q * (1.0 / math.sqrt(HEAD_SIZE))).astype(bf16)
    for rows, at in ((near_ref, 0), (far_ref, half)):
        kv_ref[at : at + half] = dot_nn(rows[...], wkv_ref[...]).astype(bf16)
    kv_ref[keys:] = dot_nn(normed_ref[prompt:], wkv_ref[...]).astype(bf16)
    q_top, q_low = q_ref[:prompt], q_ref[prompt:]
    q_p = jnp.concatenate([q_top * m for m in masks], axis=0)
    s = dot_nt(q_p, kv_ref[:keys, :wide])
    limit = base_ref[0] + (iota((QUAD * prompt, 1), 0) & (prompt - 1))
    s = jnp.where(key_places(base_ref[1], keys, prompt, chips, iota((1, keys), 1)) <= limit, s, very_low)
    top = jnp.max(s, axis=1, keepdims=True)
    p = jnp.exp(s - top)
    total = jnp.sum(p, axis=1, keepdims=True)
    out = dot_nn(p.astype(bf16), kv_ref[:keys, wide:]) * (1.0 / total)
    lse_ref[:, : QUAD * prompt] = to_row(top + jnp.log(total))
    top_out = sum(out[h * prompt : (h + 1) * prompt] * masks_f[h] for h in range(QUAD))
    low_out = 0.0
    per = 2
    for part in range(QUAD // per):
        hs = range(part * per, (part + 1) * per)
        rows = per * CLEN
        q_c = jnp.concatenate([q_low * masks[h] for h in hs], axis=0)
        s = dot_nt(q_c, kv_ref[:keys, :wide])
        own = dot_nt(q_c, kv_ref[keys:, :wide])
        own = jnp.where(
            iota((1, CLEN), 1) <= (iota((rows, 1), 0) & (CLEN - 1)), own, very_low
        )
        top = jnp.maximum(
            jnp.max(s, axis=1, keepdims=True), jnp.max(own, axis=1, keepdims=True)
        )
        p = jnp.exp(s - top)
        p_own = jnp.exp(own - top)
        total = jnp.sum(p, axis=1, keepdims=True) + jnp.sum(p_own, axis=1, keepdims=True)
        out = dot_nn(p.astype(bf16), kv_ref[:keys, wide:])
        out = out + dot_nn(p_own.astype(bf16), kv_ref[keys:, wide:])
        out = out * (1.0 / total)
        at = QUAD * prompt + part * rows
        lse_ref[:, at : at + rows] = to_row(top + jnp.log(total))
        for i, h in enumerate(hs):
            low_out = low_out + out[i * CLEN : (i + 1) * CLEN] * masks_f[h]
    attn = jnp.concatenate([top_out, low_out], axis=0)
    o_ref[...] = attn
    o_all[g] = attn.astype(bf16)

    @pl.when(g == o_all.shape[0] - 1)
    def _():
        attended = jnp.concatenate([o_all[i] for i in range(o_all.shape[0])], axis=1)
        route(
            attended, x_ref, wout_ref, gain_ref, wr_ref, prior_ref, eff_ref, efft_ref, og_ref,
            resid_ref, two_ref, ch_ref, send_ref, sel_ref, selt_ref, gate_ref, cap,
        )


def attn_fwd(
    base, normed, near, far, w_query, w_kv, x, w_out, gain, wr, prior, eff, efft, og,
    chips, cap, micro,
):
    rows, width = normed.shape[1:]
    half = near.shape[0]
    every = 2 * half + CLEN
    quads = HEADS // QUAD
    wide = QUAD * HEAD_SIZE
    slots = EXPERTS * cap
    col = lambda n, w=wide: pl.BlockSpec((n, w), lambda g, b: (0, g))
    whole = lambda n, w=width: pl.BlockSpec((n, w), lambda g, b: (0, 0))
    of_micro = lambda a: pl.BlockSpec((None,) + a.shape[1:], lambda g, b: (micro, 0, 0))
    routed = [
        ((rows, width), f32), ((rows, width), bf16), ((rows, LANES), f32), ((slots, 2 * width), bf16),
        ((slots, rows), bf16), ((rows, slots), bf16), ((slots, LANES), f32),
    ]
    return pl.pallas_call(
        functools.partial(attn_fwd_kernel, chips=chips, cap=cap),
        grid_spec=pltpu.PrefetchScalarGridSpec(
            num_scalar_prefetch=1,
            grid=(quads,),
            in_specs=[
                of_micro(normed), whole(half), whole(half), col(width), col(width, 2 * wide),
                of_micro(x), whole(width), whole(1), whole(width, LANES), of_micro(prior),
                of_micro(eff), of_micro(efft), of_micro(og),
            ],
            out_specs=[
                col(rows),
                pl.BlockSpec((None, 8, QUAD * rows), lambda g, b: (g, 0, 0)),
                col(rows),
                col(every, 2 * wide),
            ]
            + [whole(*s) for s, _ in routed],
            scratch_shapes=[pltpu.VMEM((quads, rows, wide), bf16)],
        ),
        out_shape=[
            jax.ShapeDtypeStruct((rows, width), f32),
            jax.ShapeDtypeStruct((quads, 8, QUAD * rows), f32),
            jax.ShapeDtypeStruct((rows, width), bf16),
            jax.ShapeDtypeStruct((every, 2 * width), bf16),
        ]
        + [jax.ShapeDtypeStruct(s, t) for s, t in routed],
        compiler_params=params(),
        cost_estimate=pl.CostEstimate(
            flops=16 * rows * every * width + 4 * every * width * width,
            bytes_accessed=4 * every * width,
            transcendentals=rows * every * HEADS,
        ),
        name="attn_fwd",
    )(base, normed, near, far, w_query, w_kv, x, w_out, gain, wr, prior, eff, efft, og)


def attn_bwd_kernel(
    base_ref, q_ref, kv_ref, o_ref, lse_ref,
    resid_ref, two_ref, ch_ref, eff_ref, og_ref, ret_ref, sel_ref, selt_ref, gate_ref,
    wout_ref, gain_ref, wr_ref, cv_ref, *rest, block, chips, cap
):
    (
        dq_ref, dkv_ref, mixed_ref, rtot_ref, branch_ref, dl_ref, small_ref, qm, dom, dqt, do_all
    ) = rest[-11:]
    g = pl.program_id(0)
    quads = do_all.shape[0]

    @pl.when(g == 0)
    def _():
        grad = combine(
            resid_ref, two_ref, ch_ref, eff_ref, og_ref, ret_ref, sel_ref, selt_ref, gate_ref,
            wout_ref, gain_ref, wr_ref, cv_ref,
            mixed_ref, rtot_ref, branch_ref, dl_ref, small_ref, cap,
        )
        for i in range(quads):
            do_all[i] = grad[:, i * QUAD * HEAD_SIZE : (i + 1) * QUAD * HEAD_SIZE]

    do_now = do_all[g]
    prompt = q_ref.shape[0] - CLEN
    keys = kv_ref.shape[0] - CLEN
    wide = QUAD * HEAD_SIZE
    qm[...] = spread(q_ref[...], prompt, bf16)
    dom[...] = spread(do_now, prompt, bf16)
    prod = spread(do_now.astype(f32) * o_ref[...], prompt, f32)
    ones = jnp.ones((8, prod.shape[1]), bf16)
    prod_high, prod_low = halves(prod)
    delta = (dot_nt(ones, prod_high) + dot_nt(ones, prod_low))[0:1]
    lse = lse_ref[0:1, :]
    first = QUAD * prompt
    ahead = (iota((prompt, first), 1) & (prompt - 1)) - iota((prompt, first), 0)
    q_all, do_all = qm[...], dom[...]

    def one(rows, mask):
        kk, vv = kv_ref[rows, :wide], kv_ref[rows, wide:]
        p = jnp.exp(dot_nt(kk, q_all) - lse)
        p = mask(p)
        ds = p * (dot_nt(vv, do_all) - delta)
        pb, dsb = p.astype(bf16), ds.astype(bf16)
        dkv_ref[rows, :wide] = dot_nn(dsb, q_all).astype(bf16)
        dkv_ref[rows, wide:] = dot_nn(pb, do_all).astype(bf16)
        return dot_tn(kk, dsb)

    def own_mask(p):
        lane = iota((1, p.shape[1]), 1)
        own_row = jnp.where(lane < first, -1, (lane - first) & (CLEN - 1))
        return jnp.where(iota((CLEN, 1), 0) <= own_row, p, 0.0)

    dqt[...] = one(pl.ds(keys, CLEN), own_mask)

    def step(i, unused):
        at = i * block

        def mask(p):
            rows = []
            for r in range(0, block, prompt):
                gap = key_places(base_ref[1], keys, prompt, chips, at + r) - base_ref[0]
                rows.append(jnp.where(ahead >= gap, p[r : r + prompt, :first], 0.0))
            return jnp.concatenate([jnp.concatenate(rows, axis=0), p[:, first:]], axis=1)

        dqt[...] += one(pl.ds(at, block), mask)
        return unused

    for i in range(keys // block):
        step(i, 0)
    dq = gather_heads(dqt[...].T, prompt, f32)
    dq = (dq * (1.0 / math.sqrt(HEAD_SIZE))).astype(bf16)
    dq_ref[...] = dq


def attn_bwd(
    base, q, kv, o, lse, resid, two, ch, eff, og, ret, sel, selt, gate, w_out, gain, wr, cv,
    chips, cap, micro, before, block=1024,
):
    rows, width = q.shape
    every = kv.shape[0]
    quads = HEADS // QUAD
    wide = QUAD * HEAD_SIZE
    micros = eff.shape[0]
    col = lambda n, w=wide: pl.BlockSpec((n, w), lambda g, b: (0, g))
    whole = lambda a: pl.BlockSpec(a.shape, lambda g, b: (0, 0))
    of_micro = lambda a: pl.BlockSpec((None,) + a.shape[1:], lambda g, b: (micro, 0, 0))
    mixing = [
        jax.ShapeDtypeStruct((micros, rows, width), bf16),
        jax.ShapeDtypeStruct((micros, rows, width), f32),
        jax.ShapeDtypeStruct((rows, width), bf16),
        jax.ShapeDtypeStruct((micros, rows, LANES), f32),
        jax.ShapeDtypeStruct((24, width), f32),
    ]
    args = (base, q, kv, o, lse, resid, two, ch, eff, og, ret, sel, selt, gate, w_out, gain, wr, cv)
    return pl.pallas_call(
        functools.partial(
            attn_bwd_kernel, block=min(block, (every - CLEN) // 2), chips=chips, cap=cap
        ),
        grid_spec=pltpu.PrefetchScalarGridSpec(
            num_scalar_prefetch=1,
            grid=(quads,),
            in_specs=[
                col(rows), col(every, 2 * wide), col(rows),
                pl.BlockSpec((None, 8, QUAD * rows), lambda g, b: (g, 0, 0)),
                whole(resid), whole(two), whole(ch), of_micro(eff), of_micro(og), whole(ret),
                whole(sel), whole(selt), whole(gate), whole(w_out), whole(gain), whole(wr), whole(cv),
            ]
            + [pl.BlockSpec(memory_space=pl.ANY) for _ in before],
            out_specs=[col(rows), col(every, 2 * wide)]
            + [of_micro(a) if len(a.shape) == 3 else whole(a) for a in mixing],
            scratch_shapes=[
                pltpu.VMEM((QUAD * rows, wide), bf16),
                pltpu.VMEM((QUAD * rows, wide), bf16),
                pltpu.VMEM((wide, QUAD * rows), f32),
                pltpu.VMEM((quads, rows, wide), bf16),
            ],
        ),
        out_shape=[
            jax.ShapeDtypeStruct((rows, width), bf16),
            jax.ShapeDtypeStruct((every, 2 * width), bf16),
        ]
        + mixing,
        input_output_aliases={len(args) + i: out for i, out in enumerate((2, 3, 5)[: len(before)])},
        compiler_params=params(),
        cost_estimate=pl.CostEstimate(
            flops=40 * rows * every * width,
            bytes_accessed=8 * every * width,
            transcendentals=rows * every * HEADS,
        ),
        name="attn_bwd",
    )(*args, *before)


def back_proj_kernel(*refs, count):
    ins, (w_ref, out_ref) = refs[:count], refs[count:]
    for m in range(count):

        @pl.when(pl.program_id(0) == m)
        def _():
            out_ref[...] = dot_nt(ins[m][...], w_ref[...]).astype(bf16)


def back_proj(dkvs, w_kv, which):
    count = len(dkvs)
    width = w_kv.shape[0]
    half = (dkvs[0].shape[0] - CLEN) // 2
    return pl.pallas_call(
        functools.partial(back_proj_kernel, count=count),
        grid=(count,),
        in_specs=[pl.BlockSpec((half, 2 * width), lambda t: (which, 0)) for _ in dkvs]
        + [pl.BlockSpec((width, 2 * width), lambda t: (0, 0))],
        out_specs=pl.BlockSpec((None, half, width), lambda t: (t, 0, 0)),
        out_shape=jax.ShapeDtypeStruct((count, half, width), bf16),
        compiler_params=params(),
        cost_estimate=pl.CostEstimate(
            flops=count * half * width * width, bytes_accessed=2 * count * half * width, transcendentals=0
        ),
        name="back_proj",
    )(*dkvs, w_kv)


def own_proj_kernel(*refs, count):
    ins, (wq_ref, wkv_ref, out_ref) = refs[: 2 * count], refs[2 * count :]
    for m in range(count):
        dq = dot_nt(ins[2 * m][...], wq_ref[...])
        prompt = dq.shape[0] - CLEN
        out_ref[m, :prompt] = dq[:prompt]
        out_ref[m, prompt:] = dq[prompt:] + dot_nt(ins[2 * m + 1][...], wkv_ref[...])


def own_proj(parts, w_query, w_kv):
    rows, width = parts[0][0].shape
    every = parts[0][1].shape[0]
    whole = lambda n, w=width: pl.BlockSpec((n, w), lambda i: (0, 0))
    tail = pl.BlockSpec((CLEN, 2 * width), lambda i: (every // CLEN - 1, 0))
    count = len(parts)
    return pl.pallas_call(
        functools.partial(own_proj_kernel, count=count),
        grid=(1,),
        in_specs=[whole(rows), tail] * count + [whole(width), whole(width, 2 * width)],
        out_shape=jax.ShapeDtypeStruct((count, rows, width), f32),
        compiler_params=params(),
        cost_estimate=pl.CostEstimate(
            flops=6 * count * rows * width * width, bytes_accessed=6 * width * width, transcendentals=0
        ),
        name="own_proj",
    )(*[a for p in parts for a in p], w_query, w_kv)


def route(
    attended, x_ref, wout_ref, gain_ref, wr_ref, prior_ref, eff_ref, efft_ref, og_ref,
    resid_ref, two_ref, ch_ref, send_ref, sel_ref, selt_ref, gate_ref, cap,
):
    rows, width = x_ref.shape
    slots = EXPERTS * cap
    resid = x_ref[...].astype(f32) + dot_nn(attended, wout_ref[...])
    resid_ref[...] = resid
    inv = lax.rsqrt(jnp.mean(resid * resid, axis=1, keepdims=True) + norm_eps)
    two = (resid * inv * gain_ref[...]).astype(bf16)
    two_ref[...] = two
    lane = iota((1, LANES), 1)
    logits = dot_nn(two, wr_ref[...]) + prior_ref[...]
    masked = jnp.where(lane < TARGETS, logits, very_low)
    e = jnp.exp(masked - jnp.max(masked, axis=1, keepdims=True))
    ch = e * (1.0 / jnp.sum(e, axis=1, keepdims=True))
    for j in range(CONSTS):
        at = TARGETS + 2 * j
        diff = logits[:, at + 1 : at + 2] - logits[:, at : at + 1]
        ch = jnp.where(lane == at, 1.0 / (1.0 + jnp.exp(diff)), ch)
        ch = jnp.where(lane == at + 1, 1.0 / (1.0 + jnp.exp(-diff)), ch)
    ch_ref[...] = ch
    target = iota((16, rows), 0)
    hot_t = ((target == efft_ref[0:1, :]) | (target == efft_ref[1:2, :])).astype(f32)
    before = (iota((rows, rows), 0) < iota((rows, rows), 1)).astype(f32).astype(bf16)
    rank_t = dot_nn(hot_t.astype(bf16), before)
    rank_t = jnp.where(hot_t > 0.0, rank_t, -1.0)
    place = iota((cap, 1), 0).astype(f32)
    sel = jnp.concatenate(
        [(place == rank_t[i : i + 1, :]).astype(f32) for i in range(EXPERTS)], axis=0
    )
    sel_b = sel.astype(bf16)
    sel_ref[...] = sel_b
    hot = ((lane == eff_ref[:, 0:1]) | (lane == eff_ref[:, 1:2])).astype(f32)
    after = (iota((rows, rows), 0) > iota((rows, rows), 1)).astype(f32).astype(bf16)
    rank = dot_nn(after, hot.astype(bf16))
    rank = jnp.where(hot > 0.0, rank, -1.0)
    slot = iota((1, slots), 1)
    widen = (slot // cap == iota((LANES, 1), 0)).astype(f32).astype(bf16)
    rank_s = dot_nn(rank.astype(bf16), widen)
    selt_ref[...] = (rank_s == (slot % cap).astype(f32)).astype(f32).astype(bf16)
    ch_high, ch_low = halves(ch)
    ch_s = dot_nn(sel_b, ch_high) + dot_nn(sel_b, ch_low)
    of_slot = iota((slots, 1), 0) // cap
    gate = jnp.sum(jnp.where(lane == of_slot, ch_s, 0.0), axis=1, keepdims=True)
    gate_ref[...] = jnp.broadcast_to(gate, gate_ref.shape)
    send_ref[:, :width] = dot_nn(sel_b, two).astype(bf16)
    send_ref[:, width:] = (gate * dot_nn(sel_b, og_ref[...])).astype(bf16)


def expert_kernel(
    x_ref, g_ref, wg_ref, wu_ref, wd_ref, out_ref, hid_ref, gg_ref, ug_ref, fwd, back
):
    step = pl.program_id(0)
    width = x_ref.shape[1]

    @pl.when(step == 0)
    def _():
        fwd[...] = jnp.zeros_like(fwd)
        back[...] = jnp.zeros_like(back)

    x, g = x_ref[...], g_ref[...]
    gate = dot_nn(x, wg_ref[...])
    up = dot_nn(x, wu_ref[...])
    hid_grad = dot_nt(g, wd_ref[...])
    sig = 1.0 / (1.0 + jnp.exp(-gate))
    act = gate * sig
    hid = (act * up).astype(bf16)
    gg = (hid_grad * up * (sig + act * (1.0 - sig))).astype(bf16)
    ug = (hid_grad * act).astype(bf16)
    hid_ref[...] = hid
    gg_ref[...] = gg
    ug_ref[...] = ug
    fwd[...] += dot_nn(hid, wd_ref[...])
    back[...] += dot_nt(gg, wg_ref[...]) + dot_nt(ug, wu_ref[...])

    @pl.when(step == pl.num_programs(0) - 1)
    def _():
        out_ref[:, :width] = fwd[...].astype(bf16)
        out_ref[:, width:] = back[...].astype(bf16)


def experts(rows_in, w_gate, w_up, w_down, tile=512):
    rows = rows_in.shape[0]
    width = rows_in.shape[1] // 2
    hidden = w_gate.shape[2]
    half = lambda i: pl.BlockSpec((rows, width), lambda t, i=i: (0, i))
    inner = pl.BlockSpec((None, width, tile), lambda t: (0, 0, t))
    mid = pl.BlockSpec((rows, tile), lambda t: (0, t))
    return pl.pallas_call(
        expert_kernel,
        grid=(hidden // tile,),
        in_specs=[half(0), half(1), inner, inner, pl.BlockSpec((None, tile, width), lambda t: (0, t, 0))],
        out_specs=[pl.BlockSpec((rows, 2 * width), lambda t: (0, 0)), mid, mid, mid],
        out_shape=[jax.ShapeDtypeStruct((rows, 2 * width), bf16)]
        + [jax.ShapeDtypeStruct((rows, hidden), bf16)] * 3,
        scratch_shapes=[pltpu.VMEM((rows, width), f32), pltpu.VMEM((rows, width), f32)],
        compiler_params=params(),
        cost_estimate=pl.CostEstimate(
            flops=14 * rows * width * hidden,
            bytes_accessed=6 * width * hidden,
            transcendentals=rows * hidden,
        ),
        name="experts",
    )(rows_in, rows_in, w_gate, w_up, w_down)


def expert_wgrad_kernel(*refs, count):
    ins, (dg_ref, du_ref, dd_ref, xt) = refs[: 5 * count], refs[5 * count :]
    rows = ins[0].shape[0]

    @pl.when(pl.program_id(0) == 0)
    def _():
        for m in range(count):
            xt[:, m * rows : (m + 1) * rows] = ins[5 * m][...].T

    g, hid, gg, ug = (
        jnp.concatenate([ins[5 * m + i][...] for m in range(count)], axis=0) for i in range(1, 5)
    )
    dg_ref[...] = dot_nn(xt[...], gg).astype(bf16)
    du_ref[...] = dot_nn(xt[...], ug).astype(bf16)
    dd_ref[...] = dot_tn(hid, g).astype(bf16)


def expert_wgrad(parts, tile=512):
    rows = parts[0][0].shape[0]
    width = parts[0][0].shape[1] // 2
    hidden = parts[0][1].shape[1]
    half = lambda i: pl.BlockSpec((rows, width), lambda t, i=i: (0, i))
    mid = pl.BlockSpec((rows, tile), lambda t: (0, t))
    specs, args = [], []
    for rows_in, hid, gg, ug in parts:
        specs += [half(0), half(1), mid, mid, mid]
        args += [rows_in, rows_in, hid, gg, ug]
    inner = pl.BlockSpec((width, tile), lambda t: (0, t))
    return pl.pallas_call(
        functools.partial(expert_wgrad_kernel, count=len(parts)),
        grid=(hidden // tile,),
        in_specs=specs,
        out_specs=[inner, inner, pl.BlockSpec((tile, width), lambda t: (t, 0))],
        out_shape=[
            jax.ShapeDtypeStruct((width, hidden), bf16),
            jax.ShapeDtypeStruct((width, hidden), bf16),
            jax.ShapeDtypeStruct((hidden, width), bf16),
        ],
        scratch_shapes=[pltpu.VMEM((width, len(parts) * rows), bf16)],
        compiler_params=params(),
        cost_estimate=pl.CostEstimate(
            flops=6 * len(parts) * rows * width * hidden,
            bytes_accessed=6 * width * hidden,
            transcendentals=0,
        ),
        name="expert_wgrad",
    )(*args)


def combine(
    resid_ref, two_ref, ch_ref, eff_ref, og_ref, ret_ref, sel_ref, selt_ref, gate_ref,
    wout_ref, gain_ref, wr_ref, cv_ref,
    mixed_ref, rtot_ref, branch_ref, dl_ref, small_ref, cap,
):
    rows, width = resid_ref.shape
    slots = EXPERTS * cap
    lane = iota((1, LANES), 1)
    resid, two_b, ch = resid_ref[...], two_ref[...], ch_ref[...]
    two = two_b.astype(f32)
    og_b = og_ref[...]
    og = og_b.astype(f32)
    eo = ret_ref[:, :width].astype(f32)
    sel, selt = sel_ref[...], selt_ref[...]
    hot = ((lane == eff_ref[:, 0:1]) | (lane == eff_ref[:, 1:2])).astype(f32)
    dgate = jnp.sum(dot_nn(sel, og_b) * eo, axis=1, keepdims=True)
    by_target = jnp.where(lane == iota((slots, 1), 0) // cap, dgate, 0.0)
    by_high, by_low = halves(by_target)
    dval = dot_nn(selt, by_high) + dot_nn(selt, by_low)
    self_dot = jnp.sum(og * two, axis=1, keepdims=True)
    cv_dot = dot_nt(og_b, cv_ref[...])
    gates = ch * hot
    keep = gates[:, EXPERTS + 1 : EXPERTS + 2]
    dval = jnp.where(lane == EXPERTS + 1, self_dot, dval)
    mixed = resid + dot_nn(selt, (gate_ref[:, 0:1] * eo).astype(bf16))
    dl_const = jnp.zeros((rows, LANES), f32)
    coef_cv = jnp.zeros((rows, LANES), f32)
    for j in range(CONSTS):
        e, at = EXPERTS + 2 + j, TARGETS + 2 * j
        a0, a1 = ch[:, at : at + 1], ch[:, at + 1 : at + 2]
        gate = gates[:, e : e + 1]
        with_cv = cv_dot[:, e : e + 1]
        dval = jnp.where(lane == e, a0 * self_dot + a1 * with_cv, dval)
        keep = keep + gate * a0
        mixed = mixed + (gate * a1) * cv_ref[e : e + 1, :].astype(f32)
        coef_cv = jnp.where(lane == TARGETS + 2 * CONSTS + j, gate * a1, coef_cv)
        da0, da1 = gate * self_dot, gate * with_cv
        mean = a0 * da0 + a1 * da1
        dl_const = jnp.where(lane == at, a0 * (da0 - mean), dl_const)
        dl_const = jnp.where(lane == at + 1, a1 * (da1 - mean), dl_const)
    mixed = mixed + keep * two
    mixed_ref[...] = mixed.astype(bf16)
    ch = jnp.where(lane < TARGETS, ch, 0.0)
    dch = hot * dval
    dl = ch * (dch - jnp.sum(ch * dch, axis=1, keepdims=True)) + dl_const
    dl_ref[...] = dl
    dl_hi, dl_lo = halves(dl)
    cc_hi, cc_lo = halves(coef_cv)
    small = dot_tn(dl_hi, two_b) + dot_tn(dl_lo, two_b) + dot_tn(cc_hi, og_b) + dot_tn(cc_lo, og_b)
    two_grad = (
        keep * og
        + dot_nt(dl_hi, wr_ref[...])
        + dot_nt(dl_lo, wr_ref[...])
        + dot_nn(selt, ret_ref[:, width:])
    )
    inv = lax.rsqrt(jnp.mean(resid * resid, axis=1, keepdims=True) + norm_eps)
    xhat = resid * inv
    gain_grad = jnp.sum(two_grad * xhat, axis=0, keepdims=True)
    small_ref[...] = jnp.where(
        iota((small_ref.shape[0], 1), 0) == TARGETS + 3 * CONSTS, gain_grad, small[: small_ref.shape[0]]
    )
    scaled = two_grad * gain_ref[...]
    rtot = og + inv * (scaled - xhat * jnp.mean(scaled * xhat, axis=1, keepdims=True))
    rtot_ref[...] = rtot
    branch = rtot.astype(bf16)
    branch_ref[...] = branch
    return dot_nt(branch, wout_ref[...]).astype(bf16)


def of_micro(array, micro):
    return pl.BlockSpec((None,) + array.shape[1:], lambda i: (micro,) + (0,) * (array.ndim - 1))


def all_of(array):
    return pl.BlockSpec(array.shape, lambda i: (0,) * array.ndim)


UNIT = 48
PACK = 160
PART = 512


def units(grad):
    low = grad.astype(bf16)
    each = low.shape[0] // UNIT // 2
    for j in range(low.shape[1] // LANES):
        for k in range(2 * each):
            unit = low[k * UNIT : (k + 1) * UNIT, j * LANES : (j + 1) * LANES]
            yield j, k // each, k % each, unit


def wgrad_qo_kernel(*refs, count):
    ins, out_ref = refs[: 4 * count], refs[4 * count]
    stack = lambda i: jnp.concatenate([ins[4 * m + i][...] for m in range(count)], axis=0)
    normed, dq, attn, branch = (stack(i) for i in range(4))
    query = dot_tn(normed, dq)
    out = dot_tn(attn.astype(bf16), branch)
    half = PART // 2
    each = query.shape[0] // UNIT // 2
    for step in range(query.shape[1] // half):
        at = slice(step * half, (step + 1) * half)
        for j, c, k, unit in units(jnp.concatenate([query[:, at], out[:, at]], axis=1)):
            out_ref[c, j * each + k, step * UNIT : (step + 1) * UNIT, :] = unit


def wgrad_qo(parts):
    rows, width = parts[0][1].shape
    count = len(parts)
    specs = [s for m, p in enumerate(parts) for s in [of_micro(p[0], m)] + [all_of(a) for a in p[1:]]]
    shape = (2, PART // LANES * (width // UNIT // 2), 2 * width // PART * UNIT, LANES)
    return pl.pallas_call(
        functools.partial(wgrad_qo_kernel, count=count),
        grid=(1,),
        in_specs=specs,
        out_shape=jax.ShapeDtypeStruct(shape, bf16),
        compiler_params=params(),
        cost_estimate=pl.CostEstimate(
            flops=4 * count * rows * width * width,
            bytes_accessed=6 * width * width,
            transcendentals=0,
        ),
        name="wgrad_qo",
    )(*[a for p in parts for a in p])


def wgrad_kv_kernel(core_ref, *refs, count):
    ins, (qo_ref, give_ref, keep_ref) = refs[: 5 * count], refs[5 * count :]
    t = pl.program_id(0)
    grad = 0.0
    for m in range(count):
        near, far, normed, dkv, _ = ins[5 * m : 5 * m + 5]
        half, rows = near.shape[0], normed.shape[0]
        grad = grad + dot_tn(near[...], dkv[:half]) + dot_tn(far[...], dkv[half : 2 * half])
        grad = grad + dot_tn(normed[rows - CLEN :], dkv[2 * half :])

    def fill(cores):
        each = grad.shape[0] // UNIT // 2
        rows = pl.ds(pl.multiple_of(t * UNIT, 16), UNIT)
        for j, c, k, unit in units(grad):
            cores[c][(2 * j + 1) * each + k, rows, :] = unit
        for c, ref in enumerate(cores):
            for j in range(PART // LANES):
                ref[2 * j * each : (2 * j + 1) * each, rows, :] = qo_ref[c, j * each : (j + 1) * each]

        @pl.when(t == 0)
        def _():
            small = sum(ins[5 * m + 4][...] for m in range(count)).astype(bf16)
            for ref in cores:
                ref[:, 3 * UNIT :, :] = jnp.zeros((ref.shape[0], PACK - 3 * UNIT, LANES), bf16)
            for i in range(small.shape[1] // LANES):
                block = small[:, i * LANES : (i + 1) * LANES]
                ref, chunk = cores[i // 3], i % 3 * 2 * each
                ref[chunk, 3 * UNIT : 3 * UNIT + 16, :] = block[:16]
                ref[chunk + 1, 3 * UNIT : 3 * UNIT + 8, :] = block[16:24]

    @pl.when(core_ref[0] == 0)
    def _():
        fill((keep_ref, give_ref))

    @pl.when(core_ref[0] != 0)
    def _():
        fill((give_ref, keep_ref))


def wgrad_kv(core, qo, parts):
    rows, width = parts[0][2].shape[1:]
    half = parts[0][0].shape[0]
    whole = lambda n: pl.BlockSpec((n, width), lambda t, c: (0, 0))
    specs, args = [], []
    for m, p in enumerate(parts):
        specs += [
            whole(half), whole(half),
            pl.BlockSpec((None, rows, width), lambda t, c, m=m: (m, 0, 0)),
            pl.BlockSpec((2 * half + CLEN, PART), lambda t, c: (0, t)), whole(24),
        ]
        args += list(p)
    count = len(parts)
    specs.append(pl.BlockSpec(qo.shape[:2] + (UNIT, LANES), lambda t, c: (0, 0, t, 0)))
    shape = (2 * qo.shape[1], PACK, LANES)
    return pl.pallas_call(
        functools.partial(wgrad_kv_kernel, count=count),
        grid_spec=pltpu.PrefetchScalarGridSpec(
            num_scalar_prefetch=1,
            grid=(2 * width // PART,),
            in_specs=specs,
            out_specs=[pl.BlockSpec(shape, lambda t, c: (0, 0, 0))] * 2,
        ),
        out_shape=[jax.ShapeDtypeStruct(shape, bf16)] * 2,
        compiler_params=params(),
        cost_estimate=pl.CostEstimate(
            flops=4 * count * (2 * half + CLEN) * width * width,
            bytes_accessed=12 * count * half * width,
            transcendentals=0,
        ),
        name="wgrad_kv",
    )(core, *args, qo)


def unpack_rows(part_ref, weights, query, key, value, out):
    rows = query.shape[0]
    each = rows // UNIT
    cols = PART // 2 // LANES
    for first, refs in ((0, (query, out)), (each, (key, value))):
        for j in range(2 * cols):
            ref, at = refs[j // cols], (j % cols) * LANES
            for k in range(each):
                ref[k * UNIT : (k + 1) * UNIT, at : at + LANES] = part_ref[
                    2 * j * each + first + k
                ].astype(f32)
    total = 0.0
    for grad, w_ref in zip((query, key, value), weights):
        prod = grad[...] * w_ref[...].astype(f32)
        total = total + sum(prod[:, i * LANES : (i + 1) * LANES] for i in range(cols))
    high, low = halves(total)
    ones = jnp.ones((8, LANES), bf16)
    return dot_nt(ones, high) + dot_nt(ones, low)


def unpack_mine_kernel(core_ref, part_ref, wq_ref, wk_ref, wv_ref, query, key, value, out, sums):
    total = unpack_rows(part_ref, (wq_ref, wk_ref, wv_ref), query, key, value, out)

    @pl.when(pl.program_id(0) == 0)
    def _():
        sums[...] = total

    @pl.when(pl.program_id(0) > 0)
    def _():
        sums[...] += total


def unpack_other_kernel(
    core_ref, part_ref, wq_ref, wk_ref, wv_ref, gain_ref, mine_sums, mine_tail, other_tail, *rest
):
    query, key, value, out, norm_gain, ffn_gain, router, const, const_vec, sums = rest[-10:]
    step = pl.program_id(0)
    total = unpack_rows(part_ref, (wq_ref, wk_ref, wv_ref), query, key, value, out)

    @pl.when(step == 0)
    def _():
        sums[...] = total

    @pl.when(step > 0)
    def _():
        sums[...] += total

    def finish(parts, tails):
        rows = sums.shape[1]
        each = rows // UNIT
        for c, part in enumerate(parts):
            at = slice(c * rows, (c + 1) * rows)
            norm_gain[at] = (part[0:1, :] / gain_ref[:, at])[0]
        for i in range(2 * rows // LANES):
            at = slice(i * LANES, (i + 1) * LANES)
            chunk = i % 3 * 2 * each
            small = tails[i // 3][chunk].astype(f32)
            rest = tails[i // 3][chunk + 1].astype(f32)
            router[:, at] = small[:TARGETS]
            for c in range(CONSTS):
                const[c, :, at] = small[TARGETS + 2 * c : TARGETS + 2 * c + 2]
            const_vec[:, at] = rest[:CONSTS]
            ffn_gain[at] = rest[CONSTS]

    last = step == pl.num_programs(0) - 1

    @pl.when(last & (core_ref[0] == 0))
    def _():
        finish((mine_sums, sums), (mine_tail, other_tail))

    @pl.when(last & (core_ref[0] != 0))
    def _():
        finish((sums, mine_sums), (other_tail, mine_tail))


def unpack(core, mine, swap, gain, w_query, w_key, w_value):
    width = w_query.shape[0]
    chunks = mine.shape[0]
    half = width // 2
    other = swap(mine)
    body = pl.BlockSpec((chunks, UNIT, LANES), lambda t, c: (0, t, 0))
    tail = pl.BlockSpec((chunks, PACK - 3 * UNIT, LANES), lambda t, c: (0, 3 * UNIT // (PACK - 3 * UNIT), 0))
    whole = lambda s: pl.BlockSpec(s, lambda t, c: (0,) * len(s))
    block = (half, PART // 2)
    by_core = lambda f: pl.BlockSpec(block, lambda t, c: (f(c[0]), t))
    grid = (2 * width // PART,)
    dense = [jax.ShapeDtypeStruct((width, width), f32)] * 4
    cost = pl.CostEstimate(
        flops=2 * width * width, bytes_accessed=12 * width * width, transcendentals=0
    )
    first = by_core(lambda c: c)
    *mats, sums = pl.pallas_call(
        unpack_mine_kernel,
        grid_spec=pltpu.PrefetchScalarGridSpec(
            num_scalar_prefetch=1,
            grid=grid,
            in_specs=[body, first, first, first],
            out_specs=[first] * 4 + [whole((8, half))],
        ),
        out_shape=dense + [jax.ShapeDtypeStruct((8, half), f32)],
        compiler_params=params(),
        cost_estimate=cost,
        name="unpack_mine",
    )(core, mine, w_query, w_key, w_value)
    second = by_core(lambda c: 1 - c)
    small = [(width,), (width,), (TARGETS, width), (CONSTS, 2, width), (CONSTS, width)]
    args = (core, other, w_query, w_key, w_value, gain, sums, mine, other)
    return pl.pallas_call(
        unpack_other_kernel,
        grid_spec=pltpu.PrefetchScalarGridSpec(
            num_scalar_prefetch=1,
            grid=grid,
            in_specs=[body, second, second, second, whole((1, width)), whole((8, half)), tail, tail]
            + [pl.BlockSpec(memory_space=pl.ANY)] * 4,
            out_specs=[second] * 4 + [whole(s) for s in small],
            scratch_shapes=[pltpu.VMEM((8, half), f32)],
        ),
        out_shape=dense + [jax.ShapeDtypeStruct(s, f32) for s in small],
        input_output_aliases={len(args) + i: i for i in range(4)},
        compiler_params=params(),
        cost_estimate=cost,
        name="unpack_other",
    )(*args, *mats)


def token_grad_kernel(x_ref, gain_ref, mine_ref, rtot_ref, *rest):
    parts, out_ref = rest[:-1], rest[-1]
    prompt = parts[0].shape[0]
    x = x_ref[...].astype(f32)
    scale = lax.rsqrt(jnp.mean(x * x, axis=1, keepdims=True) + norm_eps)
    mine = mine_ref[...]
    total = sum(p[...].astype(f32) for p in parts)
    grad = jnp.concatenate([mine[:prompt] + total, mine[prompt:]], axis=0) * gain_ref[...]
    xhat = x * scale
    grad = scale * (grad - xhat * jnp.mean(grad * xhat, axis=1, keepdims=True))
    out_ref[...] = (rtot_ref[...] + grad).astype(bf16)


def token_grad(x, gain, mine, rtot, parts):
    of_micro = lambda a: pl.BlockSpec((None,) + a.shape[1:], lambda m: (m, 0, 0))
    return pl.pallas_call(
        token_grad_kernel,
        grid=(x.shape[0],),
        in_specs=[of_micro(x), pl.BlockSpec(gain.shape, lambda m: (0, 0)), of_micro(mine), of_micro(rtot)]
        + [of_micro(p) for p in parts],
        out_specs=of_micro(x),
        out_shape=jax.ShapeDtypeStruct(x.shape, bf16),
        compiler_params=params(),
        cost_estimate=pl.CostEstimate(
            flops=16 * x.size, bytes_accessed=14 * x.size, transcendentals=0
        ),
        name="token_grad",
    )(x, gain, mine, rtot, *parts)


def swap_cores(rows):
    return lax.ppermute(rows, "core", [(0, 1), (1, 0)])


def exchange(blocks, axes):
    return lax.all_to_all(blocks, axes, split_axis=0, concat_axis=0, tiled=True)


def spread_out(piece, axes):
    count = lax.axis_size(axes)
    return exchange(jnp.broadcast_to(piece[None], (count,) + piece.shape), axes)


def ring_parts(parts, axis, dim):
    count = lax.axis_size(axis)
    me = lax.axis_index(axis)
    part = lambda i: lax.dynamic_index_in_dim(parts, i, dim, keepdims=False)
    out = [part(me)]
    for step in range(1, count):
        ring = [(i, (i + step) % count) for i in range(count)]
        out.append(lax.ppermute(part((me + step) % count), axis, ring))
    return out


def after(value, *others):
    return lax.optimization_barrier((value, *others))[0]


def on_device(
    tokens, prior_logits, routes, drops, cont_lengths, norm_gain, w_query, w_key, w_value, w_out,
    ffn_gain, w_router, w_const, const_vec, w_gate, w_up, w_down, out_grad,
):
    micros, rows, width = tokens.shape[0], tokens.shape[3], tokens.shape[4]
    prompt = rows - CLEN
    cap = -(-(rows * 3 // 16) // 8) * 8
    chips = (lax.axis_size("context"), lax.axis_size("z"))
    half = chips[0] * chips[1] * prompt
    core = lax.axis_index("core").astype(jnp.int32)
    base = jnp.stack([lax.axis_index(("context", "z", "core")).astype(jnp.int32) * prompt, core])
    score_scale = 1.0 / math.sqrt(HEAD_SIZE)
    gain_one = norm_gain.astype(f32)
    gain_two = ffn_gain.astype(f32).reshape(1, width)

    gain_row = gain_one.reshape(1, width)
    core_arg = core.reshape(1)
    x = tokens[:, 0, 0]
    normed, copies, own_rows = first_norm(x, gain_row, chips[0] * chips[1])
    gathered = [exchange(copies, CHIPS)]
    for m in range(1, micros):
        gathered.append(lax.all_gather(own_rows[m * prompt : (m + 1) * prompt], CHIPS, axis=0))

    wr = jnp.concatenate(
        [w_router] + [w_const[j] for j in range(CONSTS)]
        + [jnp.zeros((width, LANES - TARGETS - 2 * CONSTS), bf16)], axis=1,
    )
    cv = jnp.zeros((LANES, width), bf16).at[EXPERTS + 2 : EXPERTS + 2 + CONSTS].set(const_vec)
    wide = QUAD * HEAD_SIZE
    w_kv = jnp.concatenate(
        [w[:, g * wide : (g + 1) * wide] for g in range(HEADS // QUAD) for w in (w_key, w_value)], axis=1
    )
    row_ids = jnp.arange(rows, dtype=jnp.int32)
    og = out_grad[:, 0, 0]
    live = row_ids[None] < prompt + cont_lengths[:, 0]
    active = (1 - drops[:, 0, 0]) * live[..., None].astype(jnp.int32)
    eff = jnp.where(active > 0, routes[:, 0, 0], -1)
    efft = jnp.swapaxes(eff, 1, 2)
    prior = jnp.pad(prior_logits[:, 0, 0], ((0, 0), (0, 0), (0, LANES - TARGETS)))

    st = []
    for m in range(micros):
        s = {}
        if m:
            gathered[m] = after(gathered[m], st[m - 1]["attn"])
        else:
            gathered[m] = after(gathered[m], w_kv, wr, cv, eff, efft, prior, base, core_arg, gain_row, gain_two)
        s["near"] = gathered[m].reshape(half, width)
        s["far"] = swap_cores(s["near"])
        (
            s["attn"], s["lse"], s["q"], s["kv"],
            s["resid"], s["two"], s["ch"], send, s["sel"], s["selt"], s["gate"],
        ) = attn_fwd(
            base, normed, s["near"], s["far"], w_query, w_kv,
            x, w_out, gain_two, wr, prior, eff, efft, og, chips, cap, m,
        )
        s["recv"] = exchange(send.reshape(EXPERTS, cap, 2 * width), EXPERT).reshape(
            EXPERTS * cap, 2 * width
        )
        st.append(s)
    for s in st:
        ret, s["hid"], s["gg"], s["ug"] = experts(s["recv"], w_gate, w_up, w_down)
        s["ret"] = exchange(ret.reshape(EXPERTS, cap, 2 * width), EXPERT).reshape(
            EXPERTS * cap, 2 * width
        )
    wide_grads = expert_wgrad([(s["recv"], s["hid"], s["gg"], s["ug"]) for s in st])
    for m in range(micros - 1):
        st[m]["ret"] = after(st[m]["ret"], wide_grads, st[m + 1]["ret"])
    wide_sum = lax.psum(tuple(wide_grads), ("dp", "context"))

    kv_parts, qo_parts, back_parts, before = [], [], [], ()
    for m, s in enumerate(st):
        dq, dkv, mixed, rtot, branch, dl, small = attn_bwd(
            base, s["q"], s["kv"], s["attn"], s["lse"],
            s["resid"], s["two"], s["ch"], eff, og, s["ret"], s["sel"], s["selt"], s["gate"],
            w_out, gain_two, wr, cv, chips, cap, m, before,
        )
        before = (mixed, rtot, dl)
        kv_parts.append((s["near"], s["far"], normed, dkv, small))
        qo_parts.append((normed, dq, s["attn"], branch))
        back_parts.append((dq, dkv))
    qo = wgrad_qo(qo_parts)
    give, keep = wgrad_kv(core_arg, qo, kv_parts)
    dkvs = [dkv for _, dkv in back_parts]
    dkvs[0] = after(dkvs[0], give)
    give_rows = back_proj(dkvs, w_kv, 1)
    come = after(swap_cores(give), give_rows)
    keep = (keep.astype(f32) + come.astype(f32)).astype(bf16)
    dense = exchange(keep.reshape((lax.axis_size(FIRST), -1) + keep.shape[1:]), FIRST)
    come = swap_cores(give_rows)
    keep = back_proj(dkvs, w_kv, 0)
    rows_sum = (keep.astype(f32) + come.astype(f32)).astype(bf16)
    dense = after(dense, rows_sum)
    rows_sum = rows_sum.reshape(micros, chips[1], chips[0] * prompt, width)
    rows_sum = sum(p.astype(f32) for p in ring_parts(rows_sum, "z", 1)).astype(bf16)
    mine = own_proj(back_parts, w_query, w_kv)
    dense = after(jnp.sum(dense.astype(f32), axis=0).astype(bf16), mine)
    dense = jnp.sum(exchange(dense, REST).astype(f32), axis=0).astype(bf16)
    dense = after(dense, wide_sum, rows_sum)
    dense = spread_out(dense, ALL_CHIPS)
    wide_out = [g.astype(f32)[None] for g in wide_sum]
    prior_grad = dl[:, :, :TARGETS]
    rows_sum = after(rows_sum, wide_out, prior_grad)
    parts = ring_parts(rows_sum.reshape(micros, chips[0], prompt, width), "context", 1)
    x_grad = token_grad(x, gain_row, mine, rtot, parts)
    dense = after(dense, parts)
    query, key, value, out, norm_gain, ffn_gain, router, const, vec = unpack(
        core_arg, dense, swap_cores, gain_row, w_query, w_key, w_value
    )
    return (
        mixed[:, None, None],
        x_grad[:, None, None],
        prior_grad[:, None, None],
        norm_gain,
        query,
        key,
        value,
        out,
        ffn_gain,
        router.T,
        jnp.swapaxes(const, 1, 2),
        vec,
        *wide_out,
    )


def solution(mesh):
    shape = mesh.devices.shape
    split = Mesh(
        mesh.devices.reshape(shape[0], shape[1], shape[2] // 2, 2), ("dp", "context", "z", "core")
    )
    slot = P(None, "dp", ("context", "z", "core"), None, None)
    expert = P(("z", "core"), None, None)
    return jax.shard_map(
        on_device,
        mesh=split,
        in_specs=(
            slot, slot, slot, slot, P(None, "dp", ("context", "z", "core")),
            *(P(),) * 9,
            *(expert,) * 3,
            slot,
        ),
        out_specs=(slot, slot, slot, *(P(),) * 9, *(expert,) * 3),
        check_vma=False,
    )
```

```python
import functools
import math

import jax
import jax.numpy as jnp
from jax import lax
from jax.experimental import pallas as pl
from jax.experimental.pallas import tpu as pltpu
from jax.sharding import Mesh, PartitionSpec as P

HEADS = 12
HEAD_SIZE = 64
EXPERTS = 8
CONSTS = 2
TARGETS = 12
CLEN = 128
QUAD = 4
LANES = 128

norm_eps = 1e-05
very_low = -1e30
highest = lax.Precision.HIGHEST
f32 = jnp.float32
bf16 = jnp.bfloat16
CHIPS = ("z", "context")
FIRST, REST = "z", ("dp", "context")
ALL_CHIPS = (FIRST,) + REST
EXPERT = ("z", "core")


def dot_nn(left, right, **kw):
    return jnp.dot(left, right, preferred_element_type=f32, **kw)


def dot_nt(left, right, **kw):
    return lax.dot_general(left, right, (((1,), (1,)), ((), ())), preferred_element_type=f32, **kw)


def dot_tn(left, right, **kw):
    return lax.dot_general(left, right, (((0,), (0,)), ((), ())), preferred_element_type=f32, **kw)


def halves(wide):
    high = wide.astype(bf16)
    return high, (wide - high.astype(f32)).astype(bf16)


def iota(shape, dim):
    return lax.broadcasted_iota(jnp.int32, shape, dim)


def params():
    return pltpu.CompilerParams(vmem_limit_bytes=63_400_000)


def head_masks(dtype):
    lane_head = iota((1, QUAD * HEAD_SIZE), 1) // HEAD_SIZE
    return [(lane_head == h).astype(f32).astype(dtype) for h in range(QUAD)]


def spread(rows, prompt, dtype):
    masks = head_masks(dtype)
    return jnp.concatenate(
        [rows[:prompt] * m for m in masks] + [rows[prompt:] * m for m in masks], axis=0
    )


def gather_heads(stacked, prompt, dtype):
    masks = head_masks(dtype)
    top, low = 0.0, 0.0
    first = QUAD * prompt
    for h in range(QUAD):
        top = top + stacked[h * prompt : (h + 1) * prompt] * masks[h]
        low = low + stacked[first + h * CLEN : first + (h + 1) * CLEN] * masks[h]
    return jnp.concatenate([top, low], axis=0)


def first_norm_kernel(x_ref, gain_ref, normed_ref, copies_ref, *prompt_refs):
    x = x_ref[...].astype(f32)
    scale = lax.rsqrt(jnp.mean(x * x, axis=1, keepdims=True) + norm_eps)
    normed = (x * scale * gain_ref[...].astype(f32).reshape(1, -1)).astype(bf16)
    normed_ref[...] = normed
    micro = pl.program_id(0)
    prompt = copies_ref.shape[1]

    @pl.when(micro == 0)
    def _():
        for i in range(copies_ref.shape[0]):
            copies_ref[i] = normed[:prompt]

    for m, ref in enumerate(prompt_refs):

        @pl.when(micro == m + 1)
        def _():
            ref[...] = normed[:prompt]


def first_norm(x, gain, copies):
    micros, rows, width = x.shape
    of_micro = pl.BlockSpec((None, rows, width), lambda m: (m, 0, 0))
    shapes = [(copies, rows - CLEN, width)] + [(rows - CLEN, width)] * (micros - 1)
    whole = lambda s: pl.BlockSpec(s, lambda m: (0,) * len(s))
    return pl.pallas_call(
        first_norm_kernel,
        grid=(micros,),
        in_specs=[of_micro, whole((width,))],
        out_specs=[of_micro] + [whole(s) for s in shapes],
        out_shape=[jax.ShapeDtypeStruct(s, bf16) for s in [x.shape] + shapes],
        compiler_params=params(),
        cost_estimate=pl.CostEstimate(
            flops=8 * micros * rows * width, bytes_accessed=4 * micros * rows * width, transcendentals=0
        ),
        name="first_norm",
    )(x, gain)


def key_places(core, keys, prompt, chips, j):
    half = keys // 2
    other = jnp.where(j >= half, 1, 0)
    chip = (j - other * half) // prompt
    chip = (chip % chips[0]) * chips[1] + chip // chips[0]
    slot = chip * 2 + jnp.where(other > 0, 1 - core, core)
    return slot * prompt + (j & (prompt - 1))


def attn_fwd_kernel(
    base_ref, normed_ref, near_ref, far_ref, wq_ref, wkv_ref,
    x_ref, wout_ref, gain_ref, wr_ref, prior_ref, eff_ref, efft_ref, og_ref,
    o_ref, lse_ref, q_ref, kv_ref,
    resid_ref, two_ref, ch_ref, send_ref, sel_ref, selt_ref, gate_ref, o_all,
    *, chips, cap,
):
    g = pl.program_id(0)
    prompt = q_ref.shape[0] - CLEN
    keys = kv_ref.shape[0] - CLEN
    half = keys // 2
    wide = QUAD * HEAD_SIZE
    masks = head_masks(bf16)
    masks_f = head_masks(f32)
    ones = jnp.ones((8, LANES), f32)

    def to_row(column):
        spare = jnp.where(iota((column.shape[0], LANES), 1) == 0, column, 0.0)
        return dot_nt(ones, spare, precision=highest)

    q = dot_nn(normed_ref[...], wq_ref[...]).astype(bf16).astype(f32)
    q_ref[...] = (q * (1.0 / math.sqrt(HEAD_SIZE))).astype(bf16)
    for rows, at in ((near_ref, 0), (far_ref, half)):
        kv_ref[at : at + half] = dot_nn(rows[...], wkv_ref[...]).astype(bf16)
    kv_ref[keys:] = dot_nn(normed_ref[prompt:], wkv_ref[...]).astype(bf16)
    q_top, q_low = q_ref[:prompt], q_ref[prompt:]
    q_p = jnp.concatenate([q_top * m for m in masks], axis=0)
    s = dot_nt(q_p, kv_ref[:keys, :wide])
    limit = base_ref[0] + (iota((QUAD * prompt, 1), 0) & (prompt - 1))
    s = jnp.where(key_places(base_ref[1], keys, prompt, chips, iota((1, keys), 1)) <= limit, s, very_low)
    top = jnp.max(s, axis=1, keepdims=True)
    p = jnp.exp(s - top)
    total = jnp.sum(p, axis=1, keepdims=True)
    out = dot_nn(p.astype(bf16), kv_ref[:keys, wide:]) * (1.0 / total)
    lse_ref[:, : QUAD * prompt] = to_row(top + jnp.log(total))
    top_out = sum(out[h * prompt : (h + 1) * prompt] * masks_f[h] for h in range(QUAD))
    low_out = 0.0
    per = 2
    for part in range(QUAD // per):
        hs = range(part * per, (part + 1) * per)
        rows = per * CLEN
        q_c = jnp.concatenate([q_low * masks[h] for h in hs], axis=0)
        s = dot_nt(q_c, kv_ref[:keys, :wide])
        own = dot_nt(q_c, kv_ref[keys:, :wide])
        own = jnp.where(
            iota((1, CLEN), 1) <= (iota((rows, 1), 0) & (CLEN - 1)), own, very_low
        )
        top = jnp.maximum(
            jnp.max(s, axis=1, keepdims=True), jnp.max(own, axis=1, keepdims=True)
        )
        p = jnp.exp(s - top)
        p_own = jnp.exp(own - top)
        total = jnp.sum(p, axis=1, keepdims=True) + jnp.sum(p_own, axis=1, keepdims=True)
        out = dot_nn(p.astype(bf16), kv_ref[:keys, wide:])
        out = out + dot_nn(p_own.astype(bf16), kv_ref[keys:, wide:])
        out = out * (1.0 / total)
        at = QUAD * prompt + part * rows
        lse_ref[:, at : at + rows] = to_row(top + jnp.log(total))
        for i, h in enumerate(hs):
            low_out = low_out + out[i * CLEN : (i + 1) * CLEN] * masks_f[h]
    attn = jnp.concatenate([top_out, low_out], axis=0)
    o_ref[...] = attn
    o_all[g] = attn.astype(bf16)

    @pl.when(g == o_all.shape[0] - 1)
    def _():
        attended = jnp.concatenate([o_all[i] for i in range(o_all.shape[0])], axis=1)
        route(
            attended, x_ref, wout_ref, gain_ref, wr_ref, prior_ref, eff_ref, efft_ref, og_ref,
            resid_ref, two_ref, ch_ref, send_ref, sel_ref, selt_ref, gate_ref, cap,
        )


def attn_fwd(
    base, normed, near, far, w_query, w_kv, x, w_out, gain, wr, prior, eff, efft, og,
    chips, cap, micro,
):
    rows, width = normed.shape[1:]
    half = near.shape[0]
    every = 2 * half + CLEN
    quads = HEADS // QUAD
    wide = QUAD * HEAD_SIZE
    slots = EXPERTS * cap
    col = lambda n, w=wide: pl.BlockSpec((n, w), lambda g, b: (0, g))
    whole = lambda n, w=width: pl.BlockSpec((n, w), lambda g, b: (0, 0))
    of_micro = lambda a: pl.BlockSpec((None,) + a.shape[1:], lambda g, b: (micro, 0, 0))
    routed = [
        ((rows, width), f32), ((rows, width), bf16), ((rows, LANES), f32), ((slots, 2 * width), bf16),
        ((slots, rows), bf16), ((rows, slots), bf16), ((slots, LANES), f32),
    ]
    return pl.pallas_call(
        functools.partial(attn_fwd_kernel, chips=chips, cap=cap),
        grid_spec=pltpu.PrefetchScalarGridSpec(
            num_scalar_prefetch=1,
            grid=(quads,),
            in_specs=[
                of_micro(normed), whole(half), whole(half), col(width), col(width, 2 * wide),
                of_micro(x), whole(width), whole(1), whole(width, LANES), of_micro(prior),
                of_micro(eff), of_micro(efft), of_micro(og),
            ],
            out_specs=[
                col(rows),
                pl.BlockSpec((None, 8, QUAD * rows), lambda g, b: (g, 0, 0)),
                col(rows),
                col(every, 2 * wide),
            ]
            + [whole(*s) for s, _ in routed],
            scratch_shapes=[pltpu.VMEM((quads, rows, wide), bf16)],
        ),
        out_shape=[
            jax.ShapeDtypeStruct((rows, width), f32),
            jax.ShapeDtypeStruct((quads, 8, QUAD * rows), f32),
            jax.ShapeDtypeStruct((rows, width), bf16),
            jax.ShapeDtypeStruct((every, 2 * width), bf16),
        ]
        + [jax.ShapeDtypeStruct(s, t) for s, t in routed],
        compiler_params=params(),
        cost_estimate=pl.CostEstimate(
            flops=16 * rows * every * width + 4 * every * width * width,
            bytes_accessed=4 * every * width,
            transcendentals=rows * every * HEADS,
        ),
        name="attn_fwd",
    )(base, normed, near, far, w_query, w_kv, x, w_out, gain, wr, prior, eff, efft, og)


def attn_bwd_kernel(
    base_ref, q_ref, kv_ref, o_ref, lse_ref,
    resid_ref, two_ref, ch_ref, eff_ref, og_ref, ret_ref, sel_ref, selt_ref, gate_ref,
    wout_ref, gain_ref, wr_ref, cv_ref, *rest, block, chips, cap
):
    (
        dq_ref, dkv_ref, mixed_ref, rtot_ref, branch_ref, dl_ref, small_ref, qm, dom, dqt, do_all
    ) = rest[-11:]
    g = pl.program_id(0)
    quads = do_all.shape[0]

    @pl.when(g == 0)
    def _():
        grad = combine(
            resid_ref, two_ref, ch_ref, eff_ref, og_ref, ret_ref, sel_ref, selt_ref, gate_ref,
            wout_ref, gain_ref, wr_ref, cv_ref,
            mixed_ref, rtot_ref, branch_ref, dl_ref, small_ref, cap,
        )
        for i in range(quads):
            do_all[i] = grad[:, i * QUAD * HEAD_SIZE : (i + 1) * QUAD * HEAD_SIZE]

    do_now = do_all[g]
    prompt = q_ref.shape[0] - CLEN
    keys = kv_ref.shape[0] - CLEN
    wide = QUAD * HEAD_SIZE
    qm[...] = spread(q_ref[...], prompt, bf16)
    dom[...] = spread(do_now, prompt, bf16)
    prod = spread(do_now.astype(f32) * o_ref[...], prompt, f32)
    ones = jnp.ones((8, prod.shape[1]), bf16)
    prod_high, prod_low = halves(prod)
    delta = (dot_nt(ones, prod_high) + dot_nt(ones, prod_low))[0:1]
    lse = lse_ref[0:1, :]
    first = QUAD * prompt
    ahead = (iota((prompt, first), 1) & (prompt - 1)) - iota((prompt, first), 0)
    q_all, do_all = qm[...], dom[...]

    def one(rows, mask):
        kk, vv = kv_ref[rows, :wide], kv_ref[rows, wide:]
        p = jnp.exp(dot_nt(kk, q_all) - lse)
        p = mask(p)
        ds = p * (dot_nt(vv, do_all) - delta)
        pb, dsb = p.astype(bf16), ds.astype(bf16)
        dkv_ref[rows, :wide] = dot_nn(dsb, q_all).astype(bf16)
        dkv_ref[rows, wide:] = dot_nn(pb, do_all).astype(bf16)
        return dot_tn(kk, dsb)

    def own_mask(p):
        lane = iota((1, p.shape[1]), 1)
        own_row = jnp.where(lane < first, -1, (lane - first) & (CLEN - 1))
        return jnp.where(iota((CLEN, 1), 0) <= own_row, p, 0.0)

    dqt[...] = one(pl.ds(keys, CLEN), own_mask)

    def step(i, unused):
        at = i * block

        def mask(p):
            rows = []
            for r in range(0, block, prompt):
                gap = key_places(base_ref[1], keys, prompt, chips, at + r) - base_ref[0]
                rows.append(jnp.where(ahead >= gap, p[r : r + prompt, :first], 0.0))
            return jnp.concatenate([jnp.concatenate(rows, axis=0), p[:, first:]], axis=1)

        dqt[...] += one(pl.ds(at, block), mask)
        return unused

    for i in range(keys // block):
        step(i, 0)
    dq = gather_heads(dqt[...].T, prompt, f32)
    dq = (dq * (1.0 / math.sqrt(HEAD_SIZE))).astype(bf16)
    dq_ref[...] = dq


def attn_bwd(
    base, q, kv, o, lse, resid, two, ch, eff, og, ret, sel, selt, gate, w_out, gain, wr, cv,
    chips, cap, micro, before, block=1024,
):
    rows, width = q.shape
    every = kv.shape[0]
    quads = HEADS // QUAD
    wide = QUAD * HEAD_SIZE
    micros = eff.shape[0]
    col = lambda n, w=wide: pl.BlockSpec((n, w), lambda g, b: (0, g))
    whole = lambda a: pl.BlockSpec(a.shape, lambda g, b: (0, 0))
    of_micro = lambda a: pl.BlockSpec((None,) + a.shape[1:], lambda g, b: (micro, 0, 0))
    mixing = [
        jax.ShapeDtypeStruct((micros, rows, width), bf16),
        jax.ShapeDtypeStruct((micros, rows, width), f32),
        jax.ShapeDtypeStruct((rows, width), bf16),
        jax.ShapeDtypeStruct((micros, rows, LANES), f32),
        jax.ShapeDtypeStruct((24, width), f32),
    ]
    args = (base, q, kv, o, lse, resid, two, ch, eff, og, ret, sel, selt, gate, w_out, gain, wr, cv)
    return pl.pallas_call(
        functools.partial(
            attn_bwd_kernel, block=min(block, (every - CLEN) // 2), chips=chips, cap=cap
        ),
        grid_spec=pltpu.PrefetchScalarGridSpec(
            num_scalar_prefetch=1,
            grid=(quads,),
            in_specs=[
                col(rows), col(every, 2 * wide), col(rows),
                pl.BlockSpec((None, 8, QUAD * rows), lambda g, b: (g, 0, 0)),
                whole(resid), whole(two), whole(ch), of_micro(eff), of_micro(og), whole(ret),
                whole(sel), whole(selt), whole(gate), whole(w_out), whole(gain), whole(wr), whole(cv),
            ]
            + [pl.BlockSpec(memory_space=pl.ANY) for _ in before],
            out_specs=[col(rows), col(every, 2 * wide)]
            + [of_micro(a) if len(a.shape) == 3 else whole(a) for a in mixing],
            scratch_shapes=[
                pltpu.VMEM((QUAD * rows, wide), bf16),
                pltpu.VMEM((QUAD * rows, wide), bf16),
                pltpu.VMEM((wide, QUAD * rows), f32),
                pltpu.VMEM((quads, rows, wide), bf16),
            ],
        ),
        out_shape=[
            jax.ShapeDtypeStruct((rows, width), bf16),
            jax.ShapeDtypeStruct((every, 2 * width), bf16),
        ]
        + mixing,
        input_output_aliases={len(args) + i: out for i, out in enumerate((2, 3, 5)[: len(before)])},
        compiler_params=params(),
        cost_estimate=pl.CostEstimate(
            flops=40 * rows * every * width,
            bytes_accessed=8 * every * width,
            transcendentals=rows * every * HEADS,
        ),
        name="attn_bwd",
    )(*args, *before)


def back_proj_kernel(*refs, count):
    ins, (w_ref, out_ref) = refs[:count], refs[count:]
    for m in range(count):

        @pl.when(pl.program_id(0) == m)
        def _():
            out_ref[...] = dot_nt(ins[m][...], w_ref[...]).astype(bf16)


def back_proj(dkvs, w_kv, which):
    count = len(dkvs)
    width = w_kv.shape[0]
    half = (dkvs[0].shape[0] - CLEN) // 2
    return pl.pallas_call(
        functools.partial(back_proj_kernel, count=count),
        grid=(count,),
        in_specs=[pl.BlockSpec((half, 2 * width), lambda t: (which, 0)) for _ in dkvs]
        + [pl.BlockSpec((width, 2 * width), lambda t: (0, 0))],
        out_specs=pl.BlockSpec((None, half, width), lambda t: (t, 0, 0)),
        out_shape=jax.ShapeDtypeStruct((count, half, width), bf16),
        compiler_params=params(),
        cost_estimate=pl.CostEstimate(
            flops=count * half * width * width, bytes_accessed=2 * count * half * width, transcendentals=0
        ),
        name="back_proj",
    )(*dkvs, w_kv)


def own_proj_kernel(*refs, count):
    ins, (wq_ref, wkv_ref, out_ref) = refs[: 2 * count], refs[2 * count :]
    for m in range(count):
        dq = dot_nt(ins[2 * m][...], wq_ref[...])
        prompt = dq.shape[0] - CLEN
        out_ref[m, :prompt] = dq[:prompt]
        out_ref[m, prompt:] = dq[prompt:] + dot_nt(ins[2 * m + 1][...], wkv_ref[...])


def own_proj(parts, w_query, w_kv):
    rows, width = parts[0][0].shape
    every = parts[0][1].shape[0]
    whole = lambda n, w=width: pl.BlockSpec((n, w), lambda i: (0, 0))
    tail = pl.BlockSpec((CLEN, 2 * width), lambda i: (every // CLEN - 1, 0))
    count = len(parts)
    return pl.pallas_call(
        functools.partial(own_proj_kernel, count=count),
        grid=(1,),
        in_specs=[whole(rows), tail] * count + [whole(width), whole(width, 2 * width)],
        out_shape=jax.ShapeDtypeStruct((count, rows, width), f32),
        compiler_params=params(),
        cost_estimate=pl.CostEstimate(
            flops=6 * count * rows * width * width, bytes_accessed=6 * width * width, transcendentals=0
        ),
        name="own_proj",
    )(*[a for p in parts for a in p], w_query, w_kv)


def route(
    attended, x_ref, wout_ref, gain_ref, wr_ref, prior_ref, eff_ref, efft_ref, og_ref,
    resid_ref, two_ref, ch_ref, send_ref, sel_ref, selt_ref, gate_ref, cap,
):
    rows, width = x_ref.shape
    slots = EXPERTS * cap
    resid = x_ref[...].astype(f32) + dot_nn(attended, wout_ref[...])
    resid_ref[...] = resid
    inv = lax.rsqrt(jnp.mean(resid * resid, axis=1, keepdims=True) + norm_eps)
    two = (resid * inv * gain_ref[...]).astype(bf16)
    two_ref[...] = two
    lane = iota((1, LANES), 1)
    logits = dot_nn(two, wr_ref[...]) + prior_ref[...]
    masked = jnp.where(lane < TARGETS, logits, very_low)
    e = jnp.exp(masked - jnp.max(masked, axis=1, keepdims=True))
    ch = e * (1.0 / jnp.sum(e, axis=1, keepdims=True))
    for j in range(CONSTS):
        at = TARGETS + 2 * j
        diff = logits[:, at + 1 : at + 2] - logits[:, at : at + 1]
        ch = jnp.where(lane == at, 1.0 / (1.0 + jnp.exp(diff)), ch)
        ch = jnp.where(lane == at + 1, 1.0 / (1.0 + jnp.exp(-diff)), ch)
    ch_ref[...] = ch
    target = iota((16, rows), 0)
    hot_t = ((target == efft_ref[0:1, :]) | (target == efft_ref[1:2, :])).astype(f32)
    before = (iota((rows, rows), 0) < iota((rows, rows), 1)).astype(f32).astype(bf16)
    rank_t = dot_nn(hot_t.astype(bf16), before)
    rank_t = jnp.where(hot_t > 0.0, rank_t, -1.0)
    place = iota((cap, 1), 0).astype(f32)
    sel = jnp.concatenate(
        [(place == rank_t[i : i + 1, :]).astype(f32) for i in range(EXPERTS)], axis=0
    )
    sel_b = sel.astype(bf16)
    sel_ref[...] = sel_b
    hot = ((lane == eff_ref[:, 0:1]) | (lane == eff_ref[:, 1:2])).astype(f32)
    after = (iota((rows, rows), 0) > iota((rows, rows), 1)).astype(f32).astype(bf16)
    rank = dot_nn(after, hot.astype(bf16))
    rank = jnp.where(hot > 0.0, rank, -1.0)
    slot = iota((1, slots), 1)
    widen = (slot // cap == iota((LANES, 1), 0)).astype(f32).astype(bf16)
    rank_s = dot_nn(rank.astype(bf16), widen)
    selt_ref[...] = (rank_s == (slot % cap).astype(f32)).astype(f32).astype(bf16)
    ch_high, ch_low = halves(ch)
    ch_s = dot_nn(sel_b, ch_high) + dot_nn(sel_b, ch_low)
    of_slot = iota((slots, 1), 0) // cap
    gate = jnp.sum(jnp.where(lane == of_slot, ch_s, 0.0), axis=1, keepdims=True)
    gate_ref[...] = jnp.broadcast_to(gate, gate_ref.shape)
    send_ref[:, :width] = dot_nn(sel_b, two).astype(bf16)
    send_ref[:, width:] = (gate * dot_nn(sel_b, og_ref[...])).astype(bf16)


def expert_kernel(
    x_ref, g_ref, wg_ref, wu_ref, wd_ref, out_ref, hid_ref, gg_ref, ug_ref, fwd, back
):
    step = pl.program_id(0)
    width = x_ref.shape[1]

    @pl.when(step == 0)
    def _():
        fwd[...] = jnp.zeros_like(fwd)
        back[...] = jnp.zeros_like(back)

    x, g = x_ref[...], g_ref[...]
    gate = dot_nn(x, wg_ref[...])
    up = dot_nn(x, wu_ref[...])
    hid_grad = dot_nt(g, wd_ref[...])
    sig = 1.0 / (1.0 + jnp.exp(-gate))
    act = gate * sig
    hid = (act * up).astype(bf16)
    gg = (hid_grad * up * (sig + act * (1.0 - sig))).astype(bf16)
    ug = (hid_grad * act).astype(bf16)
    hid_ref[...] = hid
    gg_ref[...] = gg
    ug_ref[...] = ug
    fwd[...] += dot_nn(hid, wd_ref[...])
    back[...] += dot_nt(gg, wg_ref[...]) + dot_nt(ug, wu_ref[...])

    @pl.when(step == pl.num_programs(0) - 1)
    def _():
        out_ref[:, :width] = fwd[...].astype(bf16)
        out_ref[:, width:] = back[...].astype(bf16)


def experts(rows_in, w_gate, w_up, w_down, tile=512):
    rows = rows_in.shape[0]
    width = rows_in.shape[1] // 2
    hidden = w_gate.shape[2]
    half = lambda i: pl.BlockSpec((rows, width), lambda t, i=i: (0, i))
    inner = pl.BlockSpec((None, width, tile), lambda t: (0, 0, t))
    mid = pl.BlockSpec((rows, tile), lambda t: (0, t))
    return pl.pallas_call(
        expert_kernel,
        grid=(hidden // tile,),
        in_specs=[half(0), half(1), inner, inner, pl.BlockSpec((None, tile, width), lambda t: (0, t, 0))],
        out_specs=[pl.BlockSpec((rows, 2 * width), lambda t: (0, 0)), mid, mid, mid],
        out_shape=[jax.ShapeDtypeStruct((rows, 2 * width), bf16)]
        + [jax.ShapeDtypeStruct((rows, hidden), bf16)] * 3,
        scratch_shapes=[pltpu.VMEM((rows, width), f32), pltpu.VMEM((rows, width), f32)],
        compiler_params=params(),
        cost_estimate=pl.CostEstimate(
            flops=14 * rows * width * hidden,
            bytes_accessed=6 * width * hidden,
            transcendentals=rows * hidden,
        ),
        name="experts",
    )(rows_in, rows_in, w_gate, w_up, w_down)


def expert_wgrad_kernel(*refs, count):
    ins, (dg_ref, du_ref, dd_ref) = refs[: 5 * count], refs[5 * count :]
    x, g, hid, gg, ug = (
        jnp.concatenate([ins[5 * m + i][...] for m in range(count)], axis=0) for i in range(5)
    )
    dg_ref[...] = dot_tn(x, gg).astype(bf16)
    du_ref[...] = dot_tn(x, ug).astype(bf16)
    dd_ref[...] = dot_tn(hid, g).astype(bf16)


def expert_wgrad(parts, tile=512):
    rows = parts[0][0].shape[0]
    width = parts[0][0].shape[1] // 2
    hidden = parts[0][1].shape[1]
    half = lambda i: pl.BlockSpec((rows, width), lambda t, i=i: (0, i))
    mid = pl.BlockSpec((rows, tile), lambda t: (0, t))
    specs, args = [], []
    for rows_in, hid, gg, ug in parts:
        specs += [half(0), half(1), mid, mid, mid]
        args += [rows_in, rows_in, hid, gg, ug]
    inner = pl.BlockSpec((width, tile), lambda t: (0, t))
    return pl.pallas_call(
        functools.partial(expert_wgrad_kernel, count=len(parts)),
        grid=(hidden // tile,),
        in_specs=specs,
        out_specs=[inner, inner, pl.BlockSpec((tile, width), lambda t: (t, 0))],
        out_shape=[
            jax.ShapeDtypeStruct((width, hidden), bf16),
            jax.ShapeDtypeStruct((width, hidden), bf16),
            jax.ShapeDtypeStruct((hidden, width), bf16),
        ],
        compiler_params=params(),
        cost_estimate=pl.CostEstimate(
            flops=6 * len(parts) * rows * width * hidden,
            bytes_accessed=6 * width * hidden,
            transcendentals=0,
        ),
        name="expert_wgrad",
    )(*args)


def combine(
    resid_ref, two_ref, ch_ref, eff_ref, og_ref, ret_ref, sel_ref, selt_ref, gate_ref,
    wout_ref, gain_ref, wr_ref, cv_ref,
    mixed_ref, rtot_ref, branch_ref, dl_ref, small_ref, cap,
):
    rows, width = resid_ref.shape
    slots = EXPERTS * cap
    lane = iota((1, LANES), 1)
    resid, two_b, ch = resid_ref[...], two_ref[...], ch_ref[...]
    two = two_b.astype(f32)
    og_b = og_ref[...]
    og = og_b.astype(f32)
    eo = ret_ref[:, :width].astype(f32)
    sel, selt = sel_ref[...], selt_ref[...]
    hot = ((lane == eff_ref[:, 0:1]) | (lane == eff_ref[:, 1:2])).astype(f32)
    dgate = jnp.sum(dot_nn(sel, og_b) * eo, axis=1, keepdims=True)
    by_target = jnp.where(lane == iota((slots, 1), 0) // cap, dgate, 0.0)
    by_high, by_low = halves(by_target)
    dval = dot_nn(selt, by_high) + dot_nn(selt, by_low)
    self_dot = jnp.sum(og * two, axis=1, keepdims=True)
    cv_dot = dot_nt(og_b, cv_ref[...])
    gates = ch * hot
    keep = gates[:, EXPERTS + 1 : EXPERTS + 2]
    dval = jnp.where(lane == EXPERTS + 1, self_dot, dval)
    mixed = resid + dot_nn(selt, (gate_ref[:, 0:1] * eo).astype(bf16))
    dl_const = jnp.zeros((rows, LANES), f32)
    coef_cv = jnp.zeros((rows, LANES), f32)
    for j in range(CONSTS):
        e, at = EXPERTS + 2 + j, TARGETS + 2 * j
        a0, a1 = ch[:, at : at + 1], ch[:, at + 1 : at + 2]
        gate = gates[:, e : e + 1]
        with_cv = cv_dot[:, e : e + 1]
        dval = jnp.where(lane == e, a0 * self_dot + a1 * with_cv, dval)
        keep = keep + gate * a0
        mixed = mixed + (gate * a1) * cv_ref[e : e + 1, :].astype(f32)
        coef_cv = jnp.where(lane == TARGETS + 2 * CONSTS + j, gate * a1, coef_cv)
        da0, da1 = gate * self_dot, gate * with_cv
        mean = a0 * da0 + a1 * da1
        dl_const = jnp.where(lane == at, a0 * (da0 - mean), dl_const)
        dl_const = jnp.where(lane == at + 1, a1 * (da1 - mean), dl_const)
    mixed = mixed + keep * two
    mixed_ref[...] = mixed.astype(bf16)
    ch = jnp.where(lane < TARGETS, ch, 0.0)
    dch = hot * dval
    dl = ch * (dch - jnp.sum(ch * dch, axis=1, keepdims=True)) + dl_const
    dl_ref[...] = dl
    dl_hi, dl_lo = halves(dl)
    cc_hi, cc_lo = halves(coef_cv)
    small = dot_tn(dl_hi, two_b) + dot_tn(dl_lo, two_b) + dot_tn(cc_hi, og_b) + dot_tn(cc_lo, og_b)
    two_grad = (
        keep * og
        + dot_nt(dl_hi, wr_ref[...])
        + dot_nt(dl_lo, wr_ref[...])
        + dot_nn(selt, ret_ref[:, width:])
    )
    inv = lax.rsqrt(jnp.mean(resid * resid, axis=1, keepdims=True) + norm_eps)
    xhat = resid * inv
    gain_grad = jnp.sum(two_grad * xhat, axis=0, keepdims=True)
    small_ref[...] = jnp.where(
        iota((small_ref.shape[0], 1), 0) == TARGETS + 3 * CONSTS, gain_grad, small[: small_ref.shape[0]]
    )
    scaled = two_grad * gain_ref[...]
    rtot = og + inv * (scaled - xhat * jnp.mean(scaled * xhat, axis=1, keepdims=True))
    rtot_ref[...] = rtot
    branch = rtot.astype(bf16)
    branch_ref[...] = branch
    return dot_nt(branch, wout_ref[...]).astype(bf16)


def of_micro(array, micro):
    return pl.BlockSpec((None,) + array.shape[1:], lambda i: (micro,) + (0,) * (array.ndim - 1))


def all_of(array):
    return pl.BlockSpec(array.shape, lambda i: (0,) * array.ndim)


UNIT = 48
PACK = 160
PART = 512


def units(grad):
    low = grad.astype(bf16)
    each = low.shape[0] // UNIT // 2
    for j in range(low.shape[1] // LANES):
        for k in range(2 * each):
            unit = low[k * UNIT : (k + 1) * UNIT, j * LANES : (j + 1) * LANES]
            yield j, k // each, k % each, unit


def wgrad_qo_kernel(*refs, count):
    ins, out_ref = refs[: 4 * count], refs[4 * count]
    stack = lambda i: jnp.concatenate([ins[4 * m + i][...] for m in range(count)], axis=0)
    normed, dq, attn, branch = (stack(i) for i in range(4))
    query = dot_tn(normed, dq)
    out = dot_tn(attn.astype(bf16), branch)
    half = PART // 2
    each = query.shape[0] // UNIT // 2
    for step in range(query.shape[1] // half):
        at = slice(step * half, (step + 1) * half)
        for j, c, k, unit in units(jnp.concatenate([query[:, at], out[:, at]], axis=1)):
            out_ref[c, j * each + k, step * UNIT : (step + 1) * UNIT, :] = unit


def wgrad_qo(parts):
    rows, width = parts[0][1].shape
    count = len(parts)
    specs = [s for m, p in enumerate(parts) for s in [of_micro(p[0], m)] + [all_of(a) for a in p[1:]]]
    shape = (2, PART // LANES * (width // UNIT // 2), 2 * width // PART * UNIT, LANES)
    return pl.pallas_call(
        functools.partial(wgrad_qo_kernel, count=count),
        grid=(1,),
        in_specs=specs,
        out_shape=jax.ShapeDtypeStruct(shape, bf16),
        compiler_params=params(),
        cost_estimate=pl.CostEstimate(
            flops=4 * count * rows * width * width,
            bytes_accessed=6 * width * width,
            transcendentals=0,
        ),
        name="wgrad_qo",
    )(*[a for p in parts for a in p])


def wgrad_kv_kernel(core_ref, *refs, count):
    ins, (qo_ref, give_ref, keep_ref) = refs[: 5 * count], refs[5 * count :]
    t = pl.program_id(0)
    grad = 0.0
    for m in range(count):
        near, far, normed, dkv, _ = ins[5 * m : 5 * m + 5]
        half, rows = near.shape[0], normed.shape[0]
        grad = grad + dot_tn(near[...], dkv[:half]) + dot_tn(far[...], dkv[half : 2 * half])
        grad = grad + dot_tn(normed[rows - CLEN :], dkv[2 * half :])

    def fill(cores):
        each = grad.shape[0] // UNIT // 2
        rows = pl.ds(pl.multiple_of(t * UNIT, 16), UNIT)
        for j, c, k, unit in units(grad):
            cores[c][(2 * j + 1) * each + k, rows, :] = unit
        for c, ref in enumerate(cores):
            for j in range(PART // LANES):
                ref[2 * j * each : (2 * j + 1) * each, rows, :] = qo_ref[c, j * each : (j + 1) * each]

        @pl.when(t == 0)
        def _():
            small = sum(ins[5 * m + 4][...] for m in range(count))
            small = jnp.concatenate([small, jnp.zeros((8, small.shape[1]), f32)], axis=0).astype(bf16)
            for ref in cores:
                ref[:, 3 * UNIT :, :] = jnp.zeros((ref.shape[0], PACK - 3 * UNIT, LANES), bf16)
            for i in range(small.shape[1] // LANES):
                block = small[:, i * LANES : (i + 1) * LANES]
                ref, chunk = cores[i // 3], i % 3 * 2 * each
                ref[chunk, 3 * UNIT : 3 * UNIT + 16, :] = block[:16]
                ref[chunk + 1, 3 * UNIT : 3 * UNIT + 16, :] = block[16:]

    @pl.when(core_ref[0] == 0)
    def _():
        fill((keep_ref, give_ref))

    @pl.when(core_ref[0] != 0)
    def _():
        fill((give_ref, keep_ref))


def wgrad_kv(core, qo, parts):
    rows, width = parts[0][2].shape[1:]
    half = parts[0][0].shape[0]
    whole = lambda n: pl.BlockSpec((n, width), lambda t, c: (0, 0))
    specs, args = [], []
    for m, p in enumerate(parts):
        specs += [
            whole(half), whole(half),
            pl.BlockSpec((None, rows, width), lambda t, c, m=m: (m, 0, 0)),
            pl.BlockSpec((2 * half + CLEN, PART), lambda t, c: (0, t)), whole(24),
        ]
        args += list(p)
    count = len(parts)
    specs.append(pl.BlockSpec(qo.shape[:2] + (UNIT, LANES), lambda t, c: (0, 0, t, 0)))
    shape = (2 * qo.shape[1], PACK, LANES)
    return pl.pallas_call(
        functools.partial(wgrad_kv_kernel, count=count),
        grid_spec=pltpu.PrefetchScalarGridSpec(
            num_scalar_prefetch=1,
            grid=(2 * width // PART,),
            in_specs=specs,
            out_specs=[pl.BlockSpec(shape, lambda t, c: (0, 0, 0))] * 2,
        ),
        out_shape=[jax.ShapeDtypeStruct(shape, bf16)] * 2,
        compiler_params=params(),
        cost_estimate=pl.CostEstimate(
            flops=4 * count * (2 * half + CLEN) * width * width,
            bytes_accessed=12 * count * half * width,
            transcendentals=0,
        ),
        name="wgrad_kv",
    )(core, *args, qo)


def unpack_rows(part_ref, weights, query, key, value, out):
    rows = query.shape[0]
    each = rows // UNIT
    cols = PART // 2 // LANES
    for first, refs in ((0, (query, out)), (each, (key, value))):
        for j in range(2 * cols):
            ref, at = refs[j // cols], (j % cols) * LANES
            for k in range(each):
                ref[k * UNIT : (k + 1) * UNIT, at : at + LANES] = part_ref[
                    2 * j * each + first + k
                ].astype(f32)
    total = 0.0
    for grad, w_ref in zip((query, key, value), weights):
        prod = grad[...] * w_ref[...].astype(f32)
        total = total + sum(prod[:, i * LANES : (i + 1) * LANES] for i in range(cols))
    high, low = halves(total)
    ones = jnp.ones((8, LANES), bf16)
    return dot_nt(ones, high) + dot_nt(ones, low)


def unpack_mine_kernel(core_ref, part_ref, wq_ref, wk_ref, wv_ref, query, key, value, out, sums):
    total = unpack_rows(part_ref, (wq_ref, wk_ref, wv_ref), query, key, value, out)

    @pl.when(pl.program_id(0) == 0)
    def _():
        sums[...] = total

    @pl.when(pl.program_id(0) > 0)
    def _():
        sums[...] += total


def unpack_other_kernel(
    core_ref, part_ref, wq_ref, wk_ref, wv_ref, gain_ref, mine_sums, mine_tail, other_tail, *rest
):
    query, key, value, out, norm_gain, ffn_gain, router, const, const_vec, sums = rest[-10:]
    step = pl.program_id(0)
    total = unpack_rows(part_ref, (wq_ref, wk_ref, wv_ref), query, key, value, out)

    @pl.when(step == 0)
    def _():
        sums[...] = total

    @pl.when(step > 0)
    def _():
        sums[...] += total

    def finish(parts, tails):
        rows = sums.shape[1]
        each = rows // UNIT
        for c, part in enumerate(parts):
            at = slice(c * rows, (c + 1) * rows)
            norm_gain[at] = (part[0:1, :] / gain_ref[:, at])[0]
        for i in range(2 * rows // LANES):
            at = slice(i * LANES, (i + 1) * LANES)
            chunk = i % 3 * 2 * each
            small = tails[i // 3][chunk].astype(f32)
            rest = tails[i // 3][chunk + 1].astype(f32)
            router[:, at] = small[:TARGETS]
            for c in range(CONSTS):
                const[c, :, at] = small[TARGETS + 2 * c : TARGETS + 2 * c + 2]
            const_vec[:, at] = rest[:CONSTS]
            ffn_gain[at] = rest[CONSTS]

    last = step == pl.num_programs(0) - 1

    @pl.when(last & (core_ref[0] == 0))
    def _():
        finish((mine_sums, sums), (mine_tail, other_tail))

    @pl.when(last & (core_ref[0] != 0))
    def _():
        finish((sums, mine_sums), (other_tail, mine_tail))


def unpack(core, mine, swap, gain, w_query, w_key, w_value):
    width = w_query.shape[0]
    chunks = mine.shape[0]
    half = width // 2
    other = swap(mine)
    body = pl.BlockSpec((chunks, UNIT, LANES), lambda t, c: (0, t, 0))
    tail = pl.BlockSpec((chunks, PACK - 3 * UNIT, LANES), lambda t, c: (0, 3 * UNIT // (PACK - 3 * UNIT), 0))
    whole = lambda s: pl.BlockSpec(s, lambda t, c: (0,) * len(s))
    block = (half, PART // 2)
    by_core = lambda f: pl.BlockSpec(block, lambda t, c: (f(c[0]), t))
    grid = (2 * width // PART,)
    dense = [jax.ShapeDtypeStruct((width, width), f32)] * 4
    cost = pl.CostEstimate(
        flops=2 * width * width, bytes_accessed=12 * width * width, transcendentals=0
    )
    first = by_core(lambda c: c)
    *mats, sums = pl.pallas_call(
        unpack_mine_kernel,
        grid_spec=pltpu.PrefetchScalarGridSpec(
            num_scalar_prefetch=1,
            grid=grid,
            in_specs=[body, first, first, first],
            out_specs=[first] * 4 + [whole((8, half))],
        ),
        out_shape=dense + [jax.ShapeDtypeStruct((8, half), f32)],
        compiler_params=params(),
        cost_estimate=cost,
        name="unpack_mine",
    )(core, mine, w_query, w_key, w_value)
    second = by_core(lambda c: 1 - c)
    small = [(width,), (width,), (TARGETS, width), (CONSTS, 2, width), (CONSTS, width)]
    args = (core, other, w_query, w_key, w_value, gain, sums, mine, other)
    return pl.pallas_call(
        unpack_other_kernel,
        grid_spec=pltpu.PrefetchScalarGridSpec(
            num_scalar_prefetch=1,
            grid=grid,
            in_specs=[body, second, second, second, whole((1, width)), whole((8, half)), tail, tail]
            + [pl.BlockSpec(memory_space=pl.ANY)] * 4,
            out_specs=[second] * 4 + [whole(s) for s in small],
            scratch_shapes=[pltpu.VMEM((8, half), f32)],
        ),
        out_shape=dense + [jax.ShapeDtypeStruct(s, f32) for s in small],
        input_output_aliases={len(args) + i: i for i in range(4)},
        compiler_params=params(),
        cost_estimate=cost,
        name="unpack_other",
    )(*args, *mats)


def token_grad_kernel(x_ref, gain_ref, mine_ref, rtot_ref, *rest):
    parts, out_ref = rest[:-1], rest[-1]
    prompt = parts[0].shape[0]
    x = x_ref[...].astype(f32)
    scale = lax.rsqrt(jnp.mean(x * x, axis=1, keepdims=True) + norm_eps)
    mine = mine_ref[...]
    total = sum(p[...].astype(f32) for p in parts)
    grad = jnp.concatenate([mine[:prompt] + total, mine[prompt:]], axis=0) * gain_ref[...]
    xhat = x * scale
    grad = scale * (grad - xhat * jnp.mean(grad * xhat, axis=1, keepdims=True))
    out_ref[...] = (rtot_ref[...] + grad).astype(bf16)


def token_grad(x, gain, mine, rtot, parts):
    of_micro = lambda a: pl.BlockSpec((None,) + a.shape[1:], lambda m: (m, 0, 0))
    return pl.pallas_call(
        token_grad_kernel,
        grid=(x.shape[0],),
        in_specs=[of_micro(x), pl.BlockSpec(gain.shape, lambda m: (0, 0)), of_micro(mine), of_micro(rtot)]
        + [of_micro(p) for p in parts],
        out_specs=of_micro(x),
        out_shape=jax.ShapeDtypeStruct(x.shape, bf16),
        compiler_params=params(),
        cost_estimate=pl.CostEstimate(
            flops=16 * x.size, bytes_accessed=14 * x.size, transcendentals=0
        ),
        name="token_grad",
    )(x, gain, mine, rtot, *parts)


def add_kernel(*refs):
    refs[-1][...] = sum(r[...].astype(f32) for r in refs[:-1]).astype(bf16)


def add(arrays, steps=4):
    shape = arrays[0].shape
    block = pl.BlockSpec((shape[0] // steps,) + shape[1:], lambda t: (t,) + (0,) * (len(shape) - 1))
    return pl.pallas_call(
        add_kernel,
        grid=(steps,),
        in_specs=[block] * len(arrays),
        out_specs=block,
        out_shape=jax.ShapeDtypeStruct(shape, bf16),
        compiler_params=params(),
        cost_estimate=pl.CostEstimate(
            flops=arrays[0].size, bytes_accessed=2 * arrays[0].size, transcendentals=0
        ),
        name="add",
    )(*arrays)


def sum_copies_kernel(parts_ref, out_ref):
    total = sum(parts_ref[i].astype(f32) for i in range(parts_ref.shape[0])).astype(bf16)
    for i in range(out_ref.shape[0]):
        out_ref[i] = total


def sum_copies(parts, copies):
    return pl.pallas_call(
        sum_copies_kernel,
        out_shape=jax.ShapeDtypeStruct((copies,) + parts.shape[1:], bf16),
        compiler_params=params(),
        cost_estimate=pl.CostEstimate(
            flops=parts.size, bytes_accessed=2 * parts.size, transcendentals=0
        ),
        name="sum_copies",
    )(parts)


def swap_cores(rows):
    return lax.ppermute(rows, "core", [(0, 1), (1, 0)])


def exchange(blocks, axes):
    return lax.all_to_all(blocks, axes, split_axis=0, concat_axis=0, tiled=True)


def spread_out(piece, axes):
    count = lax.axis_size(axes)
    return exchange(jnp.broadcast_to(piece[None], (count,) + piece.shape), axes)


def ring_parts(parts, axis, dim):
    count = lax.axis_size(axis)
    me = lax.axis_index(axis)
    part = lambda i: lax.dynamic_index_in_dim(parts, i, dim, keepdims=False)
    out = [part(me)]
    for step in range(1, count):
        ring = [(i, (i + step) % count) for i in range(count)]
        out.append(lax.ppermute(part((me + step) % count), axis, ring))
    return out


def after(value, *others):
    return lax.optimization_barrier((value, *others))[0]


def on_device(
    tokens, prior_logits, routes, drops, cont_lengths, norm_gain, w_query, w_key, w_value, w_out,
    ffn_gain, w_router, w_const, const_vec, w_gate, w_up, w_down, out_grad,
):
    micros, rows, width = tokens.shape[0], tokens.shape[3], tokens.shape[4]
    prompt = rows - CLEN
    cap = -(-(rows * 3 // 16) // 8) * 8
    chips = (lax.axis_size("context"), lax.axis_size("z"))
    half = chips[0] * chips[1] * prompt
    core = lax.axis_index("core").astype(jnp.int32)
    base = jnp.stack([lax.axis_index(("context", "z", "core")).astype(jnp.int32) * prompt, core])
    score_scale = 1.0 / math.sqrt(HEAD_SIZE)
    gain_one = norm_gain.astype(f32)
    gain_two = ffn_gain.astype(f32).reshape(1, width)

    gain_row = gain_one.reshape(1, width)
    core_arg = core.reshape(1)
    x = tokens[:, 0, 0]
    normed, copies, *own_rows = first_norm(x, norm_gain, chips[0] * chips[1])
    gathered = [exchange(copies, CHIPS)]
    gathered += [lax.all_gather(rows_m, CHIPS, axis=0) for rows_m in own_rows]

    wr = jnp.concatenate(
        [w_router] + [w_const[j] for j in range(CONSTS)]
        + [jnp.zeros((width, LANES - TARGETS - 2 * CONSTS), bf16)], axis=1,
    )
    cv = jnp.zeros((LANES, width), bf16).at[EXPERTS + 2 : EXPERTS + 2 + CONSTS].set(const_vec)
    wide = QUAD * HEAD_SIZE
    w_kv = jnp.concatenate(
        [w[:, g * wide : (g + 1) * wide] for g in range(HEADS // QUAD) for w in (w_key, w_value)], axis=1
    )
    row_ids = jnp.arange(rows, dtype=jnp.int32)
    og = out_grad[:, 0, 0]
    live = row_ids[None] < prompt + cont_lengths[:, 0]
    active = (1 - drops[:, 0, 0]) * live[..., None].astype(jnp.int32)
    eff = jnp.where(active > 0, routes[:, 0, 0], -1)
    efft = jnp.swapaxes(eff, 1, 2)
    prior = jnp.pad(prior_logits[:, 0, 0], ((0, 0), (0, 0), (0, LANES - TARGETS)))

    st = []
    for m in range(micros):
        s = {}
        if m:
            gathered[m] = after(gathered[m], st[m - 1]["attn"])
        else:
            gathered[m] = after(gathered[m], w_kv, wr, cv, eff, efft, prior, base, core_arg, gain_row, gain_two)
        s["near"] = gathered[m].reshape(half, width)
        s["far"] = swap_cores(s["near"])
        (
            s["attn"], s["lse"], s["q"], s["kv"],
            s["resid"], s["two"], s["ch"], send, s["sel"], s["selt"], s["gate"],
        ) = attn_fwd(
            base, normed, s["near"], s["far"], w_query, w_kv,
            x, w_out, gain_two, wr, prior, eff, efft, og, chips, cap, m,
        )
        s["recv"] = exchange(send.reshape(EXPERTS, cap, 2 * width), EXPERT).reshape(
            EXPERTS * cap, 2 * width
        )
        st.append(s)
    for s in st:
        ret, s["hid"], s["gg"], s["ug"] = experts(s["recv"], w_gate, w_up, w_down)
        s["ret"] = exchange(ret.reshape(EXPERTS, cap, 2 * width), EXPERT).reshape(
            EXPERTS * cap, 2 * width
        )
    wide_grads = expert_wgrad([(s["recv"], s["hid"], s["gg"], s["ug"]) for s in st])
    for m in range(micros - 1):
        st[m]["ret"] = after(st[m]["ret"], wide_grads)
    wide_sum = lax.psum(tuple(wide_grads), ("dp", "context"))

    kv_parts, qo_parts, back_parts, before = [], [], [], ()
    for m, s in enumerate(st):
        dq, dkv, mixed, rtot, branch, dl, small = attn_bwd(
            base, s["q"], s["kv"], s["attn"], s["lse"],
            s["resid"], s["two"], s["ch"], eff, og, s["ret"], s["sel"], s["selt"], s["gate"],
            w_out, gain_two, wr, cv, chips, cap, m, before,
        )
        before = (mixed, rtot, dl)
        if m < micros - 1:
            st[m + 1]["ret"] = after(st[m + 1]["ret"], dkv)
        kv_parts.append((s["near"], s["far"], normed, dkv, small))
        qo_parts.append((normed, dq, s["attn"], branch))
        back_parts.append((dq, dkv))
    qo = wgrad_qo(qo_parts)
    give, keep = wgrad_kv(core_arg, qo, kv_parts)
    dkvs = [dkv for _, dkv in back_parts]
    dkvs[0] = after(dkvs[0], give)
    give_rows = back_proj(dkvs, w_kv, 1)
    come = after(swap_cores(give), give_rows)
    keep = (keep.astype(f32) + come.astype(f32)).astype(bf16)
    dense = exchange(keep.reshape((lax.axis_size(FIRST), -1) + keep.shape[1:]), FIRST)
    come = swap_cores(give_rows)
    keep = back_proj(dkvs, w_kv, 0)
    rows_sum = (keep.astype(f32) + come.astype(f32)).astype(bf16)
    dense = after(dense, rows_sum)
    rows_sum = rows_sum.reshape(micros, chips[1], chips[0] * prompt, width)
    rows_parts = ring_parts(rows_sum, "z", 1)
    rows_sum = add(rows_parts, micros)
    mine = own_proj(back_parts, w_query, w_kv)
    dense = after(jnp.sum(dense.astype(f32), axis=0).astype(bf16), mine)
    dense = sum_copies(exchange(dense, REST), lax.axis_size(ALL_CHIPS))
    dense = exchange(after(dense, wide_sum, rows_parts), ALL_CHIPS)
    wide_out = [g.astype(f32)[None] for g in wide_sum]
    prior_grad = dl[:, :, :TARGETS]
    rows_sum = after(rows_sum, wide_out, prior_grad)
    parts = ring_parts(rows_sum.reshape(micros, chips[0], prompt, width), "context", 1)
    x_grad = token_grad(x, gain_row, mine, rtot, parts)
    dense = after(dense, parts)
    query, key, value, out, norm_gain, ffn_gain, router, const, vec = unpack(
        core_arg, dense, swap_cores, gain_row, w_query, w_key, w_value
    )
    return (
        mixed[:, None, None],
        x_grad[:, None, None],
        prior_grad[:, None, None],
        norm_gain,
        query,
        key,
        value,
        out,
        ffn_gain,
        router.T,
        jnp.swapaxes(const, 1, 2),
        vec,
        *wide_out,
    )


def solution(mesh):
    shape = mesh.devices.shape
    split = Mesh(
        mesh.devices.reshape(shape[0], shape[1], shape[2] // 2, 2), ("dp", "context", "z", "core")
    )
    slot = P(None, "dp", ("context", "z", "core"), None, None)
    expert = P(("z", "core"), None, None)
    return jax.shard_map(
        on_device,
        mesh=split,
        in_specs=(
            slot, slot, slot, slot, P(None, "dp", ("context", "z", "core")),
            *(P(),) * 9,
            *(expert,) * 3,
            slot,
        ),
        out_specs=(slot, slot, slot, *(P(),) * 9, *(expert,) * 3),
        check_vma=False,
    )
```

```python
import functools
import math

import jax
import jax.numpy as jnp
from jax import lax
from jax.experimental import pallas as pl
from jax.experimental.pallas import tpu as pltpu
from jax.sharding import Mesh, PartitionSpec as P

HEADS = 12
HEAD_SIZE = 64
EXPERTS = 8
CONSTS = 2
TARGETS = 12
CLEN = 128
QUAD = 4
LANES = 128

norm_eps = 1e-05
very_low = -1e30
highest = lax.Precision.HIGHEST
f32 = jnp.float32
bf16 = jnp.bfloat16
CHIPS = ("z", "context")
FIRST, REST = "z", ("dp", "context")
ALL_CHIPS = (FIRST,) + REST
EXPERT = ("z", "core")


def dot_nn(left, right, **kw):
    return jnp.dot(left, right, preferred_element_type=f32, **kw)


def dot_nt(left, right, **kw):
    return lax.dot_general(left, right, (((1,), (1,)), ((), ())), preferred_element_type=f32, **kw)


def dot_tn(left, right, **kw):
    return lax.dot_general(left, right, (((0,), (0,)), ((), ())), preferred_element_type=f32, **kw)


def halves(wide):
    high = wide.astype(bf16)
    return high, (wide - high.astype(f32)).astype(bf16)


def iota(shape, dim):
    return lax.broadcasted_iota(jnp.int32, shape, dim)


def params():
    return pltpu.CompilerParams(vmem_limit_bytes=63_400_000)


def head_masks(dtype):
    lane_head = iota((1, QUAD * HEAD_SIZE), 1) // HEAD_SIZE
    return [(lane_head == h).astype(f32).astype(dtype) for h in range(QUAD)]


def spread(rows, prompt, dtype):
    masks = head_masks(dtype)
    return jnp.concatenate(
        [rows[:prompt] * m for m in masks] + [rows[prompt:] * m for m in masks], axis=0
    )


def gather_heads(stacked, prompt, dtype):
    masks = head_masks(dtype)
    top, low = 0.0, 0.0
    first = QUAD * prompt
    for h in range(QUAD):
        top = top + stacked[h * prompt : (h + 1) * prompt] * masks[h]
        low = low + stacked[first + h * CLEN : first + (h + 1) * CLEN] * masks[h]
    return jnp.concatenate([top, low], axis=0)


def first_norm_kernel(x_ref, gain_ref, normed_ref, copies_ref, *prompt_refs):
    x = x_ref[...].astype(f32)
    scale = lax.rsqrt(jnp.mean(x * x, axis=1, keepdims=True) + norm_eps)
    normed = (x * scale * gain_ref[...].astype(f32).reshape(1, -1)).astype(bf16)
    normed_ref[...] = normed
    micro = pl.program_id(0)
    prompt = copies_ref.shape[1]

    @pl.when(micro == 0)
    def _():
        for i in range(copies_ref.shape[0]):
            copies_ref[i] = normed[:prompt]

    for m, ref in enumerate(prompt_refs):

        @pl.when(micro == m + 1)
        def _():
            ref[...] = normed[:prompt]


def first_norm(x, gain, copies):
    micros, rows, width = x.shape
    of_micro = pl.BlockSpec((None, rows, width), lambda m: (m, 0, 0))
    shapes = [(copies, rows - CLEN, width)] + [(rows - CLEN, width)] * (micros - 1)
    whole = lambda s: pl.BlockSpec(s, lambda m: (0,) * len(s))
    return pl.pallas_call(
        first_norm_kernel,
        grid=(micros,),
        in_specs=[of_micro, whole((width,))],
        out_specs=[of_micro] + [whole(s) for s in shapes],
        out_shape=[jax.ShapeDtypeStruct(s, bf16) for s in [x.shape] + shapes],
        compiler_params=params(),
        cost_estimate=pl.CostEstimate(
            flops=8 * micros * rows * width, bytes_accessed=4 * micros * rows * width, transcendentals=0
        ),
        name="first_norm",
    )(x, gain)


def key_places(core, keys, prompt, chips, j):
    half = keys // 2
    other = jnp.where(j >= half, 1, 0)
    chip = (j - other * half) // prompt
    chip = (chip % chips[0]) * chips[1] + chip // chips[0]
    slot = chip * 2 + jnp.where(other > 0, 1 - core, core)
    return slot * prompt + (j & (prompt - 1))


def attn_fwd_kernel(
    base_ref, normed_ref, near_ref, far_ref, wq_ref, wkv_ref,
    x_ref, wout_ref, gain_ref, wr_ref, prior_ref, eff_ref, efft_ref, og_ref,
    o_ref, lse_ref, q_ref, kv_ref,
    resid_ref, two_ref, ch_ref, send_ref, sel_ref, selt_ref, gate_ref, o_all,
    *, chips, cap,
):
    g = pl.program_id(0)
    prompt = q_ref.shape[0] - CLEN
    keys = kv_ref.shape[0] - CLEN
    half = keys // 2
    wide = QUAD * HEAD_SIZE
    masks = head_masks(bf16)
    masks_f = head_masks(f32)
    ones = jnp.ones((8, LANES), f32)

    def to_row(column):
        spare = jnp.where(iota((column.shape[0], LANES), 1) == 0, column, 0.0)
        return dot_nt(ones, spare, precision=highest)

    q = dot_nn(normed_ref[...], wq_ref[...]).astype(bf16).astype(f32)
    q_ref[...] = (q * (1.0 / math.sqrt(HEAD_SIZE))).astype(bf16)
    for rows, at in ((near_ref, 0), (far_ref, half)):
        kv_ref[at : at + half] = dot_nn(rows[...], wkv_ref[...]).astype(bf16)
    kv_ref[keys:] = dot_nn(normed_ref[prompt:], wkv_ref[...]).astype(bf16)
    q_top, q_low = q_ref[:prompt], q_ref[prompt:]
    q_p = jnp.concatenate([q_top * m for m in masks], axis=0)
    s = dot_nt(q_p, kv_ref[:keys, :wide])
    limit = base_ref[0] + (iota((QUAD * prompt, 1), 0) & (prompt - 1))
    s = jnp.where(key_places(base_ref[1], keys, prompt, chips, iota((1, keys), 1)) <= limit, s, very_low)
    top = jnp.max(s, axis=1, keepdims=True)
    p = jnp.exp(s - top)
    total = jnp.sum(p, axis=1, keepdims=True)
    out = dot_nn(p.astype(bf16), kv_ref[:keys, wide:]) * (1.0 / total)
    lse_ref[:, : QUAD * prompt] = to_row(top + jnp.log(total))
    top_out = sum(out[h * prompt : (h + 1) * prompt] * masks_f[h] for h in range(QUAD))
    low_out = 0.0
    per = 2
    for part in range(QUAD // per):
        hs = range(part * per, (part + 1) * per)
        rows = per * CLEN
        q_c = jnp.concatenate([q_low * masks[h] for h in hs], axis=0)
        s = dot_nt(q_c, kv_ref[:keys, :wide])
        own = dot_nt(q_c, kv_ref[keys:, :wide])
        own = jnp.where(
            iota((1, CLEN), 1) <= (iota((rows, 1), 0) & (CLEN - 1)), own, very_low
        )
        top = jnp.maximum(
            jnp.max(s, axis=1, keepdims=True), jnp.max(own, axis=1, keepdims=True)
        )
        p = jnp.exp(s - top)
        p_own = jnp.exp(own - top)
        total = jnp.sum(p, axis=1, keepdims=True) + jnp.sum(p_own, axis=1, keepdims=True)
        out = dot_nn(p.astype(bf16), kv_ref[:keys, wide:])
        out = out + dot_nn(p_own.astype(bf16), kv_ref[keys:, wide:])
        out = out * (1.0 / total)
        at = QUAD * prompt + part * rows
        lse_ref[:, at : at + rows] = to_row(top + jnp.log(total))
        for i, h in enumerate(hs):
            low_out = low_out + out[i * CLEN : (i + 1) * CLEN] * masks_f[h]
    attn = jnp.concatenate([top_out, low_out], axis=0)
    o_ref[...] = attn
    o_all[g] = attn.astype(bf16)

    @pl.when(g == o_all.shape[0] - 1)
    def _():
        attended = jnp.concatenate([o_all[i] for i in range(o_all.shape[0])], axis=1)
        route(
            attended, x_ref, wout_ref, gain_ref, wr_ref, prior_ref, eff_ref, efft_ref, og_ref,
            resid_ref, two_ref, ch_ref, send_ref, sel_ref, selt_ref, gate_ref, cap,
        )


def attn_fwd(
    base, normed, near, far, w_query, w_kv, x, w_out, gain, wr, prior, eff, efft, og,
    chips, cap, micro,
):
    rows, width = normed.shape[1:]
    half = near.shape[0]
    every = 2 * half + CLEN
    quads = HEADS // QUAD
    wide = QUAD * HEAD_SIZE
    slots = EXPERTS * cap
    col = lambda n, w=wide: pl.BlockSpec((n, w), lambda g, b: (0, g))
    whole = lambda n, w=width: pl.BlockSpec((n, w), lambda g, b: (0, 0))
    of_micro = lambda a: pl.BlockSpec((None,) + a.shape[1:], lambda g, b: (micro, 0, 0))
    routed = [
        ((rows, width), f32), ((rows, width), bf16), ((rows, LANES), f32), ((slots, 2 * width), bf16),
        ((slots, rows), bf16), ((rows, slots), bf16), ((slots, LANES), f32),
    ]
    return pl.pallas_call(
        functools.partial(attn_fwd_kernel, chips=chips, cap=cap),
        grid_spec=pltpu.PrefetchScalarGridSpec(
            num_scalar_prefetch=1,
            grid=(quads,),
            in_specs=[
                of_micro(normed), whole(half), whole(half), col(width), col(width, 2 * wide),
                of_micro(x), whole(width), whole(1), whole(width, LANES), of_micro(prior),
                of_micro(eff), of_micro(efft), of_micro(og),
            ],
            out_specs=[
                col(rows),
                pl.BlockSpec((None, 8, QUAD * rows), lambda g, b: (g, 0, 0)),
                col(rows),
                col(every, 2 * wide),
            ]
            + [whole(*s) for s, _ in routed],
            scratch_shapes=[pltpu.VMEM((quads, rows, wide), bf16)],
        ),
        out_shape=[
            jax.ShapeDtypeStruct((rows, width), f32),
            jax.ShapeDtypeStruct((quads, 8, QUAD * rows), f32),
            jax.ShapeDtypeStruct((rows, width), bf16),
            jax.ShapeDtypeStruct((every, 2 * width), bf16),
        ]
        + [jax.ShapeDtypeStruct(s, t) for s, t in routed],
        compiler_params=params(),
        cost_estimate=pl.CostEstimate(
            flops=16 * rows * every * width + 4 * every * width * width,
            bytes_accessed=4 * every * width,
            transcendentals=rows * every * HEADS,
        ),
        name="attn_fwd",
    )(base, normed, near, far, w_query, w_kv, x, w_out, gain, wr, prior, eff, efft, og)


def attn_bwd_kernel(
    base_ref, q_ref, kv_ref, o_ref, lse_ref,
    resid_ref, two_ref, ch_ref, eff_ref, og_ref, ret_ref, sel_ref, selt_ref, gate_ref,
    wout_ref, gain_ref, wr_ref, cv_ref, *rest, block, chips, cap
):
    (
        dq_ref, dkv_ref, mixed_ref, rtot_ref, branch_ref, dl_ref, small_ref, qm, dom, dqt, do_all
    ) = rest[-11:]
    g = pl.program_id(0)
    quads = do_all.shape[0]

    @pl.when(g == 0)
    def _():
        grad = combine(
            resid_ref, two_ref, ch_ref, eff_ref, og_ref, ret_ref, sel_ref, selt_ref, gate_ref,
            wout_ref, gain_ref, wr_ref, cv_ref,
            mixed_ref, rtot_ref, branch_ref, dl_ref, small_ref, cap,
        )
        for i in range(quads):
            do_all[i] = grad[:, i * QUAD * HEAD_SIZE : (i + 1) * QUAD * HEAD_SIZE]

    do_now = do_all[g]
    prompt = q_ref.shape[0] - CLEN
    keys = kv_ref.shape[0] - CLEN
    wide = QUAD * HEAD_SIZE
    qm[...] = spread(q_ref[...], prompt, bf16)
    dom[...] = spread(do_now, prompt, bf16)
    prod = spread(do_now.astype(f32) * o_ref[...], prompt, f32)
    ones = jnp.ones((8, prod.shape[1]), bf16)
    prod_high, prod_low = halves(prod)
    delta = (dot_nt(ones, prod_high) + dot_nt(ones, prod_low))[0:1]
    lse = lse_ref[0:1, :]
    first = QUAD * prompt
    ahead = (iota((prompt, first), 1) & (prompt - 1)) - iota((prompt, first), 0)
    q_all, do_all = qm[...], dom[...]

    def one(rows, mask):
        kk, vv = kv_ref[rows, :wide], kv_ref[rows, wide:]
        p = jnp.exp(dot_nt(kk, q_all) - lse)
        p = mask(p)
        ds = p * (dot_nt(vv, do_all) - delta)
        pb, dsb = p.astype(bf16), ds.astype(bf16)
        dkv_ref[rows, :wide] = dot_nn(dsb, q_all).astype(bf16)
        dkv_ref[rows, wide:] = dot_nn(pb, do_all).astype(bf16)
        return dot_tn(kk, dsb)

    def own_mask(p):
        lane = iota((1, p.shape[1]), 1)
        own_row = jnp.where(lane < first, -1, (lane - first) & (CLEN - 1))
        return jnp.where(iota((CLEN, 1), 0) <= own_row, p, 0.0)

    dqt[...] = one(pl.ds(keys, CLEN), own_mask)

    def step(i, unused):
        at = i * block

        def mask(p):
            rows = []
            for r in range(0, block, prompt):
                gap = key_places(base_ref[1], keys, prompt, chips, at + r) - base_ref[0]
                rows.append(jnp.where(ahead >= gap, p[r : r + prompt, :first], 0.0))
            return jnp.concatenate([jnp.concatenate(rows, axis=0), p[:, first:]], axis=1)

        dqt[...] += one(pl.ds(at, block), mask)
        return unused

    for i in range(keys // block):
        step(i, 0)
    dq = gather_heads(dqt[...].T, prompt, f32)
    dq = (dq * (1.0 / math.sqrt(HEAD_SIZE))).astype(bf16)
    dq_ref[...] = dq


def attn_bwd(
    base, q, kv, o, lse, resid, two, ch, eff, og, ret, sel, selt, gate, w_out, gain, wr, cv,
    chips, cap, micro, before, block=1024,
):
    rows, width = q.shape
    every = kv.shape[0]
    quads = HEADS // QUAD
    wide = QUAD * HEAD_SIZE
    micros = eff.shape[0]
    col = lambda n, w=wide: pl.BlockSpec((n, w), lambda g, b: (0, g))
    whole = lambda a: pl.BlockSpec(a.shape, lambda g, b: (0, 0))
    of_micro = lambda a: pl.BlockSpec((None,) + a.shape[1:], lambda g, b: (micro, 0, 0))
    mixing = [
        jax.ShapeDtypeStruct((micros, rows, width), bf16),
        jax.ShapeDtypeStruct((micros, rows, width), f32),
        jax.ShapeDtypeStruct((rows, width), bf16),
        jax.ShapeDtypeStruct((micros, rows, LANES), f32),
        jax.ShapeDtypeStruct((24, width), f32),
    ]
    args = (base, q, kv, o, lse, resid, two, ch, eff, og, ret, sel, selt, gate, w_out, gain, wr, cv)
    return pl.pallas_call(
        functools.partial(
            attn_bwd_kernel, block=min(block, (every - CLEN) // 2), chips=chips, cap=cap
        ),
        grid_spec=pltpu.PrefetchScalarGridSpec(
            num_scalar_prefetch=1,
            grid=(quads,),
            in_specs=[
                col(rows), col(every, 2 * wide), col(rows),
                pl.BlockSpec((None, 8, QUAD * rows), lambda g, b: (g, 0, 0)),
                whole(resid), whole(two), whole(ch), of_micro(eff), of_micro(og), whole(ret),
                whole(sel), whole(selt), whole(gate), whole(w_out), whole(gain), whole(wr), whole(cv),
            ]
            + [pl.BlockSpec(memory_space=pl.ANY) for _ in before],
            out_specs=[col(rows), col(every, 2 * wide)]
            + [of_micro(a) if len(a.shape) == 3 else whole(a) for a in mixing],
            scratch_shapes=[
                pltpu.VMEM((QUAD * rows, wide), bf16),
                pltpu.VMEM((QUAD * rows, wide), bf16),
                pltpu.VMEM((wide, QUAD * rows), f32),
                pltpu.VMEM((quads, rows, wide), bf16),
            ],
        ),
        out_shape=[
            jax.ShapeDtypeStruct((rows, width), bf16),
            jax.ShapeDtypeStruct((every, 2 * width), bf16),
        ]
        + mixing,
        input_output_aliases={len(args) + i: out for i, out in enumerate((2, 3, 5)[: len(before)])},
        compiler_params=params(),
        cost_estimate=pl.CostEstimate(
            flops=40 * rows * every * width,
            bytes_accessed=8 * every * width,
            transcendentals=rows * every * HEADS,
        ),
        name="attn_bwd",
    )(*args, *before)


def back_proj_kernel(*refs, count, steps):
    ins, (w_ref, out_ref) = refs[:count], refs[count:]
    for m in range(count):

        @pl.when(pl.program_id(0) // steps == m)
        def _():
            out_ref[...] = dot_nt(ins[m][...], w_ref[...]).astype(bf16)


def back_proj(dkvs, w_kv, which, steps=2):
    count = len(dkvs)
    width = dkvs[0].shape[1] // 2
    half = (dkvs[0].shape[0] - CLEN) // 2
    rows = half // steps
    at = lambda m: lambda t: (which * steps + jnp.clip(t - m * steps, 0, steps - 1), 0)
    return pl.pallas_call(
        functools.partial(back_proj_kernel, count=count, steps=steps),
        grid=(count * steps,),
        in_specs=[pl.BlockSpec((rows, 2 * width), at(m)) for m in range(count)]
        + [pl.BlockSpec(w_kv.shape, lambda t: (0, 0))],
        out_specs=pl.BlockSpec((None, rows, width), lambda t: (t // steps, t % steps, 0)),
        out_shape=jax.ShapeDtypeStruct((count, half, width), bf16),
        compiler_params=params(),
        cost_estimate=pl.CostEstimate(
            flops=count * half * width * width, bytes_accessed=2 * count * half * width, transcendentals=0
        ),
        name="back_proj",
    )(*dkvs, w_kv)


def own_proj_kernel(*refs, count):
    ins, (wq_ref, wkv_ref, out_ref) = refs[: 2 * count], refs[2 * count :]
    for m in range(count):
        dq = dot_nt(ins[2 * m][...], wq_ref[...])
        prompt = dq.shape[0] - CLEN
        out_ref[m, :prompt] = dq[:prompt]
        out_ref[m, prompt:] = dq[prompt:] + dot_nt(ins[2 * m + 1][...], wkv_ref[...])


def own_proj(parts, w_query, w_kv):
    rows, width = parts[0][0].shape
    every = parts[0][1].shape[0]
    whole = lambda n, w=width: pl.BlockSpec((n, w), lambda i: (0, 0))
    tail = pl.BlockSpec((CLEN, 2 * width), lambda i: (every // CLEN - 1, 0))
    count = len(parts)
    return pl.pallas_call(
        functools.partial(own_proj_kernel, count=count),
        grid=(1,),
        in_specs=[whole(rows), tail] * count + [whole(width), whole(width, 2 * width)],
        out_shape=jax.ShapeDtypeStruct((count, rows, width), f32),
        compiler_params=params(),
        cost_estimate=pl.CostEstimate(
            flops=6 * count * rows * width * width, bytes_accessed=6 * width * width, transcendentals=0
        ),
        name="own_proj",
    )(*[a for p in parts for a in p], w_query, w_kv)


def route(
    attended, x_ref, wout_ref, gain_ref, wr_ref, prior_ref, eff_ref, efft_ref, og_ref,
    resid_ref, two_ref, ch_ref, send_ref, sel_ref, selt_ref, gate_ref, cap,
):
    rows, width = x_ref.shape
    slots = EXPERTS * cap
    resid = x_ref[...].astype(f32) + dot_nn(attended, wout_ref[...])
    resid_ref[...] = resid
    inv = lax.rsqrt(jnp.mean(resid * resid, axis=1, keepdims=True) + norm_eps)
    two = (resid * inv * gain_ref[...]).astype(bf16)
    two_ref[...] = two
    lane = iota((1, LANES), 1)
    logits = dot_nn(two, wr_ref[...]) + prior_ref[...]
    masked = jnp.where(lane < TARGETS, logits, very_low)
    e = jnp.exp(masked - jnp.max(masked, axis=1, keepdims=True))
    ch = e * (1.0 / jnp.sum(e, axis=1, keepdims=True))
    for j in range(CONSTS):
        at = TARGETS + 2 * j
        diff = logits[:, at + 1 : at + 2] - logits[:, at : at + 1]
        ch = jnp.where(lane == at, 1.0 / (1.0 + jnp.exp(diff)), ch)
        ch = jnp.where(lane == at + 1, 1.0 / (1.0 + jnp.exp(-diff)), ch)
    ch_ref[...] = ch
    target = iota((16, rows), 0)
    hot_t = ((target == efft_ref[0:1, :]) | (target == efft_ref[1:2, :])).astype(f32)
    before = (iota((rows, rows), 0) < iota((rows, rows), 1)).astype(f32).astype(bf16)
    rank_t = dot_nn(hot_t.astype(bf16), before)
    rank_t = jnp.where(hot_t > 0.0, rank_t, -1.0)
    place = iota((cap, 1), 0).astype(f32)
    sel = jnp.concatenate(
        [(place == rank_t[i : i + 1, :]).astype(f32) for i in range(EXPERTS)], axis=0
    )
    sel_b = sel.astype(bf16)
    sel_ref[...] = sel_b
    hot = ((lane == eff_ref[:, 0:1]) | (lane == eff_ref[:, 1:2])).astype(f32)
    after = (iota((rows, rows), 0) > iota((rows, rows), 1)).astype(f32).astype(bf16)
    rank = dot_nn(after, hot.astype(bf16))
    rank = jnp.where(hot > 0.0, rank, -1.0)
    slot = iota((1, slots), 1)
    widen = (slot // cap == iota((LANES, 1), 0)).astype(f32).astype(bf16)
    rank_s = dot_nn(rank.astype(bf16), widen)
    selt_ref[...] = (rank_s == (slot % cap).astype(f32)).astype(f32).astype(bf16)
    ch_high, ch_low = halves(ch)
    ch_s = dot_nn(sel_b, ch_high) + dot_nn(sel_b, ch_low)
    of_slot = iota((slots, 1), 0) // cap
    gate = jnp.sum(jnp.where(lane == of_slot, ch_s, 0.0), axis=1, keepdims=True)
    gate_ref[...] = jnp.broadcast_to(gate, gate_ref.shape)
    send_ref[:, :width] = dot_nn(sel_b, two).astype(bf16)
    send_ref[:, width:] = (gate * dot_nn(sel_b, og_ref[...])).astype(bf16)


def expert_kernel(
    x_ref, g_ref, wg_ref, wu_ref, wd_ref, out_ref, hid_ref, gg_ref, ug_ref, fwd, back
):
    step = pl.program_id(0)
    width = x_ref.shape[1]

    @pl.when(step == 0)
    def _():
        fwd[...] = jnp.zeros_like(fwd)
        back[...] = jnp.zeros_like(back)

    x, g = x_ref[...], g_ref[...]
    gate = dot_nn(x, wg_ref[...])
    up = dot_nn(x, wu_ref[...])
    hid_grad = dot_nt(g, wd_ref[...])
    sig = 1.0 / (1.0 + jnp.exp(-gate))
    act = gate * sig
    hid = (act * up).astype(bf16)
    gg = (hid_grad * up * (sig + act * (1.0 - sig))).astype(bf16)
    ug = (hid_grad * act).astype(bf16)
    hid_ref[...] = hid
    gg_ref[...] = gg
    ug_ref[...] = ug
    fwd[...] += dot_nn(hid, wd_ref[...])
    back[...] += dot_nt(gg, wg_ref[...]) + dot_nt(ug, wu_ref[...])

    @pl.when(step == pl.num_programs(0) - 1)
    def _():
        out_ref[:, :width] = fwd[...].astype(bf16)
        out_ref[:, width:] = back[...].astype(bf16)


def experts(rows_in, w_gate, w_up, w_down, tile=512):
    rows = rows_in.shape[0]
    width = rows_in.shape[1] // 2
    hidden = w_gate.shape[2]
    half = lambda i: pl.BlockSpec((rows, width), lambda t, i=i: (0, i))
    inner = pl.BlockSpec((None, width, tile), lambda t: (0, 0, t))
    mid = pl.BlockSpec((rows, tile), lambda t: (0, t))
    return pl.pallas_call(
        expert_kernel,
        grid=(hidden // tile,),
        in_specs=[half(0), half(1), inner, inner, pl.BlockSpec((None, tile, width), lambda t: (0, t, 0))],
        out_specs=[pl.BlockSpec((rows, 2 * width), lambda t: (0, 0)), mid, mid, mid],
        out_shape=[jax.ShapeDtypeStruct((rows, 2 * width), bf16)]
        + [jax.ShapeDtypeStruct((rows, hidden), bf16)] * 3,
        scratch_shapes=[pltpu.VMEM((rows, width), f32), pltpu.VMEM((rows, width), f32)],
        compiler_params=params(),
        cost_estimate=pl.CostEstimate(
            flops=14 * rows * width * hidden,
            bytes_accessed=6 * width * hidden,
            transcendentals=rows * hidden,
        ),
        name="experts",
    )(rows_in, rows_in, w_gate, w_up, w_down)


def expert_wgrad_kernel(*refs, count):
    ins, (dg_ref, du_ref, dd_ref) = refs[: 5 * count], refs[5 * count :]
    x, g, hid, gg, ug = (
        jnp.concatenate([ins[5 * m + i][...] for m in range(count)], axis=0) for i in range(5)
    )
    dg_ref[...] = dot_tn(x, gg).astype(bf16)
    du_ref[...] = dot_tn(x, ug).astype(bf16)
    dd_ref[...] = dot_tn(hid, g).astype(bf16)


def expert_wgrad(parts, tile=512):
    rows = parts[0][0].shape[0]
    width = parts[0][0].shape[1] // 2
    hidden = parts[0][1].shape[1]
    half = lambda i: pl.BlockSpec((rows, width), lambda t, i=i: (0, i))
    mid = pl.BlockSpec((rows, tile), lambda t: (0, t))
    specs, args = [], []
    for rows_in, hid, gg, ug in parts:
        specs += [half(0), half(1), mid, mid, mid]
        args += [rows_in, rows_in, hid, gg, ug]
    inner = pl.BlockSpec((width, tile), lambda t: (0, t))
    return pl.pallas_call(
        functools.partial(expert_wgrad_kernel, count=len(parts)),
        grid=(hidden // tile,),
        in_specs=specs,
        out_specs=[inner, inner, pl.BlockSpec((tile, width), lambda t: (t, 0))],
        out_shape=[
            jax.ShapeDtypeStruct((width, hidden), bf16),
            jax.ShapeDtypeStruct((width, hidden), bf16),
            jax.ShapeDtypeStruct((hidden, width), bf16),
        ],
        compiler_params=params(),
        cost_estimate=pl.CostEstimate(
            flops=6 * len(parts) * rows * width * hidden,
            bytes_accessed=6 * width * hidden,
            transcendentals=0,
        ),
        name="expert_wgrad",
    )(*args)


def combine(
    resid_ref, two_ref, ch_ref, eff_ref, og_ref, ret_ref, sel_ref, selt_ref, gate_ref,
    wout_ref, gain_ref, wr_ref, cv_ref,
    mixed_ref, rtot_ref, branch_ref, dl_ref, small_ref, cap,
):
    rows, width = resid_ref.shape
    slots = EXPERTS * cap
    lane = iota((1, LANES), 1)
    resid, two_b, ch = resid_ref[...], two_ref[...], ch_ref[...]
    two = two_b.astype(f32)
    og_b = og_ref[...]
    og = og_b.astype(f32)
    eo = ret_ref[:, :width].astype(f32)
    sel, selt = sel_ref[...], selt_ref[...]
    hot = ((lane == eff_ref[:, 0:1]) | (lane == eff_ref[:, 1:2])).astype(f32)
    dgate = jnp.sum(dot_nn(sel, og_b) * eo, axis=1, keepdims=True)
    by_target = jnp.where(lane == iota((slots, 1), 0) // cap, dgate, 0.0)
    by_high, by_low = halves(by_target)
    dval = dot_nn(selt, by_high) + dot_nn(selt, by_low)
    self_dot = jnp.sum(og * two, axis=1, keepdims=True)
    cv_dot = dot_nt(og_b, cv_ref[...])
    gates = ch * hot
    keep = gates[:, EXPERTS + 1 : EXPERTS + 2]
    dval = jnp.where(lane == EXPERTS + 1, self_dot, dval)
    mixed = resid + dot_nn(selt, (gate_ref[:, 0:1] * eo).astype(bf16))
    dl_const = jnp.zeros((rows, LANES), f32)
    coef_cv = jnp.zeros((rows, LANES), f32)
    for j in range(CONSTS):
        e, at = EXPERTS + 2 + j, TARGETS + 2 * j
        a0, a1 = ch[:, at : at + 1], ch[:, at + 1 : at + 2]
        gate = gates[:, e : e + 1]
        with_cv = cv_dot[:, e : e + 1]
        dval = jnp.where(lane == e, a0 * self_dot + a1 * with_cv, dval)
        keep = keep + gate * a0
        mixed = mixed + (gate * a1) * cv_ref[e : e + 1, :].astype(f32)
        coef_cv = jnp.where(lane == TARGETS + 2 * CONSTS + j, gate * a1, coef_cv)
        da0, da1 = gate * self_dot, gate * with_cv
        mean = a0 * da0 + a1 * da1
        dl_const = jnp.where(lane == at, a0 * (da0 - mean), dl_const)
        dl_const = jnp.where(lane == at + 1, a1 * (da1 - mean), dl_const)
    mixed = mixed + keep * two
    mixed_ref[...] = mixed.astype(bf16)
    ch = jnp.where(lane < TARGETS, ch, 0.0)
    dch = hot * dval
    dl = ch * (dch - jnp.sum(ch * dch, axis=1, keepdims=True)) + dl_const
    dl_ref[...] = dl
    dl_hi, dl_lo = halves(dl)
    cc_hi, cc_lo = halves(coef_cv)
    small = dot_tn(dl_hi, two_b) + dot_tn(dl_lo, two_b) + dot_tn(cc_hi, og_b) + dot_tn(cc_lo, og_b)
    two_grad = (
        keep * og
        + dot_nt(dl_hi, wr_ref[...])
        + dot_nt(dl_lo, wr_ref[...])
        + dot_nn(selt, ret_ref[:, width:])
    )
    inv = lax.rsqrt(jnp.mean(resid * resid, axis=1, keepdims=True) + norm_eps)
    xhat = resid * inv
    gain_grad = jnp.sum(two_grad * xhat, axis=0, keepdims=True)
    small_ref[...] = jnp.where(
        iota((small_ref.shape[0], 1), 0) == TARGETS + 3 * CONSTS, gain_grad, small[: small_ref.shape[0]]
    )
    scaled = two_grad * gain_ref[...]
    rtot = og + inv * (scaled - xhat * jnp.mean(scaled * xhat, axis=1, keepdims=True))
    rtot_ref[...] = rtot
    branch = rtot.astype(bf16)
    branch_ref[...] = branch
    return dot_nt(branch, wout_ref[...]).astype(bf16)


UNIT = 48
PACK = 160
PART = 512


def units(grad):
    low = grad.astype(bf16)
    each = low.shape[0] // UNIT // 2
    for j in range(low.shape[1] // LANES):
        for k in range(2 * each):
            unit = low[k * UNIT : (k + 1) * UNIT, j * LANES : (j + 1) * LANES]
            yield j, k // each, k % each, unit


def wgrad_kernel(core_ref, *refs, count):
    ins, (give_ref, keep_ref, rows, sems) = refs[: 8 * count], refs[8 * count :]
    t = pl.program_id(0)
    part = lambda i: [ins[8 * m + i] for m in range(count)]
    nears, fars, normeds, dqs, attns, branches, dkvs, smalls = (part(i) for i in range(8))
    copies = [
        pltpu.make_async_copy(ref, rows.at[m, i], sems.at[2 * m + i])
        for m in range(count)
        for i, ref in enumerate((nears[m], fars[m]))
    ]

    def by_core(fill):
        @pl.when(core_ref[0] == 0)
        def _():
            fill((keep_ref, give_ref))

        @pl.when(core_ref[0] != 0)
        def _():
            fill((give_ref, keep_ref))

    @pl.when(t == 0)
    def _():
        for copy in copies:
            copy.start()
        stack = lambda refs: jnp.concatenate([r[...].astype(bf16) for r in refs], axis=0)
        query = dot_tn(stack(normeds), stack(dqs))
        out = dot_tn(stack(attns), stack(branches))
        each = query.shape[0] // UNIT // 2
        half = PART // 2
        small = sum(r[...] for r in smalls)
        small = jnp.concatenate([small, jnp.zeros((8, small.shape[1]), f32)], axis=0).astype(bf16)

        def fill(cores):
            for step in range(query.shape[1] // half):
                at = slice(step * half, (step + 1) * half)
                for j, c, k, unit in units(jnp.concatenate([query[:, at], out[:, at]], axis=1)):
                    cores[c][2 * j * each + k, step * UNIT : (step + 1) * UNIT, :] = unit
            for ref in cores:
                ref[:, 3 * UNIT :, :] = jnp.zeros((ref.shape[0], PACK - 3 * UNIT, LANES), bf16)
            for i in range(small.shape[1] // LANES):
                block = small[:, i * LANES : (i + 1) * LANES]
                ref, chunk = cores[i // 3], i % 3 * 2 * each
                ref[chunk, 3 * UNIT : 3 * UNIT + 16, :] = block[:16]
                ref[chunk + 1, 3 * UNIT : 3 * UNIT + 16, :] = block[16:]

        by_core(fill)

    @pl.when(t == 1)
    def _():
        for copy in copies:
            copy.wait()

    @pl.when(t > 0)
    def _():
        grad = 0.0
        for m in range(count):
            half = rows.shape[2]
            grad = grad + dot_tn(rows[m, 0], dkvs[m][:half])
            grad = grad + dot_tn(rows[m, 1], dkvs[m][half : 2 * half])
            own = normeds[m].shape[0] - CLEN
            grad = grad + dot_tn(normeds[m][own:], dkvs[m][2 * half :])

        def fill(cores):
            each = grad.shape[0] // UNIT // 2
            at = pl.ds(pl.multiple_of((t - 1) * UNIT, 16), UNIT)
            for j, c, k, unit in units(grad):
                cores[c][(2 * j + 1) * each + k, at, :] = unit

        by_core(fill)


def wgrad(core, parts):
    rows, width = parts[0][3].shape
    half = parts[0][0].shape[0]
    whole = lambda n: pl.BlockSpec((n, width), lambda t, c: (0, 0))
    hbm = pl.BlockSpec(memory_space=pl.ANY)
    specs, args = [], []
    for m, p in enumerate(parts):
        specs += [
            hbm, hbm, pl.BlockSpec((None, rows, width), lambda t, c, m=m: (m, 0, 0)),
            whole(rows), whole(rows), whole(rows),
            pl.BlockSpec((2 * half + CLEN, PART), lambda t, c: (0, jnp.maximum(t - 1, 0))), whole(24),
        ]
        args += list(p)
    count = len(parts)
    shape = (2 * PART // LANES * (width // UNIT // 2), PACK, LANES)
    return pl.pallas_call(
        functools.partial(wgrad_kernel, count=count),
        grid_spec=pltpu.PrefetchScalarGridSpec(
            num_scalar_prefetch=1,
            grid=(1 + 2 * width // PART,),
            in_specs=specs,
            out_specs=[pl.BlockSpec(shape, lambda t, c: (0, 0, 0))] * 2,
            scratch_shapes=[
                pltpu.VMEM((count, 2, half, width), bf16),
                pltpu.SemaphoreType.DMA((2 * count,)),
            ],
        ),
        out_shape=[jax.ShapeDtypeStruct(shape, bf16)] * 2,
        compiler_params=params(),
        cost_estimate=pl.CostEstimate(
            flops=4 * count * (2 * half + CLEN + rows) * width * width,
            bytes_accessed=12 * count * half * width,
            transcendentals=0,
        ),
        name="wgrad",
    )(core, *args)


def unpack_rows(part_ref, weights, query, key, value, out):
    rows = query.shape[0]
    each = rows // UNIT
    cols = PART // 2 // LANES
    for first, refs in ((0, (query, out)), (each, (key, value))):
        for j in range(2 * cols):
            ref, at = refs[j // cols], (j % cols) * LANES
            for k in range(each):
                ref[k * UNIT : (k + 1) * UNIT, at : at + LANES] = part_ref[
                    2 * j * each + first + k
                ].astype(f32)
    total = 0.0
    for grad, w_ref in zip((query, key, value), weights):
        prod = grad[...] * w_ref[...].astype(f32)
        total = total + sum(prod[:, i * LANES : (i + 1) * LANES] for i in range(cols))
    high, low = halves(total)
    ones = jnp.ones((8, LANES), bf16)
    return dot_nt(ones, high) + dot_nt(ones, low)


def unpack_mine_kernel(core_ref, part_ref, wq_ref, wk_ref, wv_ref, query, key, value, out, sums):
    total = unpack_rows(part_ref, (wq_ref, wk_ref, wv_ref), query, key, value, out)

    @pl.when(pl.program_id(0) == 0)
    def _():
        sums[...] = total

    @pl.when(pl.program_id(0) > 0)
    def _():
        sums[...] += total


def unpack_other_kernel(
    core_ref, part_ref, wq_ref, wk_ref, wv_ref, gain_ref, mine_sums, mine_tail, other_tail, *rest
):
    query, key, value, out, norm_gain, ffn_gain, router, const, const_vec, sums = rest[-10:]
    step = pl.program_id(0)
    total = unpack_rows(part_ref, (wq_ref, wk_ref, wv_ref), query, key, value, out)

    @pl.when(step == 0)
    def _():
        sums[...] = total

    @pl.when(step > 0)
    def _():
        sums[...] += total

    def finish(parts, tails):
        rows = sums.shape[1]
        each = rows // UNIT
        for c, part in enumerate(parts):
            at = slice(c * rows, (c + 1) * rows)
            norm_gain[at] = (part[0:1, :] / gain_ref[:, at])[0]
        for i in range(2 * rows // LANES):
            at = slice(i * LANES, (i + 1) * LANES)
            chunk = i % 3 * 2 * each
            small = tails[i // 3][chunk].astype(f32)
            rest = tails[i // 3][chunk + 1].astype(f32)
            router[:, at] = small[:TARGETS]
            for c in range(CONSTS):
                const[c, :, at] = small[TARGETS + 2 * c : TARGETS + 2 * c + 2]
            const_vec[:, at] = rest[:CONSTS]
            ffn_gain[at] = rest[CONSTS]

    last = step == pl.num_programs(0) - 1

    @pl.when(last & (core_ref[0] == 0))
    def _():
        finish((mine_sums, sums), (mine_tail, other_tail))

    @pl.when(last & (core_ref[0] != 0))
    def _():
        finish((sums, mine_sums), (other_tail, mine_tail))


def unpack(core, mine, swap, gain, w_query, w_key, w_value):
    width = w_query.shape[0]
    chunks = mine.shape[0]
    half = width // 2
    other = swap(mine)
    body = pl.BlockSpec((chunks, UNIT, LANES), lambda t, c: (0, t, 0))
    tail = pl.BlockSpec((chunks, PACK - 3 * UNIT, LANES), lambda t, c: (0, 3 * UNIT // (PACK - 3 * UNIT), 0))
    whole = lambda s: pl.BlockSpec(s, lambda t, c: (0,) * len(s))
    block = (half, PART // 2)
    by_core = lambda f: pl.BlockSpec(block, lambda t, c: (f(c[0]), t))
    grid = (2 * width // PART,)
    dense = [jax.ShapeDtypeStruct((width, width), f32)] * 4
    cost = pl.CostEstimate(
        flops=2 * width * width, bytes_accessed=12 * width * width, transcendentals=0
    )
    first = by_core(lambda c: c)
    *mats, sums = pl.pallas_call(
        unpack_mine_kernel,
        grid_spec=pltpu.PrefetchScalarGridSpec(
            num_scalar_prefetch=1,
            grid=grid,
            in_specs=[body, first, first, first],
            out_specs=[first] * 4 + [whole((8, half))],
        ),
        out_shape=dense + [jax.ShapeDtypeStruct((8, half), f32)],
        compiler_params=params(),
        cost_estimate=cost,
        name="unpack_mine",
    )(core, mine, w_query, w_key, w_value)
    second = by_core(lambda c: 1 - c)
    small = [(width,), (width,), (TARGETS, width), (CONSTS, 2, width), (CONSTS, width)]
    args = (core, other, w_query, w_key, w_value, gain, sums, mine, other)
    return pl.pallas_call(
        unpack_other_kernel,
        grid_spec=pltpu.PrefetchScalarGridSpec(
            num_scalar_prefetch=1,
            grid=grid,
            in_specs=[body, second, second, second, whole((1, width)), whole((8, half)), tail, tail]
            + [pl.BlockSpec(memory_space=pl.ANY)] * 4,
            out_specs=[second] * 4 + [whole(s) for s in small],
            scratch_shapes=[pltpu.VMEM((8, half), f32)],
        ),
        out_shape=dense + [jax.ShapeDtypeStruct(s, f32) for s in small],
        input_output_aliases={len(args) + i: i for i in range(4)},
        compiler_params=params(),
        cost_estimate=cost,
        name="unpack_other",
    )(*args, *mats)


def token_grad_kernel(x_ref, gain_ref, mine_ref, rtot_ref, *rest):
    parts, out_ref = rest[:-1], rest[-1]
    prompt = parts[0].shape[0]
    x = x_ref[...].astype(f32)
    scale = lax.rsqrt(jnp.mean(x * x, axis=1, keepdims=True) + norm_eps)
    mine = mine_ref[...]
    total = sum(p[...].astype(f32) for p in parts)
    grad = jnp.concatenate([mine[:prompt] + total, mine[prompt:]], axis=0) * gain_ref[...]
    xhat = x * scale
    grad = scale * (grad - xhat * jnp.mean(grad * xhat, axis=1, keepdims=True))
    out_ref[...] = (rtot_ref[...] + grad).astype(bf16)


def token_grad(x, gain, mine, rtot, parts):
    of_micro = lambda a: pl.BlockSpec((None,) + a.shape[1:], lambda m: (m, 0, 0))
    return pl.pallas_call(
        token_grad_kernel,
        grid=(x.shape[0],),
        in_specs=[of_micro(x), pl.BlockSpec(gain.shape, lambda m: (0, 0)), of_micro(mine), of_micro(rtot)]
        + [of_micro(p) for p in parts],
        out_specs=of_micro(x),
        out_shape=jax.ShapeDtypeStruct(x.shape, bf16),
        compiler_params=params(),
        cost_estimate=pl.CostEstimate(
            flops=16 * x.size, bytes_accessed=14 * x.size, transcendentals=0
        ),
        name="token_grad",
    )(x, gain, mine, rtot, *parts)


def add_kernel(*refs):
    refs[-1][...] = sum(r[...].astype(f32) for r in refs[:-1]).astype(bf16)


def add(arrays, steps=4):
    shape = arrays[0].shape
    block = pl.BlockSpec((shape[0] // steps,) + shape[1:], lambda t: (t,) + (0,) * (len(shape) - 1))
    return pl.pallas_call(
        add_kernel,
        grid=(steps,),
        in_specs=[block] * len(arrays),
        out_specs=block,
        out_shape=jax.ShapeDtypeStruct(shape, bf16),
        compiler_params=params(),
        cost_estimate=pl.CostEstimate(
            flops=arrays[0].size, bytes_accessed=2 * arrays[0].size, transcendentals=0
        ),
        name="add",
    )(*arrays)


def sum_copies_kernel(parts_ref, out_ref):
    total = sum(parts_ref[i].astype(f32) for i in range(parts_ref.shape[0])).astype(bf16)
    for i in range(out_ref.shape[0]):
        out_ref[i] = total


def sum_copies(parts, copies):
    return pl.pallas_call(
        sum_copies_kernel,
        out_shape=jax.ShapeDtypeStruct((copies,) + parts.shape[1:], bf16),
        compiler_params=params(),
        cost_estimate=pl.CostEstimate(
            flops=parts.size, bytes_accessed=2 * parts.size, transcendentals=0
        ),
        name="sum_copies",
    )(parts)


def swap_cores(rows):
    return lax.ppermute(rows, "core", [(0, 1), (1, 0)])


def exchange(blocks, axes):
    return lax.all_to_all(blocks, axes, split_axis=0, concat_axis=0, tiled=True)


def spread_out(piece, axes):
    count = lax.axis_size(axes)
    return exchange(jnp.broadcast_to(piece[None], (count,) + piece.shape), axes)


def ring_parts(parts, axis, dim):
    count = lax.axis_size(axis)
    me = lax.axis_index(axis)
    part = lambda i: lax.dynamic_index_in_dim(parts, i, dim, keepdims=False)
    out = [part(me)]
    for step in sorted(range(1, count), key=lambda s: -min(s, count - s)):
        ring = [(i, (i + step) % count) for i in range(count)]
        out.append(lax.ppermute(part((me + step) % count), axis, ring))
    return out


def after(value, *others):
    return lax.optimization_barrier((value, *others))[0]


def on_device(
    tokens, prior_logits, routes, drops, cont_lengths, norm_gain, w_query, w_key, w_value, w_out,
    ffn_gain, w_router, w_const, const_vec, w_gate, w_up, w_down, out_grad,
):
    micros, rows, width = tokens.shape[0], tokens.shape[3], tokens.shape[4]
    prompt = rows - CLEN
    cap = -(-(rows * 3 // 16) // 8) * 8
    chips = (lax.axis_size("context"), lax.axis_size("z"))
    half = chips[0] * chips[1] * prompt
    core = lax.axis_index("core").astype(jnp.int32)
    base = jnp.stack([lax.axis_index(("context", "z", "core")).astype(jnp.int32) * prompt, core])
    score_scale = 1.0 / math.sqrt(HEAD_SIZE)
    gain_one = norm_gain.astype(f32)
    gain_two = ffn_gain.astype(f32).reshape(1, width)

    gain_row = gain_one.reshape(1, width)
    core_arg = core.reshape(1)
    x = tokens[:, 0, 0]
    normed, copies, *own_rows = first_norm(x, norm_gain, chips[0] * chips[1])
    gathered = [exchange(copies, CHIPS)]
    gathered += [lax.all_gather(rows_m, CHIPS, axis=0) for rows_m in own_rows]

    wr = jnp.concatenate(
        [w_router] + [w_const[j] for j in range(CONSTS)]
        + [jnp.zeros((width, LANES - TARGETS - 2 * CONSTS), bf16)], axis=1,
    )
    cv = jnp.zeros((LANES, width), bf16).at[EXPERTS + 2 : EXPERTS + 2 + CONSTS].set(const_vec)
    wide = QUAD * HEAD_SIZE
    w_kv = jnp.concatenate(
        [w[:, g * wide : (g + 1) * wide] for g in range(HEADS // QUAD) for w in (w_key, w_value)], axis=1
    )
    row_ids = jnp.arange(rows, dtype=jnp.int32)
    og = out_grad[:, 0, 0]
    live = row_ids[None] < prompt + cont_lengths[:, 0]
    active = (1 - drops[:, 0, 0]) * live[..., None].astype(jnp.int32)
    eff = jnp.where(active > 0, routes[:, 0, 0], -1)
    efft = jnp.swapaxes(eff, 1, 2)
    prior = jnp.pad(prior_logits[:, 0, 0], ((0, 0), (0, 0), (0, LANES - TARGETS)))

    st = []
    for m in range(micros):
        s = {}
        if m:
            gathered[m] = after(gathered[m], st[m - 1]["attn"])
        else:
            gathered[m] = after(gathered[m], w_kv, wr, cv, eff, efft, prior, base, core_arg, gain_row, gain_two)
        s["near"] = gathered[m].reshape(half, width)
        s["far"] = swap_cores(s["near"])
        (
            s["attn"], s["lse"], s["q"], s["kv"],
            s["resid"], s["two"], s["ch"], send, s["sel"], s["selt"], s["gate"],
        ) = attn_fwd(
            base, normed, s["near"], s["far"], w_query, w_kv,
            x, w_out, gain_two, wr, prior, eff, efft, og, chips, cap, m,
        )
        s["recv"] = exchange(send.reshape(EXPERTS, cap, 2 * width), EXPERT).reshape(
            EXPERTS * cap, 2 * width
        )
        st.append(s)
    for s in st:
        ret, s["hid"], s["gg"], s["ug"] = experts(s["recv"], w_gate, w_up, w_down)
        s["ret"] = exchange(ret.reshape(EXPERTS, cap, 2 * width), EXPERT).reshape(
            EXPERTS * cap, 2 * width
        )
    wide_grads = expert_wgrad([(s["recv"], s["hid"], s["gg"], s["ug"]) for s in st])
    for m in range(micros - 1):
        st[m]["ret"] = after(st[m]["ret"], wide_grads)
    wide_sum = lax.psum(tuple(wide_grads), ("dp", "context"))

    parts, back_parts, before = [], [], ()
    for m, s in enumerate(st):
        dq, dkv, mixed, rtot, branch, dl, small = attn_bwd(
            base, s["q"], s["kv"], s["attn"], s["lse"],
            s["resid"], s["two"], s["ch"], eff, og, s["ret"], s["sel"], s["selt"], s["gate"],
            w_out, gain_two, wr, cv, chips, cap, m, before,
        )
        before = (mixed, rtot, dl)
        if m < micros - 1:
            st[m + 1]["ret"] = after(st[m + 1]["ret"], dkv)
        parts.append((s["near"], s["far"], normed, dq, s["attn"], branch, dkv, small))
        back_parts.append((dq, dkv))
    give, keep = wgrad(core_arg, parts)
    dkvs = [dkv for _, dkv in back_parts]
    dkvs[0] = after(dkvs[0], give)
    give_rows = back_proj(dkvs, w_kv, 1)
    come = after(swap_cores(give), give_rows)
    keep = (keep.astype(f32) + come.astype(f32)).astype(bf16)
    dense = exchange(keep.reshape((lax.axis_size(FIRST), -1) + keep.shape[1:]), FIRST)
    come = swap_cores(give_rows)
    keep = back_proj(dkvs, w_kv, 0)
    rows_sum = (keep.astype(f32) + come.astype(f32)).astype(bf16)
    dense = after(dense, rows_sum)
    rows_sum = rows_sum.reshape(micros, chips[1], chips[0] * prompt, width)
    rows_parts = ring_parts(rows_sum, "z", 1)
    rows_sum = add(rows_parts, micros)
    mine = own_proj(back_parts, w_query, w_kv)
    dense = after(jnp.sum(dense.astype(f32), axis=0).astype(bf16), mine)
    dense = sum_copies(exchange(dense, REST), lax.axis_size(ALL_CHIPS))
    dense = exchange(after(dense, wide_sum, rows_parts), ALL_CHIPS)
    wide_out = [g.astype(f32)[None] for g in wide_sum]
    prior_grad = jnp.swapaxes(dl, 1, 2)[:, :TARGETS]
    rows_sum, prior_grad, _ = lax.optimization_barrier((rows_sum, prior_grad, wide_out))
    parts = ring_parts(rows_sum.reshape(micros, chips[0], prompt, width), "context", 1)
    x_grad = token_grad(x, gain_row, mine, rtot, parts)
    dense = after(dense, parts)
    query, key, value, out, norm_gain, ffn_gain, router, const, vec = unpack(
        core_arg, dense, swap_cores, gain_row, w_query, w_key, w_value
    )
    return (
        mixed[:, None, None],
        x_grad[:, None, None],
        jnp.swapaxes(prior_grad, 1, 2)[:, None, None],
        norm_gain,
        query,
        key,
        value,
        out,
        ffn_gain,
        router.T,
        jnp.swapaxes(const, 1, 2),
        vec,
        *wide_out,
    )


def solution(mesh):
    shape = mesh.devices.shape
    split = Mesh(
        mesh.devices.reshape(shape[0], shape[1], shape[2] // 2, 2), ("dp", "context", "z", "core")
    )
    slot = P(None, "dp", ("context", "z", "core"), None, None)
    expert = P(("z", "core"), None, None)
    return jax.shard_map(
        on_device,
        mesh=split,
        in_specs=(
            slot, slot, slot, slot, P(None, "dp", ("context", "z", "core")),
            *(P(),) * 9,
            *(expert,) * 3,
            slot,
        ),
        out_specs=(slot, slot, slot, *(P(),) * 9, *(expert,) * 3),
        check_vma=False,
    )
```

```python
import functools
import math

import jax
import jax.numpy as jnp
from jax import lax
from jax.experimental import pallas as pl
from jax.experimental.pallas import tpu as pltpu
from jax.sharding import Mesh, PartitionSpec as P

HEADS = 12
HEAD_SIZE = 64
EXPERTS = 8
CONSTS = 2
TARGETS = 12
CLEN = 128
QUAD = 4
LANES = 128

norm_eps = 1e-05
very_low = -1e30
highest = lax.Precision.HIGHEST
f32 = jnp.float32
bf16 = jnp.bfloat16
CHIPS = ("z", "context")
FIRST, REST = "z", ("dp", "context")
ALL_CHIPS = (FIRST,) + REST
EXPERT = ("z", "core")


def dot_nn(left, right, **kw):
    return jnp.dot(left, right, preferred_element_type=f32, **kw)


def dot_nt(left, right, **kw):
    return lax.dot_general(left, right, (((1,), (1,)), ((), ())), preferred_element_type=f32, **kw)


def dot_tn(left, right, **kw):
    return lax.dot_general(left, right, (((0,), (0,)), ((), ())), preferred_element_type=f32, **kw)


def halves(wide):
    high = wide.astype(bf16)
    return high, (wide - high.astype(f32)).astype(bf16)


def iota(shape, dim):
    return lax.broadcasted_iota(jnp.int32, shape, dim)


def params():
    return pltpu.CompilerParams(vmem_limit_bytes=63_400_000)


def head_masks(dtype):
    lane_head = iota((1, QUAD * HEAD_SIZE), 1) // HEAD_SIZE
    return [(lane_head == h).astype(f32).astype(dtype) for h in range(QUAD)]


def spread(rows, prompt, dtype):
    masks = head_masks(dtype)
    return jnp.concatenate(
        [rows[:prompt] * m for m in masks] + [rows[prompt:] * m for m in masks], axis=0
    )


def gather_heads(stacked, prompt, dtype):
    masks = head_masks(dtype)
    top, low = 0.0, 0.0
    first = QUAD * prompt
    for h in range(QUAD):
        top = top + stacked[h * prompt : (h + 1) * prompt] * masks[h]
        low = low + stacked[first + h * CLEN : first + (h + 1) * CLEN] * masks[h]
    return jnp.concatenate([top, low], axis=0)


def first_norm_kernel(x_ref, gain_ref, normed_ref, copies_ref, *prompt_refs):
    x = x_ref[...].astype(f32)
    scale = lax.rsqrt(jnp.mean(x * x, axis=1, keepdims=True) + norm_eps)
    normed = (x * scale * gain_ref[...].astype(f32).reshape(1, -1)).astype(bf16)
    normed_ref[...] = normed
    micro = pl.program_id(0)
    prompt = copies_ref.shape[1]

    @pl.when(micro == 0)
    def _():
        for i in range(copies_ref.shape[0]):
            copies_ref[i] = normed[:prompt]

    for m, ref in enumerate(prompt_refs):

        @pl.when(micro == m + 1)
        def _():
            ref[...] = normed[:prompt]


def first_norm(x, gain, copies):
    micros, rows, width = x.shape
    of_micro = pl.BlockSpec((None, rows, width), lambda m: (m, 0, 0))
    shapes = [(copies, rows - CLEN, width)] + [(rows - CLEN, width)] * (micros - 1)
    whole = lambda s: pl.BlockSpec(s, lambda m: (0,) * len(s))
    return pl.pallas_call(
        first_norm_kernel,
        grid=(micros,),
        in_specs=[of_micro, whole((width,))],
        out_specs=[of_micro] + [whole(s) for s in shapes],
        out_shape=[jax.ShapeDtypeStruct(s, bf16) for s in [x.shape] + shapes],
        compiler_params=params(),
        cost_estimate=pl.CostEstimate(
            flops=8 * micros * rows * width, bytes_accessed=4 * micros * rows * width, transcendentals=0
        ),
        name="first_norm",
    )(x, gain)


def key_places(core, keys, prompt, chips, j):
    half = keys // 2
    other = jnp.where(j >= half, 1, 0)
    chip = (j - other * half) // prompt
    chip = (chip % chips[0]) * chips[1] + chip // chips[0]
    slot = chip * 2 + jnp.where(other > 0, 1 - core, core)
    return slot * prompt + (j & (prompt - 1))


def attn_fwd_kernel(
    base_ref, normed_ref, near_ref, far_ref, wq_ref, wkv_ref,
    x_ref, wout_ref, gain_ref, wr_ref, prior_ref, eff_ref, efft_ref, og_ref,
    o_ref, lse_ref, q_ref, kv_ref,
    resid_ref, two_ref, ch_ref, send_ref, sel_ref, selt_ref, gate_ref,
    *, chips, cap,
):
    g = pl.program_id(0)
    prompt = q_ref.shape[0] - CLEN
    keys = kv_ref.shape[0] - CLEN
    half = keys // 2
    wide = QUAD * HEAD_SIZE
    masks = head_masks(bf16)
    masks_f = head_masks(f32)
    ones = jnp.ones((8, LANES), f32)

    def to_row(column):
        spare = jnp.where(iota((column.shape[0], LANES), 1) == 0, column, 0.0)
        return dot_nt(ones, spare, precision=highest)

    q = dot_nn(normed_ref[...], wq_ref[...]).astype(bf16).astype(f32)
    q_ref[...] = (q * (1.0 / math.sqrt(HEAD_SIZE))).astype(bf16)
    for rows, at in ((near_ref, 0), (far_ref, half)):
        kv_ref[at : at + half] = dot_nn(rows[...], wkv_ref[...]).astype(bf16)
    kv_ref[keys:] = dot_nn(normed_ref[prompt:], wkv_ref[...]).astype(bf16)
    q_top, q_low = q_ref[:prompt], q_ref[prompt:]
    q_p = jnp.concatenate([q_top * m for m in masks], axis=0)
    s = dot_nt(q_p, kv_ref[:keys, :wide])
    limit = base_ref[0] + (iota((QUAD * prompt, 1), 0) & (prompt - 1))
    s = jnp.where(key_places(base_ref[1], keys, prompt, chips, iota((1, keys), 1)) <= limit, s, very_low)
    top = jnp.max(s, axis=1, keepdims=True)
    p = jnp.exp(s - top)
    total = jnp.sum(p, axis=1, keepdims=True)
    out = dot_nn(p.astype(bf16), kv_ref[:keys, wide:]) * (1.0 / total)
    lse_ref[:, : QUAD * prompt] = to_row(top + jnp.log(total))
    top_out = sum(out[h * prompt : (h + 1) * prompt] * masks_f[h] for h in range(QUAD))
    low_out = 0.0
    per = 2
    for part in range(QUAD // per):
        hs = range(part * per, (part + 1) * per)
        rows = per * CLEN
        q_c = jnp.concatenate([q_low * masks[h] for h in hs], axis=0)
        s = dot_nt(q_c, kv_ref[:keys, :wide])
        own = dot_nt(q_c, kv_ref[keys:, :wide])
        own = jnp.where(
            iota((1, CLEN), 1) <= (iota((rows, 1), 0) & (CLEN - 1)), own, very_low
        )
        top = jnp.maximum(
            jnp.max(s, axis=1, keepdims=True), jnp.max(own, axis=1, keepdims=True)
        )
        p = jnp.exp(s - top)
        p_own = jnp.exp(own - top)
        total = jnp.sum(p, axis=1, keepdims=True) + jnp.sum(p_own, axis=1, keepdims=True)
        out = dot_nn(p.astype(bf16), kv_ref[:keys, wide:])
        out = out + dot_nn(p_own.astype(bf16), kv_ref[keys:, wide:])
        out = out * (1.0 / total)
        at = QUAD * prompt + part * rows
        lse_ref[:, at : at + rows] = to_row(top + jnp.log(total))
        for i, h in enumerate(hs):
            low_out = low_out + out[i * CLEN : (i + 1) * CLEN] * masks_f[h]
    attn = jnp.concatenate([top_out, low_out], axis=0)
    o_ref[...] = attn
    branch = dot_nn(attn.astype(bf16), wout_ref[...])

    @pl.when(g == 0)
    def _():
        resid_ref[...] = x_ref[...].astype(f32) + branch

    @pl.when(g > 0)
    def _():
        resid_ref[...] += branch

    @pl.when(g == pl.num_programs(0) - 1)
    def _():
        route(
            gain_ref, wr_ref, prior_ref, eff_ref, efft_ref, og_ref,
            resid_ref, two_ref, ch_ref, send_ref, sel_ref, selt_ref, gate_ref, cap,
        )


def attn_fwd(
    base, normed, near, far, w_query, w_kv, x, w_out, gain, wr, prior, eff, efft, og,
    chips, cap, micro,
):
    rows, width = normed.shape[1:]
    half = near.shape[0]
    every = 2 * half + CLEN
    quads = HEADS // QUAD
    wide = QUAD * HEAD_SIZE
    slots = EXPERTS * cap
    col = lambda n, w=wide: pl.BlockSpec((n, w), lambda g, b: (0, g))
    whole = lambda n, w=width: pl.BlockSpec((n, w), lambda g, b: (0, 0))
    of_micro = lambda a: pl.BlockSpec((None,) + a.shape[1:], lambda g, b: (micro, 0, 0))
    routed = [
        ((rows, width), f32), ((rows, width), bf16), ((rows, LANES), f32), ((slots, 2 * width), bf16),
        ((slots, rows), bf16), ((rows, slots), bf16), ((slots, LANES), f32),
    ]
    return pl.pallas_call(
        functools.partial(attn_fwd_kernel, chips=chips, cap=cap),
        grid_spec=pltpu.PrefetchScalarGridSpec(
            num_scalar_prefetch=1,
            grid=(quads,),
            in_specs=[
                of_micro(normed), whole(half), whole(half), col(width), col(width, 2 * wide),
                of_micro(x), pl.BlockSpec((wide, width), lambda g, b: (g, 0)), whole(1), whole(width, LANES),
                of_micro(prior),
                of_micro(eff), of_micro(efft), of_micro(og),
            ],
            out_specs=[
                col(rows),
                pl.BlockSpec((None, 8, QUAD * rows), lambda g, b: (g, 0, 0)),
                col(rows),
                col(every, 2 * wide),
            ]
            + [whole(*s) for s, _ in routed],
        ),
        out_shape=[
            jax.ShapeDtypeStruct((rows, width), f32),
            jax.ShapeDtypeStruct((quads, 8, QUAD * rows), f32),
            jax.ShapeDtypeStruct((rows, width), bf16),
            jax.ShapeDtypeStruct((every, 2 * width), bf16),
        ]
        + [jax.ShapeDtypeStruct(s, t) for s, t in routed],
        compiler_params=params(),
        cost_estimate=pl.CostEstimate(
            flops=16 * rows * every * width + 4 * every * width * width,
            bytes_accessed=4 * every * width,
            transcendentals=rows * every * HEADS,
        ),
        name="attn_fwd",
    )(base, normed, near, far, w_query, w_kv, x, w_out, gain, wr, prior, eff, efft, og)


def attn_bwd_kernel(
    base_ref, q_ref, kv_ref, o_ref, lse_ref,
    resid_ref, two_ref, ch_ref, eff_ref, og_ref, ret_ref, sel_ref, selt_ref, gate_ref,
    wout_ref, gain_ref, wr_ref, cv_ref, *rest, block, chips, cap
):
    (
        dq_ref, dkv_ref, mixed_ref, rtot_ref, branch_ref, dl_ref, small_ref, qm, dom, dqt
    ) = rest[-10:]
    g = pl.program_id(0)

    @pl.when(g == 0)
    def _():
        combine(
            resid_ref, two_ref, ch_ref, eff_ref, og_ref, ret_ref, sel_ref, selt_ref, gate_ref,
            gain_ref, wr_ref, cv_ref,
            mixed_ref, rtot_ref, branch_ref, dl_ref, small_ref, cap,
        )

    do_now = dot_nt(branch_ref[...], wout_ref[...]).astype(bf16)
    prompt = q_ref.shape[0] - CLEN
    keys = kv_ref.shape[0] - CLEN
    wide = QUAD * HEAD_SIZE
    qm[...] = spread(q_ref[...], prompt, bf16)
    dom[...] = spread(do_now, prompt, bf16)
    prod = spread(do_now.astype(f32) * o_ref[...], prompt, f32)
    ones = jnp.ones((8, prod.shape[1]), bf16)
    prod_high, prod_low = halves(prod)
    delta = (dot_nt(ones, prod_high) + dot_nt(ones, prod_low))[0:1]
    lse = lse_ref[0:1, :]
    first = QUAD * prompt
    ahead = (iota((prompt, first), 1) & (prompt - 1)) - iota((prompt, first), 0)
    q_all, do_all = qm[...], dom[...]

    def one(rows, mask):
        kk, vv = kv_ref[rows, :wide], kv_ref[rows, wide:]
        p = jnp.exp(dot_nt(kk, q_all) - lse)
        p = mask(p)
        ds = p * (dot_nt(vv, do_all) - delta)
        pb, dsb = p.astype(bf16), ds.astype(bf16)
        dkv_ref[rows, :wide] = dot_nn(dsb, q_all).astype(bf16)
        dkv_ref[rows, wide:] = dot_nn(pb, do_all).astype(bf16)
        return dot_tn(kk, dsb)

    def own_mask(p):
        lane = iota((1, p.shape[1]), 1)
        own_row = jnp.where(lane < first, -1, (lane - first) & (CLEN - 1))
        return jnp.where(iota((CLEN, 1), 0) <= own_row, p, 0.0)

    dqt[...] = one(pl.ds(keys, CLEN), own_mask)

    def step(i, unused):
        at = i * block

        def mask(p):
            rows = []
            for r in range(0, block, prompt):
                gap = key_places(base_ref[1], keys, prompt, chips, at + r) - base_ref[0]
                rows.append(jnp.where(ahead >= gap, p[r : r + prompt, :first], 0.0))
            return jnp.concatenate([jnp.concatenate(rows, axis=0), p[:, first:]], axis=1)

        dqt[...] += one(pl.ds(at, block), mask)
        return unused

    for i in range(keys // block):
        step(i, 0)
    dq = gather_heads(dqt[...].T, prompt, f32)
    dq = (dq * (1.0 / math.sqrt(HEAD_SIZE))).astype(bf16)
    dq_ref[...] = dq


def attn_bwd(
    base, q, kv, o, lse, resid, two, ch, eff, og, ret, sel, selt, gate, w_out, gain, wr, cv,
    chips, cap, micro, before, block=1024,
):
    rows, width = q.shape
    every = kv.shape[0]
    quads = HEADS // QUAD
    wide = QUAD * HEAD_SIZE
    micros = eff.shape[0]
    col = lambda n, w=wide: pl.BlockSpec((n, w), lambda g, b: (0, g))
    whole = lambda a: pl.BlockSpec(a.shape, lambda g, b: (0, 0))
    of_micro = lambda a: pl.BlockSpec((None,) + a.shape[1:], lambda g, b: (micro, 0, 0))
    mixing = [
        jax.ShapeDtypeStruct((micros, rows, width), bf16),
        jax.ShapeDtypeStruct((micros, rows, width), f32),
        jax.ShapeDtypeStruct((rows, width), bf16),
        jax.ShapeDtypeStruct((micros, rows, LANES), f32),
        jax.ShapeDtypeStruct((24, width), f32),
    ]
    args = (base, q, kv, o, lse, resid, two, ch, eff, og, ret, sel, selt, gate, w_out, gain, wr, cv)
    return pl.pallas_call(
        functools.partial(
            attn_bwd_kernel, block=min(block, (every - CLEN) // 2), chips=chips, cap=cap
        ),
        grid_spec=pltpu.PrefetchScalarGridSpec(
            num_scalar_prefetch=1,
            grid=(quads,),
            in_specs=[
                col(rows), col(every, 2 * wide), col(rows),
                pl.BlockSpec((None, 8, QUAD * rows), lambda g, b: (g, 0, 0)),
                whole(resid), whole(two), whole(ch), of_micro(eff), of_micro(og), whole(ret),
                whole(sel), whole(selt), whole(gate), pl.BlockSpec((wide, width), lambda g, b: (g, 0)),
                whole(gain), whole(wr), whole(cv),
            ]
            + [pl.BlockSpec(memory_space=pl.ANY) for _ in before],
            out_specs=[col(rows), col(every, 2 * wide)]
            + [of_micro(a) if len(a.shape) == 3 else whole(a) for a in mixing],
            scratch_shapes=[
                pltpu.VMEM((QUAD * rows, wide), bf16),
                pltpu.VMEM((QUAD * rows, wide), bf16),
                pltpu.VMEM((wide, QUAD * rows), f32),
            ],
        ),
        out_shape=[
            jax.ShapeDtypeStruct((rows, width), bf16),
            jax.ShapeDtypeStruct((every, 2 * width), bf16),
        ]
        + mixing,
        input_output_aliases={len(args) + i: out for i, out in enumerate((2, 3, 5)[: len(before)])},
        compiler_params=params(),
        cost_estimate=pl.CostEstimate(
            flops=40 * rows * every * width,
            bytes_accessed=8 * every * width,
            transcendentals=rows * every * HEADS,
        ),
        name="attn_bwd",
    )(*args, *before)


def back_proj_kernel(*refs, count, steps):
    ins, (w_ref, out_ref) = refs[:count], refs[count:]
    for m in range(count):

        @pl.when(pl.program_id(0) // steps == m)
        def _():
            out_ref[...] = dot_nt(ins[m][...], w_ref[...]).astype(bf16)


def back_proj(dkvs, w_kv, which, steps=2):
    count = len(dkvs)
    width = dkvs[0].shape[1] // 2
    half = (dkvs[0].shape[0] - CLEN) // 2
    rows = half // steps
    at = lambda m: lambda t: (which * steps + jnp.clip(t - m * steps, 0, steps - 1), 0)
    return pl.pallas_call(
        functools.partial(back_proj_kernel, count=count, steps=steps),
        grid=(count * steps,),
        in_specs=[pl.BlockSpec((rows, 2 * width), at(m)) for m in range(count)]
        + [pl.BlockSpec(w_kv.shape, lambda t: (0, 0))],
        out_specs=pl.BlockSpec((None, rows, width), lambda t: (t // steps, t % steps, 0)),
        out_shape=jax.ShapeDtypeStruct((count, half, width), bf16),
        compiler_params=params(),
        cost_estimate=pl.CostEstimate(
            flops=count * half * width * width, bytes_accessed=2 * count * half * width, transcendentals=0
        ),
        name="back_proj",
    )(*dkvs, w_kv)


def own_proj_kernel(*refs, count):
    ins, (wq_ref, wkv_ref, out_ref) = refs[: 2 * count], refs[2 * count :]
    for m in range(count):
        dq = dot_nt(ins[2 * m][...], wq_ref[...])
        prompt = dq.shape[0] - CLEN
        out_ref[m, :prompt] = dq[:prompt]
        out_ref[m, prompt:] = dq[prompt:] + dot_nt(ins[2 * m + 1][...], wkv_ref[...])


def own_proj(parts, w_query, w_kv):
    rows, width = parts[0][0].shape
    every = parts[0][1].shape[0]
    whole = lambda n, w=width: pl.BlockSpec((n, w), lambda i: (0, 0))
    tail = pl.BlockSpec((CLEN, 2 * width), lambda i: (every // CLEN - 1, 0))
    count = len(parts)
    return pl.pallas_call(
        functools.partial(own_proj_kernel, count=count),
        grid=(1,),
        in_specs=[whole(rows), tail] * count + [whole(width), whole(width, 2 * width)],
        out_shape=jax.ShapeDtypeStruct((count, rows, width), f32),
        compiler_params=params(),
        cost_estimate=pl.CostEstimate(
            flops=6 * count * rows * width * width, bytes_accessed=6 * width * width, transcendentals=0
        ),
        name="own_proj",
    )(*[a for p in parts for a in p], w_query, w_kv)


def route(
    gain_ref, wr_ref, prior_ref, eff_ref, efft_ref, og_ref,
    resid_ref, two_ref, ch_ref, send_ref, sel_ref, selt_ref, gate_ref, cap,
):
    rows, width = resid_ref.shape
    slots = EXPERTS * cap
    resid = resid_ref[...]
    inv = lax.rsqrt(jnp.mean(resid * resid, axis=1, keepdims=True) + norm_eps)
    two = (resid * inv * gain_ref[...]).astype(bf16)
    two_ref[...] = two
    lane = iota((1, LANES), 1)
    logits = dot_nn(two, wr_ref[...]) + prior_ref[...]
    masked = jnp.where(lane < TARGETS, logits, very_low)
    e = jnp.exp(masked - jnp.max(masked, axis=1, keepdims=True))
    ch = e * (1.0 / jnp.sum(e, axis=1, keepdims=True))
    for j in range(CONSTS):
        at = TARGETS + 2 * j
        diff = logits[:, at + 1 : at + 2] - logits[:, at : at + 1]
        ch = jnp.where(lane == at, 1.0 / (1.0 + jnp.exp(diff)), ch)
        ch = jnp.where(lane == at + 1, 1.0 / (1.0 + jnp.exp(-diff)), ch)
    ch_ref[...] = ch
    target = iota((16, rows), 0)
    hot_t = ((target == efft_ref[0:1, :]) | (target == efft_ref[1:2, :])).astype(f32)
    before = (iota((rows, rows), 0) < iota((rows, rows), 1)).astype(f32).astype(bf16)
    rank_t = dot_nn(hot_t.astype(bf16), before)
    rank_t = jnp.where(hot_t > 0.0, rank_t, -1.0)
    place = iota((cap, 1), 0).astype(f32)
    sel = jnp.concatenate(
        [(place == rank_t[i : i + 1, :]).astype(f32) for i in range(EXPERTS)], axis=0
    )
    sel_b = sel.astype(bf16)
    sel_ref[...] = sel_b
    hot = ((lane == eff_ref[:, 0:1]) | (lane == eff_ref[:, 1:2])).astype(f32)
    after = (iota((rows, rows), 0) > iota((rows, rows), 1)).astype(f32).astype(bf16)
    rank = dot_nn(after, hot.astype(bf16))
    rank = jnp.where(hot > 0.0, rank, -1.0)
    slot = iota((1, slots), 1)
    widen = (slot // cap == iota((LANES, 1), 0)).astype(f32).astype(bf16)
    rank_s = dot_nn(rank.astype(bf16), widen)
    selt_ref[...] = (rank_s == (slot % cap).astype(f32)).astype(f32).astype(bf16)
    ch_high, ch_low = halves(ch)
    ch_s = dot_nn(sel_b, ch_high) + dot_nn(sel_b, ch_low)
    of_slot = iota((slots, 1), 0) // cap
    gate = jnp.sum(jnp.where(lane == of_slot, ch_s, 0.0), axis=1, keepdims=True)
    gate_ref[...] = jnp.broadcast_to(gate, gate_ref.shape)
    send_ref[:, :width] = dot_nn(sel_b, two).astype(bf16)
    send_ref[:, width:] = (gate * dot_nn(sel_b, og_ref[...])).astype(bf16)


def expert_kernel(
    x_ref, g_ref, wg_ref, wu_ref, wd_ref, out_ref, hid_ref, gg_ref, ug_ref, fwd, back
):
    step = pl.program_id(0)
    width = x_ref.shape[1]

    @pl.when(step == 0)
    def _():
        fwd[...] = jnp.zeros_like(fwd)
        back[...] = jnp.zeros_like(back)

    x, g = x_ref[...], g_ref[...]
    gate = dot_nn(x, wg_ref[...])
    up = dot_nn(x, wu_ref[...])
    hid_grad = dot_nt(g, wd_ref[...])
    sig = 1.0 / (1.0 + jnp.exp(-gate))
    act = gate * sig
    hid = (act * up).astype(bf16)
    gg = (hid_grad * up * (sig + act * (1.0 - sig))).astype(bf16)
    ug = (hid_grad * act).astype(bf16)
    hid_ref[...] = hid
    gg_ref[...] = gg
    ug_ref[...] = ug
    fwd[...] += dot_nn(hid, wd_ref[...])
    back[...] += dot_nt(gg, wg_ref[...]) + dot_nt(ug, wu_ref[...])

    @pl.when(step == pl.num_programs(0) - 1)
    def _():
        out_ref[:, :width] = fwd[...].astype(bf16)
        out_ref[:, width:] = back[...].astype(bf16)


def experts(rows_in, w_gate, w_up, w_down, tile=512):
    rows = rows_in.shape[0]
    width = rows_in.shape[1] // 2
    hidden = w_gate.shape[2]
    half = lambda i: pl.BlockSpec((rows, width), lambda t, i=i: (0, i))
    inner = pl.BlockSpec((None, width, tile), lambda t: (0, 0, t))
    mid = pl.BlockSpec((rows, tile), lambda t: (0, t))
    return pl.pallas_call(
        expert_kernel,
        grid=(hidden // tile,),
        in_specs=[half(0), half(1), inner, inner, pl.BlockSpec((None, tile, width), lambda t: (0, t, 0))],
        out_specs=[pl.BlockSpec((rows, 2 * width), lambda t: (0, 0)), mid, mid, mid],
        out_shape=[jax.ShapeDtypeStruct((rows, 2 * width), bf16)]
        + [jax.ShapeDtypeStruct((rows, hidden), bf16)] * 3,
        scratch_shapes=[pltpu.VMEM((rows, width), f32), pltpu.VMEM((rows, width), f32)],
        compiler_params=params(),
        cost_estimate=pl.CostEstimate(
            flops=14 * rows * width * hidden,
            bytes_accessed=6 * width * hidden,
            transcendentals=rows * hidden,
        ),
        name="experts",
    )(rows_in, rows_in, w_gate, w_up, w_down)


def expert_wgrad_kernel(*refs, count):
    ins, (dg_ref, du_ref, dd_ref) = refs[: 5 * count], refs[5 * count :]
    x, g, hid, gg, ug = (
        jnp.concatenate([ins[5 * m + i][...] for m in range(count)], axis=0) for i in range(5)
    )
    dg_ref[...] = dot_tn(x, gg).astype(bf16)
    du_ref[...] = dot_tn(x, ug).astype(bf16)
    dd_ref[...] = dot_tn(hid, g).astype(bf16)


def expert_wgrad(parts, tile=512):
    rows = parts[0][0].shape[0]
    width = parts[0][0].shape[1] // 2
    hidden = parts[0][1].shape[1]
    half = lambda i: pl.BlockSpec((rows, width), lambda t, i=i: (0, i))
    mid = pl.BlockSpec((rows, tile), lambda t: (0, t))
    specs, args = [], []
    for rows_in, hid, gg, ug in parts:
        specs += [half(0), half(1), mid, mid, mid]
        args += [rows_in, rows_in, hid, gg, ug]
    inner = pl.BlockSpec((width, tile), lambda t: (0, t))
    return pl.pallas_call(
        functools.partial(expert_wgrad_kernel, count=len(parts)),
        grid=(hidden // tile,),
        in_specs=specs,
        out_specs=[inner, inner, pl.BlockSpec((tile, width), lambda t: (t, 0))],
        out_shape=[
            jax.ShapeDtypeStruct((width, hidden), bf16),
            jax.ShapeDtypeStruct((width, hidden), bf16),
            jax.ShapeDtypeStruct((hidden, width), bf16),
        ],
        compiler_params=params(),
        cost_estimate=pl.CostEstimate(
            flops=6 * len(parts) * rows * width * hidden,
            bytes_accessed=6 * width * hidden,
            transcendentals=0,
        ),
        name="expert_wgrad",
    )(*args)


def combine(
    resid_ref, two_ref, ch_ref, eff_ref, og_ref, ret_ref, sel_ref, selt_ref, gate_ref,
    gain_ref, wr_ref, cv_ref,
    mixed_ref, rtot_ref, branch_ref, dl_ref, small_ref, cap,
):
    rows, width = resid_ref.shape
    slots = EXPERTS * cap
    lane = iota((1, LANES), 1)
    resid, two_b, ch = resid_ref[...], two_ref[...], ch_ref[...]
    two = two_b.astype(f32)
    og_b = og_ref[...]
    og = og_b.astype(f32)
    eo = ret_ref[:, :width].astype(f32)
    sel, selt = sel_ref[...], selt_ref[...]
    hot = ((lane == eff_ref[:, 0:1]) | (lane == eff_ref[:, 1:2])).astype(f32)
    dgate = jnp.sum(dot_nn(sel, og_b) * eo, axis=1, keepdims=True)
    by_target = jnp.where(lane == iota((slots, 1), 0) // cap, dgate, 0.0)
    by_high, by_low = halves(by_target)
    dval = dot_nn(selt, by_high) + dot_nn(selt, by_low)
    self_dot = jnp.sum(og * two, axis=1, keepdims=True)
    cv_dot = dot_nt(og_b, cv_ref[...])
    gates = ch * hot
    keep = gates[:, EXPERTS + 1 : EXPERTS + 2]
    dval = jnp.where(lane == EXPERTS + 1, self_dot, dval)
    mixed = resid + dot_nn(selt, (gate_ref[:, 0:1] * eo).astype(bf16))
    dl_const = jnp.zeros((rows, LANES), f32)
    coef_cv = jnp.zeros((rows, LANES), f32)
    for j in range(CONSTS):
        e, at = EXPERTS + 2 + j, TARGETS + 2 * j
        a0, a1 = ch[:, at : at + 1], ch[:, at + 1 : at + 2]
        gate = gates[:, e : e + 1]
        with_cv = cv_dot[:, e : e + 1]
        dval = jnp.where(lane == e, a0 * self_dot + a1 * with_cv, dval)
        keep = keep + gate * a0
        mixed = mixed + (gate * a1) * cv_ref[e : e + 1, :].astype(f32)
        coef_cv = jnp.where(lane == TARGETS + 2 * CONSTS + j, gate * a1, coef_cv)
        da0, da1 = gate * self_dot, gate * with_cv
        mean = a0 * da0 + a1 * da1
        dl_const = jnp.where(lane == at, a0 * (da0 - mean), dl_const)
        dl_const = jnp.where(lane == at + 1, a1 * (da1 - mean), dl_const)
    mixed = mixed + keep * two
    mixed_ref[...] = mixed.astype(bf16)
    ch = jnp.where(lane < TARGETS, ch, 0.0)
    dch = hot * dval
    dl = ch * (dch - jnp.sum(ch * dch, axis=1, keepdims=True)) + dl_const
    dl_ref[...] = dl
    dl_hi, dl_lo = halves(dl)
    cc_hi, cc_lo = halves(coef_cv)
    small = dot_tn(dl_hi, two_b) + dot_tn(dl_lo, two_b) + dot_tn(cc_hi, og_b) + dot_tn(cc_lo, og_b)
    two_grad = (
        keep * og
        + dot_nt(dl_hi, wr_ref[...])
        + dot_nt(dl_lo, wr_ref[...])
        + dot_nn(selt, ret_ref[:, width:])
    )
    inv = lax.rsqrt(jnp.mean(resid * resid, axis=1, keepdims=True) + norm_eps)
    xhat = resid * inv
    gain_grad = jnp.sum(two_grad * xhat, axis=0, keepdims=True)
    small_ref[...] = jnp.where(
        iota((small_ref.shape[0], 1), 0) == TARGETS + 3 * CONSTS, gain_grad, small[: small_ref.shape[0]]
    )
    scaled = two_grad * gain_ref[...]
    rtot = og + inv * (scaled - xhat * jnp.mean(scaled * xhat, axis=1, keepdims=True))
    rtot_ref[...] = rtot
    branch_ref[...] = rtot.astype(bf16)


UNIT = 48
PACK = 160
PART = 512


def units(grad):
    low = grad.astype(bf16)
    each = low.shape[0] // UNIT // 2
    for j in range(low.shape[1] // LANES):
        for k in range(2 * each):
            unit = low[k * UNIT : (k + 1) * UNIT, j * LANES : (j + 1) * LANES]
            yield j, k // each, k % each, unit


def wgrad_kernel(core_ref, *refs, count):
    ins, (give_ref, keep_ref, rows, sems) = refs[: 8 * count], refs[8 * count :]
    t = pl.program_id(0)
    part = lambda i: [ins[8 * m + i] for m in range(count)]
    nears, fars, normeds, dqs, attns, branches, dkvs, smalls = (part(i) for i in range(8))
    copies = [
        pltpu.make_async_copy(ref, rows.at[m, i], sems.at[2 * m + i])
        for m in range(count)
        for i, ref in enumerate((nears[m], fars[m]))
    ]

    def by_core(fill):
        @pl.when(core_ref[0] == 0)
        def _():
            fill((keep_ref, give_ref))

        @pl.when(core_ref[0] != 0)
        def _():
            fill((give_ref, keep_ref))

    @pl.when(t == 0)
    def _():
        for copy in copies:
            copy.start()
        stack = lambda refs: jnp.concatenate([r[...].astype(bf16) for r in refs], axis=0)
        query = dot_tn(stack(normeds), stack(dqs))
        out = dot_tn(stack(attns), stack(branches))
        each = query.shape[0] // UNIT // 2
        half = PART // 2
        small = sum(r[...] for r in smalls)
        small = jnp.concatenate([small, jnp.zeros((8, small.shape[1]), f32)], axis=0).astype(bf16)

        def fill(cores):
            for step in range(query.shape[1] // half):
                at = slice(step * half, (step + 1) * half)
                for j, c, k, unit in units(jnp.concatenate([query[:, at], out[:, at]], axis=1)):
                    cores[c][2 * j * each + k, step * UNIT : (step + 1) * UNIT, :] = unit
            for ref in cores:
                ref[:, 3 * UNIT :, :] = jnp.zeros((ref.shape[0], PACK - 3 * UNIT, LANES), bf16)
            for i in range(small.shape[1] // LANES):
                block = small[:, i * LANES : (i + 1) * LANES]
                ref, chunk = cores[i // 3], i % 3 * 2 * each
                ref[chunk, 3 * UNIT : 3 * UNIT + 16, :] = block[:16]
                ref[chunk + 1, 3 * UNIT : 3 * UNIT + 16, :] = block[16:]

        by_core(fill)

    @pl.when(t == 1)
    def _():
        for copy in copies:
            copy.wait()

    @pl.when(t > 0)
    def _():
        grad = 0.0
        for m in range(count):
            half = rows.shape[2]
            grad = grad + dot_tn(rows[m, 0], dkvs[m][:half])
            grad = grad + dot_tn(rows[m, 1], dkvs[m][half : 2 * half])
            own = normeds[m].shape[0] - CLEN
            grad = grad + dot_tn(normeds[m][own:], dkvs[m][2 * half :])

        def fill(cores):
            each = grad.shape[0] // UNIT // 2
            at = pl.ds(pl.multiple_of((t - 1) * UNIT, 16), UNIT)
            for j, c, k, unit in units(grad):
                cores[c][(2 * j + 1) * each + k, at, :] = unit

        by_core(fill)


def wgrad(core, parts):
    rows, width = parts[0][3].shape
    half = parts[0][0].shape[0]
    whole = lambda n: pl.BlockSpec((n, width), lambda t, c: (0, 0))
    hbm = pl.BlockSpec(memory_space=pl.ANY)
    specs, args = [], []
    for m, p in enumerate(parts):
        specs += [
            hbm, hbm, pl.BlockSpec((None, rows, width), lambda t, c, m=m: (m, 0, 0)),
            whole(rows), whole(rows), whole(rows),
            pl.BlockSpec((2 * half + CLEN, PART), lambda t, c: (0, jnp.maximum(t - 1, 0))), whole(24),
        ]
        args += list(p)
    count = len(parts)
    shape = (2 * PART // LANES * (width // UNIT // 2), PACK, LANES)
    return pl.pallas_call(
        functools.partial(wgrad_kernel, count=count),
        grid_spec=pltpu.PrefetchScalarGridSpec(
            num_scalar_prefetch=1,
            grid=(1 + 2 * width // PART,),
            in_specs=specs,
            out_specs=[pl.BlockSpec(shape, lambda t, c: (0, 0, 0))] * 2,
            scratch_shapes=[
                pltpu.VMEM((count, 2, half, width), bf16),
                pltpu.SemaphoreType.DMA((2 * count,)),
            ],
        ),
        out_shape=[jax.ShapeDtypeStruct(shape, bf16)] * 2,
        compiler_params=params(),
        cost_estimate=pl.CostEstimate(
            flops=4 * count * (2 * half + CLEN + rows) * width * width,
            bytes_accessed=12 * count * half * width,
            transcendentals=0,
        ),
        name="wgrad",
    )(core, *args)


def unpack_rows(part_ref, weights, query, key, value, out):
    rows = query.shape[0]
    each = rows // UNIT
    cols = PART // 2 // LANES
    for first, refs in ((0, (query, out)), (each, (key, value))):
        for j in range(2 * cols):
            ref, at = refs[j // cols], (j % cols) * LANES
            for k in range(each):
                ref[k * UNIT : (k + 1) * UNIT, at : at + LANES] = part_ref[
                    2 * j * each + first + k
                ].astype(f32)
    total = 0.0
    for grad, w_ref in zip((query, key, value), weights):
        prod = grad[...] * w_ref[...].astype(f32)
        total = total + sum(prod[:, i * LANES : (i + 1) * LANES] for i in range(cols))
    high, low = halves(total)
    ones = jnp.ones((8, LANES), bf16)
    return dot_nt(ones, high) + dot_nt(ones, low)


def unpack_mine_kernel(core_ref, part_ref, wq_ref, wk_ref, wv_ref, query, key, value, out, sums):
    total = unpack_rows(part_ref, (wq_ref, wk_ref, wv_ref), query, key, value, out)

    @pl.when(pl.program_id(0) == 0)
    def _():
        sums[...] = total

    @pl.when(pl.program_id(0) > 0)
    def _():
        sums[...] += total


def unpack_other_kernel(
    core_ref, part_ref, wq_ref, wk_ref, wv_ref, gain_ref, mine_sums, mine_tail, other_tail, *rest
):
    query, key, value, out, norm_gain, ffn_gain, router, const, const_vec, sums = rest[-10:]
    step = pl.program_id(0)
    total = unpack_rows(part_ref, (wq_ref, wk_ref, wv_ref), query, key, value, out)

    @pl.when(step == 0)
    def _():
        sums[...] = total

    @pl.when(step > 0)
    def _():
        sums[...] += total

    def finish(parts, tails):
        rows = sums.shape[1]
        each = rows // UNIT
        for c, part in enumerate(parts):
            at = slice(c * rows, (c + 1) * rows)
            norm_gain[at] = (part[0:1, :] / gain_ref[:, at])[0]
        for i in range(2 * rows // LANES):
            at = slice(i * LANES, (i + 1) * LANES)
            chunk = i % 3 * 2 * each
            small = tails[i // 3][chunk].astype(f32)
            rest = tails[i // 3][chunk + 1].astype(f32)
            router[:, at] = small[:TARGETS]
            for c in range(CONSTS):
                const[c, :, at] = small[TARGETS + 2 * c : TARGETS + 2 * c + 2]
            const_vec[:, at] = rest[:CONSTS]
            ffn_gain[at] = rest[CONSTS]

    last = step == pl.num_programs(0) - 1

    @pl.when(last & (core_ref[0] == 0))
    def _():
        finish((mine_sums, sums), (mine_tail, other_tail))

    @pl.when(last & (core_ref[0] != 0))
    def _():
        finish((sums, mine_sums), (other_tail, mine_tail))


def unpack(core, mine, swap, gain, w_query, w_key, w_value):
    width = w_query.shape[0]
    chunks = mine.shape[0]
    half = width // 2
    other = swap(mine)
    body = pl.BlockSpec((chunks, UNIT, LANES), lambda t, c: (0, t, 0))
    tail = pl.BlockSpec((chunks, PACK - 3 * UNIT, LANES), lambda t, c: (0, 3 * UNIT // (PACK - 3 * UNIT), 0))
    whole = lambda s: pl.BlockSpec(s, lambda t, c: (0,) * len(s))
    block = (half, PART // 2)
    by_core = lambda f: pl.BlockSpec(block, lambda t, c: (f(c[0]), t))
    grid = (2 * width // PART,)
    dense = [jax.ShapeDtypeStruct((width, width), f32)] * 4
    cost = pl.CostEstimate(
        flops=2 * width * width, bytes_accessed=12 * width * width, transcendentals=0
    )
    first = by_core(lambda c: c)
    *mats, sums = pl.pallas_call(
        unpack_mine_kernel,
        grid_spec=pltpu.PrefetchScalarGridSpec(
            num_scalar_prefetch=1,
            grid=grid,
            in_specs=[body, first, first, first],
            out_specs=[first] * 4 + [whole((8, half))],
        ),
        out_shape=dense + [jax.ShapeDtypeStruct((8, half), f32)],
        compiler_params=params(),
        cost_estimate=cost,
        name="unpack_mine",
    )(core, mine, w_query, w_key, w_value)
    second = by_core(lambda c: 1 - c)
    small = [(width,), (width,), (TARGETS, width), (CONSTS, 2, width), (CONSTS, width)]
    args = (core, other, w_query, w_key, w_value, gain, sums, mine, other)
    return pl.pallas_call(
        unpack_other_kernel,
        grid_spec=pltpu.PrefetchScalarGridSpec(
            num_scalar_prefetch=1,
            grid=grid,
            in_specs=[body, second, second, second, whole((1, width)), whole((8, half)), tail, tail]
            + [pl.BlockSpec(memory_space=pl.ANY)] * 4,
            out_specs=[second] * 4 + [whole(s) for s in small],
            scratch_shapes=[pltpu.VMEM((8, half), f32)],
        ),
        out_shape=dense + [jax.ShapeDtypeStruct(s, f32) for s in small],
        input_output_aliases={len(args) + i: i for i in range(4)},
        compiler_params=params(),
        cost_estimate=cost,
        name="unpack_other",
    )(*args, *mats)


def token_grad_kernel(x_ref, gain_ref, mine_ref, rtot_ref, *rest):
    parts, out_ref = rest[:-1], rest[-1]
    prompt = parts[0].shape[0]
    x = x_ref[...].astype(f32)
    scale = lax.rsqrt(jnp.mean(x * x, axis=1, keepdims=True) + norm_eps)
    mine = mine_ref[...]
    total = sum(p[...].astype(f32) for p in parts)
    grad = jnp.concatenate([mine[:prompt] + total, mine[prompt:]], axis=0) * gain_ref[...]
    xhat = x * scale
    grad = scale * (grad - xhat * jnp.mean(grad * xhat, axis=1, keepdims=True))
    out_ref[...] = (rtot_ref[...] + grad).astype(bf16)


def token_grad(x, gain, mine, rtot, parts):
    of_micro = lambda a: pl.BlockSpec((None,) + a.shape[1:], lambda m: (m, 0, 0))
    return pl.pallas_call(
        token_grad_kernel,
        grid=(x.shape[0],),
        in_specs=[of_micro(x), pl.BlockSpec(gain.shape, lambda m: (0, 0)), of_micro(mine), of_micro(rtot)]
        + [of_micro(p) for p in parts],
        out_specs=of_micro(x),
        out_shape=jax.ShapeDtypeStruct(x.shape, bf16),
        compiler_params=params(),
        cost_estimate=pl.CostEstimate(
            flops=16 * x.size, bytes_accessed=14 * x.size, transcendentals=0
        ),
        name="token_grad",
    )(x, gain, mine, rtot, *parts)


def add_kernel(*refs):
    refs[-1][...] = sum(r[...].astype(f32) for r in refs[:-1]).astype(bf16)


def add(arrays, steps=4):
    shape = arrays[0].shape
    block = pl.BlockSpec((shape[0] // steps,) + shape[1:], lambda t: (t,) + (0,) * (len(shape) - 1))
    return pl.pallas_call(
        add_kernel,
        grid=(steps,),
        in_specs=[block] * len(arrays),
        out_specs=block,
        out_shape=jax.ShapeDtypeStruct(shape, bf16),
        compiler_params=params(),
        cost_estimate=pl.CostEstimate(
            flops=arrays[0].size, bytes_accessed=2 * arrays[0].size, transcendentals=0
        ),
        name="add",
    )(*arrays)


def sum_copies_kernel(parts_ref, out_ref):
    total = sum(parts_ref[i].astype(f32) for i in range(parts_ref.shape[0])).astype(bf16)
    for i in range(out_ref.shape[0]):
        out_ref[i] = total


def sum_copies(parts, copies):
    return pl.pallas_call(
        sum_copies_kernel,
        out_shape=jax.ShapeDtypeStruct((copies,) + parts.shape[1:], bf16),
        compiler_params=params(),
        cost_estimate=pl.CostEstimate(
            flops=parts.size, bytes_accessed=2 * parts.size, transcendentals=0
        ),
        name="sum_copies",
    )(parts)


def swap_cores(rows):
    return lax.ppermute(rows, "core", [(0, 1), (1, 0)])


def exchange(blocks, axes):
    return lax.all_to_all(blocks, axes, split_axis=0, concat_axis=0, tiled=True)


def spread_out(piece, axes):
    count = lax.axis_size(axes)
    return exchange(jnp.broadcast_to(piece[None], (count,) + piece.shape), axes)


def ring_parts(parts, axis, dim):
    count = lax.axis_size(axis)
    me = lax.axis_index(axis)
    part = lambda i: lax.dynamic_index_in_dim(parts, i, dim, keepdims=False)
    out = [part(me)]
    for step in sorted(range(1, count), key=lambda s: -min(s, count - s)):
        ring = [(i, (i + step) % count) for i in range(count)]
        out.append(lax.ppermute(part((me + step) % count), axis, ring))
    return out


def after(value, *others):
    return lax.optimization_barrier((value, *others))[0]


def on_device(
    tokens, prior_logits, routes, drops, cont_lengths, norm_gain, w_query, w_key, w_value, w_out,
    ffn_gain, w_router, w_const, const_vec, w_gate, w_up, w_down, out_grad,
):
    micros, rows, width = tokens.shape[0], tokens.shape[3], tokens.shape[4]
    prompt = rows - CLEN
    cap = -(-(rows * 3 // 16) // 8) * 8
    chips = (lax.axis_size("context"), lax.axis_size("z"))
    half = chips[0] * chips[1] * prompt
    core = lax.axis_index("core").astype(jnp.int32)
    base = jnp.stack([lax.axis_index(("context", "z", "core")).astype(jnp.int32) * prompt, core])
    score_scale = 1.0 / math.sqrt(HEAD_SIZE)
    gain_one = norm_gain.astype(f32)
    gain_two = ffn_gain.astype(f32).reshape(1, width)

    gain_row = gain_one.reshape(1, width)
    core_arg = core.reshape(1)
    x = tokens[:, 0, 0]
    normed, copies, *own_rows = first_norm(x, norm_gain, chips[0] * chips[1])
    gathered = [exchange(copies, CHIPS)]
    gathered += [lax.all_gather(rows_m, CHIPS, axis=0) for rows_m in own_rows]

    wr = jnp.concatenate(
        [w_router] + [w_const[j] for j in range(CONSTS)]
        + [jnp.zeros((width, LANES - TARGETS - 2 * CONSTS), bf16)], axis=1,
    )
    cv = jnp.zeros((LANES, width), bf16).at[EXPERTS + 2 : EXPERTS + 2 + CONSTS].set(const_vec)
    wide = QUAD * HEAD_SIZE
    w_kv = jnp.concatenate(
        [w[:, g * wide : (g + 1) * wide] for g in range(HEADS // QUAD) for w in (w_key, w_value)], axis=1
    )
    row_ids = jnp.arange(rows, dtype=jnp.int32)
    og = out_grad[:, 0, 0]
    live = row_ids[None] < prompt + cont_lengths[:, 0]
    active = (1 - drops[:, 0, 0]) * live[..., None].astype(jnp.int32)
    eff = jnp.where(active > 0, routes[:, 0, 0], -1)
    efft = jnp.swapaxes(eff, 1, 2)
    prior = jnp.pad(prior_logits[:, 0, 0], ((0, 0), (0, 0), (0, LANES - TARGETS)))

    st = []
    for m in range(micros):
        s = {}
        if m:
            gathered[m] = after(gathered[m], st[m - 1]["attn"])
        else:
            gathered[m] = after(gathered[m], w_kv, wr, cv, eff, efft, prior, base, core_arg, gain_row, gain_two)
        s["near"] = gathered[m].reshape(half, width)
        s["far"] = swap_cores(s["near"])
        (
            s["attn"], s["lse"], s["q"], s["kv"],
            s["resid"], s["two"], s["ch"], send, s["sel"], s["selt"], s["gate"],
        ) = attn_fwd(
            base, normed, s["near"], s["far"], w_query, w_kv,
            x, w_out, gain_two, wr, prior, eff, efft, og, chips, cap, m,
        )
        s["recv"] = exchange(send.reshape(EXPERTS, cap, 2 * width), EXPERT).reshape(
            EXPERTS * cap, 2 * width
        )
        st.append(s)
    for s in st:
        ret, s["hid"], s["gg"], s["ug"] = experts(s["recv"], w_gate, w_up, w_down)
        s["ret"] = exchange(ret.reshape(EXPERTS, cap, 2 * width), EXPERT).reshape(
            EXPERTS * cap, 2 * width
        )
    wide_grads = expert_wgrad([(s["recv"], s["hid"], s["gg"], s["ug"]) for s in st])
    for m in range(micros - 1):
        st[m]["ret"] = after(st[m]["ret"], wide_grads)
    wide_sum = lax.psum(tuple(wide_grads), ("dp", "context"))

    parts, back_parts, before = [], [], ()
    for m, s in enumerate(st):
        dq, dkv, mixed, rtot, branch, dl, small = attn_bwd(
            base, s["q"], s["kv"], s["attn"], s["lse"],
            s["resid"], s["two"], s["ch"], eff, og, s["ret"], s["sel"], s["selt"], s["gate"],
            w_out, gain_two, wr, cv, chips, cap, m, before,
        )
        before = (mixed, rtot, dl)
        if m < micros - 1:
            st[m + 1]["ret"] = after(st[m + 1]["ret"], dkv)
        parts.append((s["near"], s["far"], normed, dq, s["attn"], branch, dkv, small))
        back_parts.append((dq, dkv))
    give, keep = wgrad(core_arg, parts)
    dkvs = [dkv for _, dkv in back_parts]
    dkvs[0] = after(dkvs[0], give)
    give_rows = back_proj(dkvs, w_kv, 1)
    come = after(swap_cores(give), give_rows)
    keep = (keep.astype(f32) + come.astype(f32)).astype(bf16)
    dense = exchange(keep.reshape((lax.axis_size(FIRST), -1) + keep.shape[1:]), FIRST)
    come = swap_cores(give_rows)
    keep = back_proj(dkvs, w_kv, 0)
    rows_sum = (keep.astype(f32) + come.astype(f32)).astype(bf16)
    dense = after(dense, rows_sum)
    rows_sum = rows_sum.reshape(micros, chips[1], chips[0] * prompt, width)
    rows_parts = ring_parts(rows_sum, "z", 1)
    rows_sum = add(rows_parts, micros)
    mine = own_proj(back_parts, w_query, w_kv)
    dense = after(jnp.sum(dense.astype(f32), axis=0).astype(bf16), mine)
    dense = sum_copies(exchange(dense, REST), lax.axis_size(ALL_CHIPS))
    dense = exchange(after(dense, wide_sum, rows_parts), ALL_CHIPS)
    wide_out = [g.astype(f32)[None] for g in wide_sum]
    prior_grad = jnp.swapaxes(dl, 1, 2)[:, :TARGETS]
    rows_sum, prior_grad, _ = lax.optimization_barrier((rows_sum, prior_grad, wide_out))
    parts = ring_parts(rows_sum.reshape(micros, chips[0], prompt, width), "context", 1)
    x_grad = token_grad(x, gain_row, mine, rtot, parts)
    dense = after(dense, parts)
    query, key, value, out, norm_gain, ffn_gain, router, const, vec = unpack(
        core_arg, dense, swap_cores, gain_row, w_query, w_key, w_value
    )
    return (
        mixed[:, None, None],
        x_grad[:, None, None],
        jnp.swapaxes(prior_grad, 1, 2)[:, None, None],
        norm_gain,
        query,
        key,
        value,
        out,
        ffn_gain,
        router.T,
        jnp.swapaxes(const, 1, 2),
        vec,
        *wide_out,
    )


def solution(mesh):
    shape = mesh.devices.shape
    split = Mesh(
        mesh.devices.reshape(shape[0], shape[1], shape[2] // 2, 2), ("dp", "context", "z", "core")
    )
    slot = P(None, "dp", ("context", "z", "core"), None, None)
    expert = P(("z", "core"), None, None)
    return jax.shard_map(
        on_device,
        mesh=split,
        in_specs=(
            slot, slot, slot, slot, P(None, "dp", ("context", "z", "core")),
            *(P(),) * 9,
            *(expert,) * 3,
            slot,
        ),
        out_specs=(slot, slot, slot, *(P(),) * 9, *(expert,) * 3),
        check_vma=False,
    )
```
